128 devices in a mesh: dp: 16 (over y, z), graph: 8 (over x, core).
Axes of the slice: x: 4, y: 4, z: 4, core: 2. Of those that a mesh axis runs over, the one named last changes fastest.
Arguments:
- nodes: bfloat16 [16, 512, 1024], P('dp', 'graph'), may hold values from -6 to 6
- node_grad: bfloat16 [16, 512, 1024], P('dp', 'graph'), may hold values from -6 to 6
- edges: bfloat16 [16, 8192, 512], P('dp', 'graph'), may hold values from -6 to 6
- source: int32 [16, 8192], P('dp', 'graph'), may hold values from 0 to 511
- target: int32 [16, 8192], P('dp', 'graph'), may hold values from 0 to 511
- trip_in: int32 [16, 16384], P('dp', 'graph'), may hold values from 0 to 8191
- trip_out: int32 [16, 16384], P('dp', 'graph'), may hold values from 0 to 1023
- basis: bfloat16 [16, 16384, 64], P('dp', 'graph'), may hold values from -6 to 6
- trip_count: int32 [16, 8], P('dp', 'graph'), may hold values from 1 to 2048, 9216 in all within a row
- w_ne: bfloat16 [2048, 512], replicated, may hold values from -0.125 to 0.125
- w_down: bfloat16 [512, 64], replicated, may hold values from -0.25 to 0.25
- w_up: bfloat16 [64, 512], replicated, may hold values from -0.75 to 0.75
- w_en: bfloat16 [512, 1024], replicated, may hold values from -0.25 to 0.25
Outputs:
- new_nodes: bfloat16 [16, 512, 1024], P('dp', 'graph')
- edge_grad: bfloat16 [16, 8192, 512], P('dp', 'graph')
- grad_ne: float32 [2048, 512], replicated
- grad_down: float32 [512, 64], replicated
- grad_up: float32 [64, 512], replicated
- grad_en: float32 [512, 1024], replicated
The draws below stay inside these ranges and needn't reach their ends.
Inputs may be any that keep to these rules, and one draw needn't show every extreme that they name: `trip_count`: in each batch some device has exactly 2048 live triplet slots; live slots come first on a device.
All inputs are finite; a program needn't handle non-finite values.
Results may differ from the reference program's by a relative error of at most 0.019.
Values may be sent and summed in bfloat16 or wider, within the bound.
No kernel may reach another device: no remote copies, remote signals or barrier semaphores. Data moves between devices by JAX's collectives and lax.ppermute only.
A program may use at most 128 MiB of HBM per device.

```python
import math
import jax
import jax.numpy as jnp
import numpy as np
from jax import lax

D = 1024
DE = 512
DT = 64
EDGE_DEV = 1024
TRIP_DEV = 2048
BATCHES = 16
NODES = 512
EDGES = 8192
TRIPS = 16384
N_GRAPH = 8


def set_ends(result, rng, least, high):
    dims = result.shape
    index_at = [jax.random.randint(jax.random.fold_in(rng, axis), (), 0, dims[axis]) for axis in range(len(dims))]
    result = result.at[tuple(index_at)].set(least)
    longest = dims.index(max(dims))
    index_at[longest] = (index_at[longest] + 1) % dims[longest]
    return result.at[tuple(index_at)].set(high)


def steps_of(key, dims, split, low, high):
    factor_of = 1.0
    for dim, blocks in split:
        steps = jax.random.uniform(jax.random.fold_in(jax.random.fold_in(key, 6), dim), (blocks,), jnp.float32, low / len(split), high / len(split))
        factor_of = factor_of * jnp.repeat(jnp.exp(steps), dims[dim] // blocks).reshape((-1,) + (1,) * (len(dims) - 1 - dim))
    return factor_of


def profile(number_of, total, bound, skew):
    portions = [(1 << 20) // math.isqrt(rank ** skew) + 1 for rank in range(2, number_of + 1)]
    spare, given = total - bound - (number_of - 1), [1] * (number_of - 1)
    while spare > 0:
        candidates = [i for i in range(number_of - 1) if given[i] < bound]
        pool, budget = sum([portions[i] for i in candidates]), spare
        for i in candidates:
            more = min(bound - given[i], max(1, budget * portions[i] // pool), spare)
            given[i] = given[i] + more
            spare = spare - more
    return np.array([bound] + given)


def ragged(own_key, number_of, total, reach, slope):
    if number_of == 2:
        one = jax.random.randint(own_key, (), max(1, total - reach), min(reach, total - 1) + 1)
        return jnp.stack([one, total - one])
    tallies = jnp.asarray(profile(number_of, total, reach, slope), jnp.int32)
    couples = (number_of - 1) // 2
    giver, receiver = tallies[1:1 + 2 * couples:2], tallies[2:2 + 2 * couples:2]
    slack = jnp.minimum(giver - 1, reach - receiver)
    moved = jax.random.randint(jax.random.fold_in(own_key, 1), (couples,), 0, 1 << 20) % (slack + 1)
    tallies = tallies.at[1:1 + 2 * couples:2].set(giver - moved).at[2:2 + 2 * couples:2].set(receiver + moved)
    return tallies[jax.random.permutation(jax.random.fold_in(own_key, 2), number_of)]


def centred(stream_key, extent, spread, most, cuts=(), held_as=jnp.bfloat16):
    loudness = steps_of(stream_key, extent, cuts, -0.22, 0.18) if cuts else 1.0
    entries = jax.random.normal(stream_key, extent, jnp.float32) * spread * loudness
    return jnp.minimum(jnp.maximum(entries, -most), most).astype(held_as)


def setup_inputs(seed: int = 0) -> dict:
    seeds = jax.random.split(jax.random.key(seed), 14)
    return {
        "nodes": centred(seeds[0], (BATCHES, NODES, D), 1.0, 6.0, ((0, 16), (1, 8))),
        "node_grad": centred(seeds[1], (BATCHES, NODES, D), 1.0, 6.0, ((0, 16), (1, 8))),
        "edges": centred(seeds[2], (BATCHES, EDGES, DE), 1.0, 6.0, ((0, 16), (1, 8))),
        "source": set_ends(jax.random.randint(seeds[3], (BATCHES, EDGES), 0, NODES), jax.random.fold_in(seeds[3], 1), 0, NODES - 1).astype(jnp.int32),
        "target": set_ends(jax.random.randint(seeds[4], (BATCHES, EDGES), 0, NODES), jax.random.fold_in(seeds[4], 1), 0, NODES - 1).astype(jnp.int32),
        "trip_in": set_ends(jax.random.randint(seeds[5], (BATCHES, TRIPS), 0, EDGES), jax.random.fold_in(seeds[5], 1), 0, EDGES - 1).astype(jnp.int32),
        "trip_out": set_ends(jax.random.randint(seeds[6], (BATCHES, TRIPS), 0, EDGE_DEV), jax.random.fold_in(seeds[6], 1), 0, EDGE_DEV - 1).astype(jnp.int32),
        "basis": centred(seeds[7], (BATCHES, TRIPS, DT), 1.0, 6.0, ((0, 16), (1, 8))),
        "trip_count": jax.vmap(lambda own: ragged(own, N_GRAPH, (N_GRAPH + 1) * TRIP_DEV // 2, TRIP_DEV, 2))(jax.random.split(seeds[8], BATCHES)).reshape((BATCHES, N_GRAPH)).astype(jnp.int32),
        "w_ne": centred(seeds[9], (2 * D, DE), (2 * D) ** -0.5, 0.125),
        "w_down": centred(seeds[10], (DE, DT), DE ** -0.5, 0.25),
        "w_up": centred(seeds[11], (DT, DE), DT ** -0.5, 0.75),
        "w_en": centred(seeds[12], (DE, D), DE ** -0.5, 0.25),
    }


def silu_grad(value):
    sig = jax.nn.sigmoid(value)
    return sig * (1.0 + value * (1.0 - sig))

def one_batch(nodes, node_grad, edges, source, target, trip_in, trip_out, basis, count, w_ne, w_down, w_up, w_en):
    edge_total = edges.shape[0]
    node_total = nodes.shape[0]
    trip_total = trip_in.shape[0]
    per_trip = trip_total // N_GRAPH
    per_edge = edge_total // N_GRAPH
    position = jnp.arange(trip_total, dtype=jnp.int32)
    owner = (position // per_trip).astype(jnp.int32)
    live = (position % per_trip < count[owner]).astype(jnp.float32)[:, None]
    out_edge = (owner * per_edge + trip_out).astype(jnp.int32)
    pair = jnp.concatenate([nodes[source], nodes[target]], axis=1)
    pre = jnp.dot(pair, w_ne, preferred_element_type=jnp.float32)
    inner = (edges.astype(jnp.float32) + jax.nn.silu(pre)).astype(jnp.bfloat16)
    down = jnp.dot(inner, w_down, preferred_element_type=jnp.float32).astype(jnp.bfloat16)
    term = down[trip_in].astype(jnp.float32) * basis.astype(jnp.float32) * live
    summed = jax.ops.segment_sum(term, out_edge, num_segments=edge_total).astype(jnp.bfloat16)
    zed = jnp.dot(summed, w_up, preferred_element_type=jnp.float32)
    outer = (inner.astype(jnp.float32) + jax.nn.silu(zed)).astype(jnp.bfloat16)
    message = jnp.dot(outer, w_en, preferred_element_type=jnp.float32)
    update = jax.ops.segment_sum(message, target, num_segments=node_total)
    new_nodes = (nodes.astype(jnp.float32) + update).astype(jnp.bfloat16)
    back = node_grad[target]
    d_outer = jnp.dot(back, w_en.T, preferred_element_type=jnp.float32)
    g_en = jnp.dot(outer.T, back, preferred_element_type=jnp.float32)
    d_zed = (d_outer * silu_grad(zed)).astype(jnp.bfloat16)
    g_up = jnp.dot(summed.T, d_zed, preferred_element_type=jnp.float32)
    d_sum = jnp.dot(d_zed, w_up.T, preferred_element_type=jnp.float32)
    d_term = d_sum[out_edge] * basis.astype(jnp.float32) * live
    d_down = jax.ops.segment_sum(d_term, trip_in, num_segments=edge_total).astype(jnp.bfloat16)
    d_inner = d_outer + jnp.dot(d_down, w_down.T, preferred_element_type=jnp.float32)
    g_down = jnp.dot(inner.T, d_down, preferred_element_type=jnp.float32)
    d_pre = (d_inner * silu_grad(pre)).astype(jnp.bfloat16)
    g_ne = jnp.dot(pair.T, d_pre, preferred_element_type=jnp.float32)
    return (new_nodes, d_inner.astype(jnp.bfloat16), g_ne, g_down, g_up, g_en)

def reference(nodes, node_grad, edges, source, target, trip_in, trip_out, basis, trip_count, w_ne, w_down, w_up, w_en):

    def step(carry, batch):
        new_nodes, edge_grad, g_ne, g_down, g_up, g_en = one_batch(*batch, w_ne, w_down, w_up, w_en)
        carry = (carry[0] + g_ne, carry[1] + g_down, carry[2] + g_up, carry[3] + g_en)
        return (carry, (new_nodes, edge_grad))
    start = (jnp.zeros(w_ne.shape, jnp.float32), jnp.zeros(w_down.shape, jnp.float32), jnp.zeros(w_up.shape, jnp.float32), jnp.zeros(w_en.shape, jnp.float32))
    sums, outs = lax.scan(step, start, (nodes, node_grad, edges, source, target, trip_in, trip_out, basis, trip_count))
    return (outs[0], outs[1], sums[0], sums[1], sums[2], sums[3])
```

```python
import jax
import jax.numpy as jnp
from jax import lax
from jax.experimental import pallas as pl
from jax.experimental.pallas import tpu as pltpu
from jax.sharding import PartitionSpec as P

BF = jnp.bfloat16
F32 = jnp.float32
NT = (((1,), (1,)), ((), ()))


def dot(a, b):
    return jnp.dot(a, b, preferred_element_type=F32)


def dot_nt(a, b):
    return lax.dot_general(a, b, NT, preferred_element_type=F32)


def call(body, outs, args, scalars=0, scratch=(), flops=0, vmem=40):
    moved = sum(a.size * a.dtype.itemsize for a in args) + sum(
        o.size * o.dtype.itemsize for o in outs
    )
    specs = [
        pl.BlockSpec(memory_space=pltpu.SMEM if i < scalars else pltpu.VMEM)
        for i in range(len(args))
    ]
    return pl.pallas_call(
        body,
        out_shape=list(outs),
        in_specs=specs,
        out_specs=[pl.BlockSpec(memory_space=pltpu.VMEM)] * len(outs),
        scratch_shapes=list(scratch),
        compiler_params=pltpu.CompilerParams(vmem_limit_bytes=vmem << 20),
        cost_estimate=pl.CostEstimate(flops=flops, bytes_accessed=moved, transcendentals=0),
    )(*args)


def sds(shape, dtype=BF):
    return jax.ShapeDtypeStruct(shape, dtype)


def at(i, size):
    return pl.ds(pl.multiple_of(i * size, size), size)


def hot(mask):
    return jnp.where(mask, 1.0, 0.0).astype(BF)


def prep_body(cnt, src_c, tgt_c, src_r, tgt_r, in_c, in_r, out_c, out_r, s, st, il, ilt, ol, olt):
    lane = lax.broadcasted_iota(jnp.int32, (256, 512), 1)
    for i in range(4):
        ch = slice(256 * i, 256 * i + 256)
        s[ch, 0:512] = hot(src_c[ch, :] == lane)
        s[ch, 512:1024] = hot(tgt_c[ch, :] == lane)
    row = lax.broadcasted_iota(jnp.int32, (128, 1024), 0)
    for i in range(4):
        ch = slice(128 * i, 128 * i + 128)
        st[ch, :] = hot(src_r[...] == row + 128 * i)
        st[512 + 128 * i : 640 + 128 * i, :] = hot(tgt_r[...] == row + 128 * i)
    live = cnt[0, 0]
    for i in range(8):
        ch = slice(256 * i, 256 * i + 256)
        pos = lax.broadcasted_iota(jnp.int32, (256, 1), 0) + 256 * i
        il[ch, :] = hot(jnp.where(pos < live, in_c[ch, :] & 511, -1) == lane)
        ol[ch, :] = hot((out_c[ch, :] & 511) == lane)
    pos = lax.broadcasted_iota(jnp.int32, (1, 2048), 1)
    in_lo = jnp.where(pos < live, in_r[...] & 511, -1)
    out_lo = out_r[...] & 511
    row = lax.broadcasted_iota(jnp.int32, (64, 2048), 0)
    for i in range(8):
        ch = slice(64 * i, 64 * i + 64)
        ilt[ch, :] = hot(in_lo == row + 64 * i)
        olt[ch, :] = hot(out_lo == row + 64 * i)


def k1_body(
    xc, n0, n1, n2, n3, m0, m1, m2, m3, s, edges, w_ne, wd, nodes_all, dsilu, inner, down, ab
):
    x, c = xc[0], xc[1]
    for k, (mine, other) in enumerate(((n0, m0), (n1, m1), (n2, m2), (n3, m3))):
        g = 2 * lax.rem(x + 4 - k, 4)
        nodes_all[at(g + c, 64), :] = mine[...]
        nodes_all[at(g + 1 - c, 64), :] = other[...]
    for i in range(2):
        ch = slice(256 * i, 256 * i + 256)
        part = nodes_all[ch, :]
        ab[ch, :] = dot(part, w_ne[0:1024, :]).astype(BF)
        ab[512 + 256 * i : 768 + 256 * i, :] = dot(part, w_ne[1024:2048, :]).astype(BF)
    for i in range(2):
        total = None
        for h in range(2):
            ch = slice(512 * h + 256 * i, 512 * h + 256 * i + 256)
            pre = dot(s[ch, :], ab[...])
            sig = jax.nn.sigmoid(pre)
            held = (edges[ch, :].astype(F32) + pre * sig).astype(BF)
            inner[ch, :] = held
            dsilu[ch, :] = (sig * (1.0 + pre * (1.0 - sig))).astype(BF)
            part = dot(held, wd[512 * h : 512 * h + 512, :])
            total = part if total is None else total + part
        down[256 * i : 256 * i + 256, :] = total.astype(BF)


def kq_body(all_grad, w_en, s, nodes_all, d_outer, nodes_t, q):
    for i in range(2):
        ch = slice(256 * i, 256 * i + 256)
        q[ch, :] = dot_nt(all_grad[ch, :], w_en[...]).astype(BF)
    for i in range(4):
        ch = slice(256 * i, 256 * i + 256)
        d_outer[ch, :] = dot(s[ch, 512:1024], q[...]).astype(BF)
    nodes_t[...] = nodes_all[...].T


def halves(value, odd, upper):
    kept = jnp.where(upper == odd, value, 0.0)
    return kept + pltpu.roll(kept, 64, 1)


def k2_body(
    xc, d0, d1, d2, d3, e0, e1, e2, e3, il, ilt, ol, olt, in_c, out_c, basis, inner, d_outer, wu,
    keep, send, outer, summed, dzed, table, gath, spread,
):
    x, c = xc[0], xc[1]
    for k, (mine, other) in enumerate(((d0, e0), (d1, e1), (d2, e2), (d3, e3))):
        g = 2 * lax.rem(x + 4 - k, 4)
        table[:, at(g + c, 128)] = mine[...]
        table[:, at(g + 1 - c, 128)] = other[...]
    upper = lax.broadcasted_iota(jnp.int32, (256, 128), 1) >= 64
    for i in range(8):
        ch = slice(256 * i, 256 * i + 256)
        got = dot(il[ch, :], table[...])
        hi = in_c[ch, :] >> 9
        acc = jnp.zeros((256, 128), F32)
        for g in range(8):
            acc = jnp.where((hi >> 1) == g, got[:, 128 * g : 128 * g + 128], acc)
        term = halves(acc, (hi & 1) == 1, upper) * basis[ch, :].astype(F32)
        gath[ch, :] = jnp.where(upper == ((out_c[ch, :] >> 9) == 1), term, 0.0).astype(BF)
    held = dot(olt[...], gath[...]).astype(BF)
    summed[...] = held
    d_sum = jnp.zeros((512, 128), F32)
    for h in range(2):
        ch = slice(512 * h, 512 * h + 512)
        w = wu[128 * h : 128 * h + 128, :]
        zed = dot(held, w)
        sig = jax.nn.sigmoid(zed)
        outer[ch, :] = (inner[ch, :].astype(F32) + zed * sig).astype(BF)
        dz = (d_outer[ch, :].astype(F32) * (sig * (1.0 + zed * (1.0 - sig)))).astype(BF)
        dzed[ch, :] = dz
        d_sum += dot_nt(dz, w)
    d_sum = d_sum.astype(BF)
    for i in range(8):
        ch = slice(256 * i, 256 * i + 256)
        got = dot(ol[ch, :], d_sum)
        term = halves(got, (out_c[ch, :] >> 9) == 1, upper) * basis[ch, :].astype(F32)
        hi = in_c[ch, :] >> 9
        term = jnp.where(upper == ((hi & 1) == 1), term, 0.0)
        for g in range(8):
            spread[ch, 128 * g : 128 * g + 128] = jnp.where((hi >> 1) == g, term, 0.0).astype(BF)
    for i in range(4):
        ch = slice(128 * i, 128 * i + 128)
        part = dot(ilt[...], spread[:, 256 * i : 256 * i + 256])
        low, high = part[:, 0:128], part[:, 128:256]
        keep[:, ch] = jnp.where(c == 0, low, high)
        send[:, ch] = jnp.where(c == 0, high, low).astype(BF)


def ko_body(outer, st, summed, dzed, o, ot, gup):
    for i in range(2):
        ch = slice(256 * i, 256 * i + 256)
        part = dot(st[512 + 256 * i : 768 + 256 * i, :], outer[...])
        o[ch, :] = part.astype(BF)
        ot[:, ch] = part.T.astype(BF)
    summed_t = summed[...].T
    gup[...] = dot(summed_t[0:64, :], dzed[0:512, :]) + dot(summed_t[64:128, :], dzed[512:1024, :])


def ka_body(xc, keep, recv, own, s1, s2, s3):
    x = xc[0]
    for k, ref in enumerate((own, s1, s2, s3)):
        ch = at(lax.rem(x + k, 4), 128)
        ref[...] = (keep[:, ch] + recv[:, ch].astype(F32)).astype(BF)


def total4(a, b, c, d):
    return (a.astype(F32) + c.astype(F32)) + (b.astype(F32) + d.astype(F32))


def k3_body(
    xc, own, r1, r2, r3, d_outer, dsilu, inner, st, wdt, ot, gup, edge_grad, keep, send, d_pre
):
    c = xc[1]
    dd = total4(own[...], r1[...], r2[...], r3[...]).astype(BF)
    for h in range(2):
        for i in range(2):
            rows = slice(256 * i, 256 * i + 256)
            ch = slice(512 * h + 256 * i, 512 * h + 256 * i + 256)
            d_inner = d_outer[ch, :].astype(F32) + dot(dd[rows, :], wdt[128 * h : 128 * h + 128, :])
            edge_grad[ch, :] = d_inner.astype(BF)
            d_pre[ch, :] = (d_inner * dsilu[ch, :].astype(F32)).astype(BF)
    for i in range(2):
        rows = slice(256 * i, 256 * i + 256)
        send[rows, :] = dot(st[at(2 * (1 - c) + i, 256), :], d_pre[...]).astype(BF)
        keep[rows, :] = dot(st[at(2 * c + i, 256), :], d_pre[...])
    ddt = dd.T
    gdown = dot(ddt[0:64, :], inner[0:512, :]) + dot(ddt[64:128, :], inner[512:1024, :])
    keep[512:576, :] = jnp.where(c == 0, gup[...], gdown)
    send[512:576, :] = jnp.where(c == 0, gdown, gup[...]).astype(BF)
    for i in range(4):
        rows = slice(576 + 64 * i, 640 + 64 * i)
        keep[rows, :] = ot[at(2 * i + c, 64), :].astype(F32)
        send[rows, :] = ot[at(2 * i + 1 - c, 64), :]


def kb_body(xc, keep, recv, own, s1, s2, s3):
    x = xc[0]
    for k, ref in enumerate((own, s1, s2, s3)):
        b = lax.rem(x + k, 4)
        ch = at(b, 128)
        ref[0:576, :] = (keep[0:576, ch] + recv[0:576, ch].astype(F32)).astype(BF)
        rows = pl.ds(pl.multiple_of(576 + 64 * b, 64), 64)
        part = (keep[rows, :] + recv[rows, :].astype(F32)).astype(BF)
        for j in range(4):
            ref[576 + 64 * j : 640 + 64 * j, :] = part[:, 128 * j : 128 * j + 128]


def k4_body(yz, own, r1, r2, r3, nodes_t, all_grad, g0, s1, s2, s3, whole):
    y = yz[0]
    sums = total4(own[...], r1[...], r2[...], r3[...])
    whole[0:1024, :] = dot(nodes_t[...], sums[0:512, :].astype(BF)).astype(BF)
    ot = sums[576:832, :].astype(BF)
    ot = jnp.concatenate([ot[64 * j : 64 * j + 64, :] for j in range(4)], axis=1)
    gen = dot(ot, all_grad[...]).astype(BF)
    for j in range(8):
        whole[1024 + 64 * j : 1088 + 64 * j, :] = gen[:, 128 * j : 128 * j + 128]
    whole[1536:1600, :] = sums[512:576, :].astype(BF)
    for k, ref in enumerate((g0, s1, s2, s3)):
        ref[...] = whole[at(lax.rem(y + k, 4), 400), :]


def sum_body(a, b, c, d, out):
    out[...] = total4(a[...], b[...], c[...], d[...]).astype(BF)


def place_body(yz, own, r1, r2, r3, out):
    y = yz[0]
    for k, ref in enumerate((own, r1, r2, r3)):
        out[at(lax.rem(y + 4 - k, 4), 400), :] = ref[...]


def end_body(xc, p0, p1, p2, p3, q0, q1, q2, q3, gne, gdt, gup, gen):
    x, c = xc[0], xc[1]
    for k, (mine, other) in enumerate(((p0, q0), (p1, q1), (p2, q2), (p3, q3))):
        b = lax.rem(x + 4 - k, 4)
        ch = at(b, 128)
        for ref, core in ((mine, c), (other, 1 - c)):
            gne[at(core, 1024), ch] = ref[0:1024, :].astype(F32)
            rows = at(2 * b + core, 64)
            for j in range(8):
                gen[rows, 128 * j : 128 * j + 128] = ref[1024 + 64 * j : 1088 + 64 * j, :].astype(
                    F32
                )
        low = jnp.where(c == 0, mine[1536:1600, :].astype(F32), other[1536:1600, :].astype(F32))
        high = jnp.where(c == 0, other[1536:1600, :].astype(F32), mine[1536:1600, :].astype(F32))
        gup[:, ch] = low
        gdt[:, ch] = high


def over_x(value, k):
    perm = [(2 * x + c, 2 * ((x + k) % 4) + c) for x in range(4) for c in range(2)]
    return lax.ppermute(value, "graph", perm)


def over_core(value):
    return lax.ppermute(value, "graph", [(i, i ^ 1) for i in range(8)])


def over_y(value, k):
    perm = [(4 * y + z, 4 * ((y + k) % 4) + z) for y in range(4) for z in range(4)]
    return lax.ppermute(value, "dp", perm)


def over_z(value, k):
    perm = [(4 * y + z, 4 * y + (z + k) % 4) for y in range(4) for z in range(4)]
    return lax.ppermute(value, "dp", perm)


def gather8(value):
    mine = [value] + [over_x(value, k) for k in (1, 2, 3)]
    return mine + [over_core(v) for v in mine]


def local(
    nodes, node_grad, edges, source, target, trip_in, trip_out, basis, trip_count,
    w_ne, w_down, w_up, w_en,
):
    g = lax.axis_index("graph")
    d = lax.axis_index("dp")
    xc = jnp.stack([g // 2, g % 2]).astype(jnp.int32)
    yz = jnp.stack([d // 4, d % 4]).astype(jnp.int32)
    node_parts = gather8(nodes[0])
    all_grad = lax.all_gather(node_grad[0], "graph", axis=0, tiled=True)

    in_c, out_c = trip_in[0][:, None], trip_out[0][:, None]
    s, st, il, ilt, ol, olt = call(
        prep_body,
        [sds((1024, 1024)), sds((1024, 1024)), sds((2048, 512)), sds((512, 2048)),
         sds((2048, 512)), sds((512, 2048))],
        [trip_count, source[0][:, None], target[0][:, None], source, target,
         in_c, trip_in, out_c, trip_out],
        scalars=1, flops=1 << 22,
    )
    none = jnp.zeros((512, 64), BF)
    wd = jnp.concatenate(
        [jnp.concatenate([w_down, none], axis=1), jnp.concatenate([none, w_down], axis=1)], axis=0
    )
    wu = jnp.concatenate([w_up, none.T, none.T, w_up], axis=0)
    wdt = jnp.concatenate([w_down.T, none.T, none.T, w_down.T], axis=0)
    basis2 = jnp.concatenate([basis[0], basis[0]], axis=1)

    nodes_all, dsilu, inner, down = call(
        k1_body,
        [sds((512, 1024)), sds((1024, 512)), sds((1024, 512)), sds((512, 128))],
        [xc, *node_parts, s, edges[0], w_ne, wd],
        scalars=1, scratch=[pltpu.VMEM((1024, 512), BF)], flops=2 << 30,
    )
    down_parts = gather8(down)
    d_outer, nodes_t = call(
        kq_body,
        [sds((1024, 512)), sds((1024, 512))],
        [all_grad, w_en, s, nodes_all],
        scratch=[pltpu.VMEM((512, 512), BF)], flops=1 << 30,
    )
    keep, send, outer, summed, dzed = call(
        k2_body,
        [sds((512, 512), F32), sds((512, 512)), sds((1024, 512)), sds((512, 128)),
         sds((1024, 512))],
        [xc, *down_parts, il, ilt, ol, olt, in_c, out_c, basis2, inner, d_outer, wu],
        scalars=1,
        scratch=[pltpu.VMEM((512, 1024), BF), pltpu.VMEM((2048, 128), BF),
                 pltpu.VMEM((2048, 1024), BF)],
        flops=4 << 30,
    )
    recv = over_core(send)
    parts = call(ka_body, [sds((512, 128))] * 4, [xc, keep, recv], scalars=1)
    dd = [parts[0]] + [over_x(parts[k], k) for k in (1, 2, 3)]
    o, ot, gup = call(
        ko_body,
        [sds((512, 512)), sds((512, 512)), sds((64, 512), F32)],
        [outer, st, summed, dzed], flops=1 << 29,
    )
    edge_grad, keep, send = call(
        k3_body,
        [sds((1024, 512)), sds((832, 512), F32), sds((832, 512))],
        [xc, *dd, d_outer, dsilu, inner, st, wdt, ot, gup],
        scalars=1, scratch=[pltpu.VMEM((1024, 512), BF)], flops=2 << 30,
    )
    recv = over_core(send)
    parts = call(kb_body, [sds((832, 128))] * 4, [xc, keep, recv], scalars=1)
    parts = [parts[0]] + [over_x(parts[k], k) for k in (1, 2, 3)]
    parts = call(
        k4_body, [sds((400, 128))] * 4, [yz, *parts, nodes_t, all_grad],
        scalars=1, scratch=[pltpu.VMEM((1600, 128), BF)], flops=1 << 28,
    )
    parts = [parts[0]] + [over_y(parts[k], k) for k in (1, 2, 3)]
    (part,) = call(sum_body, [sds((400, 128))], parts)
    (part,) = call(sum_body, [sds((400, 128))], [part] + [over_z(part, k) for k in (1, 2, 3)])
    parts = [part] + [over_y(part, k) for k in (1, 2, 3)]
    (part,) = call(place_body, [sds((1600, 128))], [yz, *parts], scalars=1)
    grad_ne, grad_down_t, grad_up, grad_en = call(
        end_body,
        [sds((2048, 512), F32), sds((64, 512), F32), sds((64, 512), F32), sds((512, 1024), F32)],
        [xc, *gather8(part)],
        scalars=1,
    )
    rows = lax.psum_scatter(o, "graph", scatter_dimension=0, tiled=True)
    new_nodes = (nodes[0].astype(F32) + dot(rows, w_en)).astype(BF)
    return (new_nodes[None], edge_grad[None], grad_ne, grad_down_t.T, grad_up, grad_en)


def solution(mesh):
    split3, split2 = P("dp", "graph", None), P("dp", "graph")
    in_specs = (split3,) * 3 + (split2,) * 4 + (split3, split2) + (P(),) * 4
    out_specs = (split3, split3, P(), P(), P(), P())
    return jax.shard_map(local, mesh=mesh, in_specs=in_specs, out_specs=out_specs, check_vma=False)
```

```python
import jax
import jax.numpy as jnp
from jax import lax
from jax.experimental import pallas as pl
from jax.experimental.pallas import tpu as pltpu
from jax.sharding import PartitionSpec as P

BF = jnp.bfloat16
F32 = jnp.float32
NT = (((1,), (1,)), ((), ()))


def dot(a, b):
    return jnp.dot(a, b, preferred_element_type=F32)


def dot_nt(a, b):
    return lax.dot_general(a, b, NT, preferred_element_type=F32)


def call(body, outs, args, scalars=0, scratch=(), flops=0, vmem=40, far_in=0, far_out=0):
    moved = sum(a.size * a.dtype.itemsize for a in args) + sum(
        o.size * o.dtype.itemsize for o in outs
    )

    def places(count, first, last):
        return [
            pl.BlockSpec(
                memory_space=pltpu.SMEM
                if i < first
                else (pltpu.HBM if i >= count - last else pltpu.VMEM)
            )
            for i in range(count)
        ]

    return pl.pallas_call(
        body,
        out_shape=list(outs),
        in_specs=places(len(args), scalars, far_in),
        out_specs=places(len(outs), 0, far_out),
        scratch_shapes=list(scratch),
        compiler_params=pltpu.CompilerParams(vmem_limit_bytes=vmem << 20),
        cost_estimate=pl.CostEstimate(flops=flops, bytes_accessed=moved, transcendentals=0),
    )(*args)


def sds(shape, dtype=BF):
    return jax.ShapeDtypeStruct(shape, dtype)


def at(i, size):
    return pl.ds(pl.multiple_of(i * size, size), size)


def hot(mask):
    return jnp.where(mask, 1.0, 0.0).astype(BF)


def left(w):
    return jnp.concatenate([w, jnp.zeros_like(w)], axis=0)


def right(w):
    return jnp.concatenate([jnp.zeros_like(w), w], axis=0)


def ends_body(src_c, tgt_c, w_far, s, w_near, sem):
    copy = pltpu.make_async_copy(w_far, w_near, sem)
    copy.start()
    lane = lax.broadcasted_iota(jnp.int32, (256, 512), 1)
    for i in range(4):
        ch = slice(256 * i, 256 * i + 256)
        s[ch, 0:512] = hot(src_c[ch, :] == lane)
        s[ch, 512:1024] = hot(tgt_c[ch, :] == lane)
    copy.wait()


def prep_body(
    cnt, src_r, tgt_r, in_c, in_r, out_c, out_r, basis_t, st, il, ilt, ol, olt, basis
):
    row = lax.broadcasted_iota(jnp.int32, (128, 1024), 0)
    for i in range(4):
        ch = slice(128 * i, 128 * i + 128)
        st[ch, :] = hot(src_r[...] == row + 128 * i)
        st[512 + 128 * i : 640 + 128 * i, :] = hot(tgt_r[...] == row + 128 * i)
    live = cnt[0, 0]
    lane = lax.broadcasted_iota(jnp.int32, (256, 512), 1)
    for i in range(8):
        ch = slice(256 * i, 256 * i + 256)
        pos = lax.broadcasted_iota(jnp.int32, (256, 1), 0) + 256 * i
        il[ch, :] = hot(jnp.where(pos < live, in_c[ch, :] & 511, -1) == lane)
        ol[ch, :] = hot((out_c[ch, :] & 511) == lane)
    pos = lax.broadcasted_iota(jnp.int32, (1, 2048), 1)
    in_lo = jnp.where(pos < live, in_r[...] & 511, -1)
    out_lo = out_r[...] & 511
    row = lax.broadcasted_iota(jnp.int32, (64, 2048), 0)
    for i in range(8):
        ch = slice(64 * i, 64 * i + 64)
        ilt[ch, :] = hot(in_lo == row + 64 * i)
        olt[ch, :] = hot(out_lo == row + 64 * i)
    basis[...] = jnp.concatenate([basis_t[...], basis_t[...]], axis=0).T


def gathered(xc, refs, out):
    x, c = xc[0], xc[1]
    for k in range(4):
        g = 2 * lax.rem(x + 4 - k, 4)
        out[at(g + c, 64), :] = refs[k][...]
        out[at(g + 1 - c, 64), :] = refs[4 + k][...]


def k1_body(xc, *refs):
    s, edges, w_ne, w_down_t, down, inner_far, dsilu_far, nodes, ab, inner, dsilu, sems = refs[8:]
    gathered(xc, refs[:8], nodes)
    for i in range(2):
        ch = slice(256 * i, 256 * i + 256)
        part = nodes[ch, :]
        ab[ch, :] = dot(part, w_ne[0:1024, :]).astype(BF)
        ab[512 + 256 * i : 768 + 256 * i, :] = dot(part, w_ne[1024:2048, :]).astype(BF)
    wd = (left(w_down_t[...]), right(w_down_t[...]))
    copies = []
    for i in range(2):
        total = None
        for h in range(2):
            ch = slice(512 * h + 256 * i, 512 * h + 256 * i + 256)
            pre = dot(s[ch, :], ab[...])
            sig = jax.nn.sigmoid(pre)
            held = (edges[ch, :].astype(F32) + pre * sig).astype(BF)
            inner[ch, :] = held
            dsilu[ch, :] = (sig * (1.0 + pre * (1.0 - sig))).astype(BF)
            for near, far in ((inner, inner_far), (dsilu, dsilu_far)):
                copy = pltpu.make_async_copy(near.at[ch, :], far.at[ch, :], sems.at[len(copies)])
                copy.start()
                copies.append(copy)
            part = dot_nt(held, wd[h])
            total = part if total is None else total + part
        down[256 * i : 256 * i + 256, :] = total.astype(BF)
    for copy in copies:
        copy.wait()


def kq_body(xc, *refs):
    w_en, tgt_c, d_outer, all_grad, q = refs[8:]
    gathered(xc, refs[:8], all_grad)
    for i in range(2):
        ch = slice(256 * i, 256 * i + 256)
        q[ch, :] = dot_nt(all_grad[ch, :], w_en[...]).astype(BF)
    lane = lax.broadcasted_iota(jnp.int32, (256, 512), 1)
    for i in range(4):
        ch = slice(256 * i, 256 * i + 256)
        d_outer[ch, :] = dot(hot(tgt_c[ch, :] == lane), q[...]).astype(BF)


def kw_body(xc, *refs):
    nodes_t, all_grad, nodes = refs[16:]
    gathered(xc, refs[:8], nodes)
    gathered(xc, refs[8:16], all_grad)
    nodes_t[...] = nodes[...].T


def halves(value, odd, upper):
    kept = jnp.where(upper == odd, value, 0.0)
    return kept + pltpu.roll(kept, 64, 1)


def k2_body(
    xc, d0, d1, d2, d3, e0, e1, e2, e3, il, ilt, ol, olt, in_c, out_c, basis, inner, d_outer, w_up,
    keep, send, outer, summed, dzed, table, gath, spread,
):
    x, c = xc[0], xc[1]
    for k, (mine, other) in enumerate(((d0, e0), (d1, e1), (d2, e2), (d3, e3))):
        g = 2 * lax.rem(x + 4 - k, 4)
        table[:, at(g + c, 128)] = mine[...]
        table[:, at(g + 1 - c, 128)] = other[...]
    upper = lax.broadcasted_iota(jnp.int32, (256, 128), 1) >= 64
    for i in range(8):
        ch = slice(256 * i, 256 * i + 256)
        got = dot(il[ch, :], table[...])
        hi = in_c[ch, :] >> 9
        acc = jnp.zeros((256, 128), F32)
        for g in range(8):
            acc = jnp.where((hi >> 1) == g, got[:, 128 * g : 128 * g + 128], acc)
        term = halves(acc, (hi & 1) == 1, upper) * basis[ch, :].astype(F32)
        gath[ch, :] = jnp.where(upper == ((out_c[ch, :] >> 9) == 1), term, 0.0).astype(BF)
    held = dot(olt[...], gath[...]).astype(BF)
    summed[...] = held
    d_sum = jnp.zeros((512, 128), F32)
    for h, w in enumerate((left(w_up[...]), right(w_up[...]))):
        ch = slice(512 * h, 512 * h + 512)
        zed = dot(held, w)
        sig = jax.nn.sigmoid(zed)
        outer[ch, :] = (inner[ch, :].astype(F32) + zed * sig).astype(BF)
        dz = (d_outer[ch, :].astype(F32) * (sig * (1.0 + zed * (1.0 - sig)))).astype(BF)
        dzed[ch, :] = dz
        d_sum += dot_nt(dz, w)
    d_sum = d_sum.astype(BF)
    for i in range(8):
        ch = slice(256 * i, 256 * i + 256)
        got = dot(ol[ch, :], d_sum)
        term = halves(got, (out_c[ch, :] >> 9) == 1, upper) * basis[ch, :].astype(F32)
        hi = in_c[ch, :] >> 9
        term = jnp.where(upper == ((hi & 1) == 1), term, 0.0)
        for g in range(8):
            spread[ch, 128 * g : 128 * g + 128] = jnp.where((hi >> 1) == g, term, 0.0).astype(BF)
    for i in range(4):
        ch = slice(128 * i, 128 * i + 128)
        part = dot(ilt[...], spread[:, 256 * i : 256 * i + 256])
        low, high = part[:, 0:128], part[:, 128:256]
        keep[:, ch] = jnp.where(c == 0, low, high)
        send[:, ch] = jnp.where(c == 0, high, low).astype(BF)


def ko_body(xc, outer, st, summed, dzed, ot, gup, keep, send):
    c = xc[1]
    for i in range(2):
        ch = slice(256 * i, 256 * i + 256)
        part = dot(st[512 + 256 * i : 768 + 256 * i, :], outer[...])
        ot[:, ch] = part.T.astype(BF)
        for j in range(2):
            low, high = part[128 * j : 128 * j + 64, :], part[128 * j + 64 : 128 * j + 128, :]
            rows = slice(128 * i + 64 * j, 128 * i + 64 * j + 64)
            keep[rows, :] = jnp.where(c == 0, low, high)
            send[rows, :] = jnp.where(c == 0, high, low).astype(BF)
    summed_t = summed[...].T
    gup[...] = dot(summed_t[0:64, :], dzed[0:512, :]) + dot(summed_t[64:128, :], dzed[512:1024, :])


def kr_body(xc, keep, recv, own, s1, s2, s3):
    x = xc[0]
    for k, ref in enumerate((own, s1, s2, s3)):
        rows = at(lax.rem(x + k, 4), 64)
        ref[...] = (keep[rows, :] + recv[rows, :].astype(F32)).astype(BF)


def kn_body(own, r1, r2, r3, nodes, w_en, out):
    rows = total4(own[...], r1[...], r2[...], r3[...]).astype(BF)
    out[...] = (nodes[...].astype(F32) + dot(rows, w_en[...])).astype(BF)


def ka_body(xc, keep, recv, own, s1, s2, s3):
    x = xc[0]
    for k, ref in enumerate((own, s1, s2, s3)):
        ch = at(lax.rem(x + k, 4), 128)
        ref[...] = (keep[:, ch] + recv[:, ch].astype(F32)).astype(BF)


def total4(a, b, c, d):
    return (a.astype(F32) + c.astype(F32)) + (b.astype(F32) + d.astype(F32))


def k3_body(
    xc, own, r1, r2, r3, d_outer, dsilu, inner, st, w_down_t, ot, gup, edge_grad, keep, send, d_pre
):
    c = xc[1]
    dd = total4(own[...], r1[...], r2[...], r3[...]).astype(BF)
    for h, w in enumerate((left(w_down_t[...]), right(w_down_t[...]))):
        for i in range(2):
            rows = slice(256 * i, 256 * i + 256)
            ch = slice(512 * h + 256 * i, 512 * h + 256 * i + 256)
            d_inner = d_outer[ch, :].astype(F32) + dot(dd[rows, :], w)
            edge_grad[ch, :] = d_inner.astype(BF)
            d_pre[ch, :] = (d_inner * dsilu[ch, :].astype(F32)).astype(BF)
    for i in range(2):
        rows = slice(256 * i, 256 * i + 256)
        send[rows, :] = dot(st[at(2 * (1 - c) + i, 256), :], d_pre[...]).astype(BF)
        keep[rows, :] = dot(st[at(2 * c + i, 256), :], d_pre[...])
    ddt = dd.T
    gdown = dot(ddt[0:64, :], inner[0:512, :]) + dot(ddt[64:128, :], inner[512:1024, :])
    keep[512:576, :] = jnp.where(c == 0, gup[...], gdown)
    send[512:576, :] = jnp.where(c == 0, gdown, gup[...]).astype(BF)
    for i in range(4):
        rows = slice(576 + 64 * i, 640 + 64 * i)
        keep[rows, :] = ot[at(2 * i + c, 64), :].astype(F32)
        send[rows, :] = ot[at(2 * i + 1 - c, 64), :]


def kb_body(xc, keep, recv, own, s1, s2, s3):
    x = xc[0]
    for k, ref in enumerate((own, s1, s2, s3)):
        b = lax.rem(x + k, 4)
        ch = at(b, 128)
        ref[0:576, :] = (keep[0:576, ch] + recv[0:576, ch].astype(F32)).astype(BF)
        rows = pl.ds(pl.multiple_of(576 + 64 * b, 64), 64)
        part = (keep[rows, :] + recv[rows, :].astype(F32)).astype(BF)
        for j in range(4):
            ref[576 + 64 * j : 640 + 64 * j, :] = part[:, 128 * j : 128 * j + 128]


def k4_body(yz, own, r1, r2, r3, nodes_t, all_grad, g0, s1, s2, s3, whole):
    y = yz[0]
    sums = total4(own[...], r1[...], r2[...], r3[...])
    whole[0:1024, :] = dot(nodes_t[...], sums[0:512, :].astype(BF)).astype(BF)
    ot = sums[576:832, :].astype(BF)
    ot = jnp.concatenate([ot[64 * j : 64 * j + 64, :] for j in range(4)], axis=1)
    gen = dot(ot, all_grad[...]).astype(BF)
    for j in range(8):
        whole[1024 + 64 * j : 1088 + 64 * j, :] = gen[:, 128 * j : 128 * j + 128]
    whole[1536:1600, :] = sums[512:576, :].astype(BF)
    for k, ref in enumerate((g0, s1, s2, s3)):
        ref[...] = whole[at(lax.rem(y + k, 4), 400), :]


def sum_body(a, b, c, d, out):
    out[...] = total4(a[...], b[...], c[...], d[...]).astype(BF)


def place_body(i, own, r1, r2, r3, out):
    rows = own.shape[0]
    for k, ref in enumerate((own, r1, r2, r3)):
        out[at(lax.rem(i[0] + 4 - k, 4), rows), :] = ref[...]


def end_body(xc, *refs):
    gne_far, gdt_far, gup_far, gen_far, gne, gdt, gup, gen, sems = refs[8:]
    x, c = xc[0], xc[1]
    copies = []

    def send(near, far):
        copy = pltpu.make_async_copy(near, far, sems.at[len(copies)])
        copy.start()
        copies.append(copy)

    for k in range(4):
        b = lax.rem(x + 4 - k, 4)
        ch = at(b, 128)
        mine, other = refs[k], refs[4 + k]
        for i, (ref, core) in enumerate(((mine, c), (other, 1 - c))):
            slot = 2 * k + i
            gne[slot] = ref[0:1024, :].astype(F32)
            send(gne.at[slot], gne_far.at[at(core, 1024), ch])
            for j in range(8):
                gen[slot, :, 128 * j : 128 * j + 128] = ref[
                    1024 + 64 * j : 1088 + 64 * j, :
                ].astype(F32)
            send(gen.at[slot], gen_far.at[at(2 * b + core, 64), :])
        mine, other = mine[1536:1600, :].astype(F32), other[1536:1600, :].astype(F32)
        gup[:, ch] = jnp.where(c == 0, mine, other)
        gdt[:, ch] = jnp.where(c == 0, other, mine)
    send(gup, gup_far)
    send(gdt, gdt_far)
    for copy in copies:
        copy.wait()


def over_x(value, k):
    perm = [(2 * x + c, 2 * ((x + k) % 4) + c) for x in range(4) for c in range(2)]
    return lax.ppermute(value, "graph", perm)


def over_core(value):
    return lax.ppermute(value, "graph", [(i, i ^ 1) for i in range(8)])


def over_y(value, k):
    perm = [(4 * y + z, 4 * ((y + k) % 4) + z) for y in range(4) for z in range(4)]
    return lax.ppermute(value, "dp", perm)


def over_z(value, k):
    perm = [(4 * y + z, 4 * y + (z + k) % 4) for y in range(4) for z in range(4)]
    return lax.ppermute(value, "dp", perm)


def gather8(value):
    mine = [value] + [over_x(value, k) for k in (1, 2, 3)]
    return mine + [over_core(v) for v in mine]


def tie(*values):
    return lax.optimization_barrier(values)


def local(
    nodes, node_grad, edges, source, target, trip_in, trip_out, basis, trip_count,
    w_ne, w_down, w_up, w_en,
):
    g = lax.axis_index("graph")
    d = lax.axis_index("dp")
    xc = jnp.stack([g // 2, g % 2]).astype(jnp.int32)
    yz = jnp.stack([d // 4, d % 4]).astype(jnp.int32)
    near = (1, 2, 3)

    n = [nodes[0]] + [over_x(nodes[0], k) for k in near]
    m = [over_core(n[0])]
    p = [node_grad[0]] + [over_x(node_grad[0], k) for k in near]
    tgt_c = target[0][:, None]
    s, w_near = call(
        ends_body,
        [sds((1024, 1024)), sds((2048, 512))],
        [source[0][:, None], tgt_c, w_ne],
        scratch=[pltpu.SemaphoreType.DMA], flops=1 << 31, vmem=16, far_in=1,
    )
    *n, s, w_near = tie(*n, s, w_near)
    m += [over_core(v) for v in n[1:]]
    down, inner, dsilu = call(
        k1_body,
        [sds((512, 128)), sds((1024, 512)), sds((1024, 512))],
        [xc, *n, *m, s, edges[0], w_near, w_down.T],
        scalars=1,
        scratch=[pltpu.VMEM((512, 1024), BF), pltpu.VMEM((1024, 512), BF),
                 pltpu.VMEM((1024, 512), BF), pltpu.VMEM((1024, 512), BF),
                 pltpu.SemaphoreType.DMA((8,))],
        flops=5 << 30, vmem=24, far_out=2,
    )

    t = [down] + [over_x(down, k) for k in near]
    u = [over_core(down)]
    u0, trip_in, p[1], p[2], p[3] = tie(u[0], trip_in, *p[1:])
    u[0] = u0
    q = [over_core(v) for v in p]
    in_c, out_c = trip_in[0][:, None], trip_out[0][:, None]
    st, il, ilt, ol, olt, basis2 = call(
        prep_body,
        [sds((1024, 1024)), sds((2048, 512)), sds((512, 2048)), sds((2048, 512)),
         sds((512, 2048)), sds((2048, 128))],
        [trip_count, source, target, in_c, trip_in, out_c, trip_out, basis[0].T],
        scalars=1, flops=4 << 30, vmem=24,
    )
    (d_outer,) = call(
        kq_body,
        [sds((1024, 512))],
        [xc, *p, *q, w_en, tgt_c],
        scalars=1, scratch=[pltpu.VMEM((512, 1024), BF), pltpu.VMEM((512, 512), BF)],
        flops=2 << 30, vmem=24,
    )
    *t, il, d_outer = tie(*t, il, d_outer)
    u += [over_core(v) for v in t[1:]]
    keep, send, outer, summed, dzed = call(
        k2_body,
        [sds((512, 512), F32), sds((512, 512)), sds((1024, 512)), sds((512, 128)),
         sds((1024, 512))],
        [xc, *t, *u, il, ilt, ol, olt, in_c, out_c, basis2, inner, d_outer, w_up],
        scalars=1,
        scratch=[pltpu.VMEM((512, 1024), BF), pltpu.VMEM((2048, 128), BF),
                 pltpu.VMEM((2048, 1024), BF)],
        flops=8 << 30, vmem=32,
    )

    recv = over_core(send)
    parts = call(ka_body, [sds((512, 128))] * 4, [xc, keep, recv], scalars=1, vmem=8)
    dd = [parts[0]] + [over_x(parts[k], k) for k in near]
    ot, gup, o_keep, o_send = call(
        ko_body,
        [sds((512, 512)), sds((64, 512), F32), sds((256, 512), F32), sds((256, 512))],
        [xc, outer, st, summed, dzed], scalars=1, flops=2 << 30, vmem=16,
    )
    o_recv = over_core(o_send)
    edge_grad, keep, send = call(
        k3_body,
        [sds((1024, 512)), sds((832, 512), F32), sds((832, 512))],
        [xc, *dd, d_outer, dsilu, inner, st, w_down.T, ot, gup],
        scalars=1, scratch=[pltpu.VMEM((1024, 512), BF)], flops=3 << 30, vmem=24,
    )

    recv = over_core(send)
    parts = call(kb_body, [sds((832, 128))] * 4, [xc, keep, recv], scalars=1, vmem=12)
    recv, o_recv, *held = tie(recv, o_recv, *n, *m, *p, *q)
    o_parts = call(kr_body, [sds((64, 512))] * 4, [xc, o_keep, o_recv], scalars=1, vmem=8)
    nodes_t, all_grad = call(
        kw_body,
        [sds((1024, 512)), sds((512, 1024))],
        [xc, *held],
        scalars=1, scratch=[pltpu.VMEM((512, 1024), BF)], flops=2 << 30, vmem=16,
    )
    parts = [parts[0]] + [over_x(parts[k], k) for k in near]
    *parts, nodes_t, all_grad = tie(*parts, nodes_t, all_grad)
    parts = call(
        k4_body, [sds((400, 128))] * 4, [yz, *parts, nodes_t, all_grad],
        scalars=1, scratch=[pltpu.VMEM((1600, 128), BF)], flops=2 << 30, vmem=16,
    )
    *o_parts, first = tie(*o_parts, parts[0])
    parts = [first] + [over_y(parts[k], k) for k in near]
    o_parts = [o_parts[0]] + [over_x(o_parts[k], k) for k in near]
    (part,) = call(sum_body, [sds((400, 128))], parts, vmem=8)
    (new_nodes,) = call(
        kn_body, [sds((64, 1024))], [*o_parts, nodes[0], w_en], flops=1 << 30, vmem=16
    )
    parts = [part] + [over_z(part, k) for k in near]
    new_nodes, *parts = tie(new_nodes, *parts)
    (part,) = call(sum_body, [sds((400, 128))], parts, vmem=8)
    parts = [part] + [over_y(part, k) for k in near]
    (part,) = call(place_body, [sds((1600, 128))], [yz, *parts], scalars=1, vmem=8)
    grad_ne, grad_down_t, grad_up, grad_en = call(
        end_body,
        [sds((2048, 512), F32), sds((64, 512), F32), sds((64, 512), F32), sds((512, 1024), F32)],
        [xc, *gather8(part)],
        scalars=1,
        scratch=[pltpu.VMEM((8, 1024, 128), F32), pltpu.VMEM((64, 512), F32),
                 pltpu.VMEM((64, 512), F32), pltpu.VMEM((8, 64, 1024), F32),
                 pltpu.SemaphoreType.DMA((18,))],
        vmem=24, far_out=4,
    )
    return (new_nodes[None], edge_grad[None], grad_ne, grad_down_t.T, grad_up, grad_en)


def solution(mesh):
    split3, split2 = P("dp", "graph", None), P("dp", "graph")
    in_specs = (split3,) * 3 + (split2,) * 4 + (split3, split2) + (P(),) * 4
    out_specs = (split3, split3, P(), P(), P(), P())
    return jax.shard_map(local, mesh=mesh, in_specs=in_specs, out_specs=out_specs, check_vma=False)
```

```python
import jax
import jax.numpy as jnp
from jax import lax
from jax.experimental import pallas as pl
from jax.experimental.pallas import tpu as pltpu
from jax.sharding import PartitionSpec as P

BF = jnp.bfloat16
F32 = jnp.float32
NT = (((1,), (1,)), ((), ()))


def dot(a, b):
    return jnp.dot(a, b, preferred_element_type=F32)


def dot_nt(a, b):
    return lax.dot_general(a, b, NT, preferred_element_type=F32)


def call(body, outs, args, scalars=0, scratch=(), vmem=40, far_in=0, far_out=0):
    def places(count, first, last):
        return [
            pl.BlockSpec(
                memory_space=pltpu.SMEM
                if i < first
                else (pltpu.HBM if i >= count - last else pltpu.VMEM)
            )
            for i in range(count)
        ]

    return pl.pallas_call(
        body,
        out_shape=[
            pltpu.HBM(o.shape, o.dtype) if i >= len(outs) - far_out else o
            for i, o in enumerate(outs)
        ],
        in_specs=places(len(args), scalars, far_in),
        out_specs=places(len(outs), 0, far_out),
        scratch_shapes=list(scratch),
        compiler_params=pltpu.CompilerParams(vmem_limit_bytes=vmem << 20),
        cost_estimate=pl.CostEstimate(flops=1, bytes_accessed=1, transcendentals=0),
    )(
        *(
            pltpu.with_memory_space_constraint(a, pltpu.HBM) if i >= len(args) - far_in else a
            for i, a in enumerate(args)
        )
    )


def sds(shape, dtype=BF):
    return jax.ShapeDtypeStruct(shape, dtype)


def at(i, size):
    return pl.ds(pl.multiple_of(i * size, size), size)


def hot(mask):
    return jnp.where(mask, 1.0, 0.0).astype(BF)


def left(w):
    return jnp.concatenate([w, jnp.zeros_like(w)], axis=0)


def right(w):
    return jnp.concatenate([jnp.zeros_like(w), w], axis=0)


def column(row):
    return jnp.broadcast_to(row.astype(F32), (128, row.shape[1])).T.astype(jnp.int32)


def hot_rows(col, width):
    lane = lax.broadcasted_iota(jnp.int32, col.shape, 1)
    return jnp.concatenate([hot(col == lane + j) for j in range(0, width, 128)], axis=1)


def prep_body(
    cnt, src_r, tgt_r, in_r, out_r, basis_t, st, il, ilt, ol, olt, basis, in_hi, out_hi
):
    row = lax.broadcasted_iota(jnp.int32, (128, 1024), 0)
    for i in range(4):
        ch = slice(128 * i, 128 * i + 128)
        st[ch, :] = hot(src_r[...] == row + 128 * i)
        st[512 + 128 * i : 640 + 128 * i, :] = hot(tgt_r[...] == row + 128 * i)
    pos = lax.broadcasted_iota(jnp.int32, (1, 2048), 1)
    live = pos < cnt[0, 0]
    in_lo = jnp.where(live, in_r[...] & 511, -1)
    out_lo = out_r[...] & 511
    for i in range(8):
        ch = slice(256 * i, 256 * i + 256)
        il[ch, :] = hot_rows(column(in_lo[:, ch]), 512)
        ol[ch, :] = hot_rows(column(out_lo[:, ch]), 512)
        in_hi[ch, :] = column(in_r[:, ch] >> 9)
        out_hi[ch, :] = column(out_r[:, ch] >> 9)
    row = lax.broadcasted_iota(jnp.int32, (64, 2048), 0)
    for i in range(8):
        ch = slice(64 * i, 64 * i + 64)
        ilt[ch, :] = hot(in_lo == row + 64 * i)
        olt[ch, :] = hot(out_lo == row + 64 * i)
    basis[...] = jnp.concatenate([basis_t[...], basis_t[...]], axis=0).T


def fetch(far, near, sem):
    copy = pltpu.make_async_copy(far, near, sem)
    copy.start()
    return copy


def gathered(xc, refs, out, sems):
    x, c = xc[0], xc[1]
    copies = []
    for k in range(4):
        g = 2 * lax.rem(x + 4 - k, 4)
        copies.append(fetch(refs[k], out.at[at(g + c, 64), :], sems.at[2 * k]))
        copies.append(fetch(refs[4 + k], out.at[at(g + 1 - c, 64), :], sems.at[2 * k + 1]))
    return copies


def k1_body(xc, *refs):
    ends_far, edges_far, w_far = refs[0:2], refs[2], refs[3]
    down, inner_far, dsilu_far, nodes, ab, w_ne, edges, ends, wd_t, inner, dsilu, sems = refs[13:]
    loads = [fetch(ends_far[i], ends.at[i], sems.at[i]) for i in range(2)]
    loads.append(fetch(refs[4], wd_t, sems.at[2]))
    halves_of_w = [
        fetch(w_far.at[rows, :], w_ne.at[rows, :], sems.at[3 + h])
        for h, rows in enumerate((slice(0, 1024), slice(1024, 2048)))
    ]
    for copy in gathered(xc, refs[5:13], nodes, sems.at[pl.ds(8, 8)]):
        copy.wait()
    load_edges = fetch(edges_far, edges, sems.at[5])
    for h in range(2):
        halves_of_w[h].wait()
        for i in range(2):
            rows = slice(512 * h + 256 * i, 512 * h + 256 * i + 256)
            ab[rows, :] = dot(
                nodes[256 * i : 256 * i + 256, :], w_ne[1024 * h : 1024 * h + 1024, :]
            ).astype(BF)
    for copy in loads:
        copy.wait()
    wd = (left(wd_t[...]), right(wd_t[...]))
    load_edges.wait()
    copies = []
    for i in range(2):
        total = None
        for h in range(2):
            ch = slice(512 * h + 256 * i, 512 * h + 256 * i + 256)
            s = jnp.concatenate(
                [hot_rows(column(ends[j, :, ch]), 512) for j in range(2)], axis=1
            )
            pre = dot(s, ab[...])
            sig = jax.nn.sigmoid(pre)
            held = (edges[ch, :].astype(F32) + pre * sig).astype(BF)
            inner[ch, :] = held
            dsilu[ch, :] = (sig * (1.0 + pre * (1.0 - sig))).astype(BF)
            for near, far in ((inner, inner_far), (dsilu, dsilu_far)):
                copies.append(fetch(near.at[ch, :], far.at[ch, :], sems.at[16 + len(copies)]))
            part = dot_nt(held, wd[h])
            total = part if total is None else total + part
        down[256 * i : 256 * i + 256, :] = total.astype(BF)
    for copy in copies:
        copy.wait()


def kq_body(xc, tgt_r, *refs):
    w_far, d_outer, all_grad, w_en, q, sems = refs[8:]
    load = fetch(w_far, w_en, sems.at[8])
    for copy in gathered(xc, refs[:8], all_grad, sems):
        copy.wait()
    load.wait()
    for i in range(2):
        ch = slice(256 * i, 256 * i + 256)
        q[ch, :] = dot_nt(all_grad[ch, :], w_en[...]).astype(BF)
    for i in range(4):
        ch = slice(256 * i, 256 * i + 256)
        d_outer[ch, :] = dot(hot_rows(column(tgt_r[:, ch]), 512), q[...]).astype(BF)


def kw_body(xc, *refs):
    nodes_t, all_grad, nodes, sems = refs[16:]
    copies = gathered(xc, refs[:8], nodes, sems)
    late = gathered(xc, refs[8:16], all_grad, sems.at[pl.ds(8, 8)])
    for copy in copies:
        copy.wait()
    nodes_t[...] = nodes[...].T
    for copy in late:
        copy.wait()


def halves(value, odd, upper):
    kept = jnp.where(upper == odd, value, 0.0)
    return kept + pltpu.roll(kept, 64, 1)


def k2_body(
    xc, d0, d1, d2, d3, e0, e1, e2, e3, il, ilt, ol, olt, in_hi, out_hi, basis, inner, d_outer, w_up,
    keep, send, outer, summed, dzed, table, gath, spread,
):
    x, c = xc[0], xc[1]
    for k, (mine, other) in enumerate(((d0, e0), (d1, e1), (d2, e2), (d3, e3))):
        g = 2 * lax.rem(x + 4 - k, 4)
        table[:, at(g + c, 128)] = mine[...]
        table[:, at(g + 1 - c, 128)] = other[...]
    upper = lax.broadcasted_iota(jnp.int32, (256, 128), 1) >= 64
    for i in range(8):
        ch = slice(256 * i, 256 * i + 256)
        got = dot(il[ch, :], table[...])
        hi = in_hi[ch, :]
        acc = jnp.zeros((256, 128), F32)
        for g in range(8):
            acc = jnp.where((hi >> 1) == g, got[:, 128 * g : 128 * g + 128], acc)
        term = halves(acc, (hi & 1) == 1, upper) * basis[ch, :].astype(F32)
        gath[ch, :] = jnp.where(upper == (out_hi[ch, :] == 1), term, 0.0).astype(BF)
    held = dot(olt[...], gath[...]).astype(BF)
    summed[...] = held
    d_sum = jnp.zeros((512, 128), F32)
    for h, w in enumerate((left(w_up[...]), right(w_up[...]))):
        ch = slice(512 * h, 512 * h + 512)
        zed = dot(held, w)
        sig = jax.nn.sigmoid(zed)
        outer[ch, :] = (inner[ch, :].astype(F32) + zed * sig).astype(BF)
        dz = (d_outer[ch, :].astype(F32) * (sig * (1.0 + zed * (1.0 - sig)))).astype(BF)
        dzed[ch, :] = dz
        d_sum += dot_nt(dz, w)
    d_sum = d_sum.astype(BF)
    for i in range(8):
        ch = slice(256 * i, 256 * i + 256)
        got = dot(ol[ch, :], d_sum)
        term = halves(got, out_hi[ch, :] == 1, upper) * basis[ch, :].astype(F32)
        hi = in_hi[ch, :]
        term = jnp.where(upper == ((hi & 1) == 1), term, 0.0)
        for g in range(8):
            spread[ch, 128 * g : 128 * g + 128] = jnp.where((hi >> 1) == g, term, 0.0).astype(BF)
    for i in range(4):
        ch = slice(128 * i, 128 * i + 128)
        part = dot(ilt[...], spread[:, 256 * i : 256 * i + 256])
        low, high = part[:, 0:128], part[:, 128:256]
        keep[:, ch] = jnp.where(c == 0, low, high)
        send[:, ch] = jnp.where(c == 0, high, low).astype(BF)


def ko_body(xc, outer, st, summed, dzed, ot, gup, keep, send):
    c = xc[1]
    for i in range(2):
        ch = slice(256 * i, 256 * i + 256)
        part = dot(st[512 + 256 * i : 768 + 256 * i, :], outer[...])
        ot[:, ch] = part.T.astype(BF)
        for j in range(2):
            low, high = part[128 * j : 128 * j + 64, :], part[128 * j + 64 : 128 * j + 128, :]
            rows = slice(128 * i + 64 * j, 128 * i + 64 * j + 64)
            keep[rows, :] = jnp.where(c == 0, low, high)
            send[rows, :] = jnp.where(c == 0, high, low).astype(BF)
    summed_t = summed[...].T
    gup[...] = dot(summed_t[0:64, :], dzed[0:512, :]) + dot(summed_t[64:128, :], dzed[512:1024, :])


def kr_body(xc, keep, recv, own, s1, s2, s3):
    x = xc[0]
    for k, ref in enumerate((own, s1, s2, s3)):
        rows = at(lax.rem(x + k, 4), 64)
        ref[...] = (keep[rows, :] + recv[rows, :].astype(F32)).astype(BF)


def kn_body(own, r1, r2, r3, nodes, w_en, out):
    rows = total4(own[...], r1[...], r2[...], r3[...]).astype(BF)
    out[...] = (nodes[...].astype(F32) + dot(rows, w_en[...])).astype(BF)


def ka_body(xc, keep, recv, own, s1, s2, s3):
    x = xc[0]
    for k, ref in enumerate((own, s1, s2, s3)):
        ch = at(lax.rem(x + k, 4), 128)
        ref[...] = (keep[:, ch] + recv[:, ch].astype(F32)).astype(BF)


def total4(a, b, c, d):
    return (a.astype(F32) + c.astype(F32)) + (b.astype(F32) + d.astype(F32))


def k3_body(
    xc, own, r1, r2, r3, d_outer, dsilu, inner, st, w_down_t, ot, gup, edge_grad, keep, send, d_pre
):
    c = xc[1]
    dd = total4(own[...], r1[...], r2[...], r3[...]).astype(BF)
    for h, w in enumerate((left(w_down_t[...]), right(w_down_t[...]))):
        for i in range(2):
            rows = slice(256 * i, 256 * i + 256)
            ch = slice(512 * h + 256 * i, 512 * h + 256 * i + 256)
            d_inner = d_outer[ch, :].astype(F32) + dot(dd[rows, :], w)
            edge_grad[ch, :] = d_inner.astype(BF)
            d_pre[ch, :] = (d_inner * dsilu[ch, :].astype(F32)).astype(BF)
    for i in range(2):
        rows = slice(256 * i, 256 * i + 256)
        send[rows, :] = dot(st[at(2 * (1 - c) + i, 256), :], d_pre[...]).astype(BF)
        keep[rows, :] = dot(st[at(2 * c + i, 256), :], d_pre[...])
    ddt = dd.T
    gdown = dot(ddt[0:64, :], inner[0:512, :]) + dot(ddt[64:128, :], inner[512:1024, :])
    keep[512:576, :] = jnp.where(c == 0, gup[...], gdown)
    send[512:576, :] = jnp.where(c == 0, gdown, gup[...]).astype(BF)
    for i in range(4):
        rows = slice(576 + 64 * i, 640 + 64 * i)
        keep[rows, :] = ot[at(2 * i + c, 64), :].astype(F32)
        send[rows, :] = ot[at(2 * i + 1 - c, 64), :]


def kb_body(xc, keep, recv, own, s1, s2, s3):
    x = xc[0]
    for k, ref in enumerate((own, s1, s2, s3)):
        b = lax.rem(x + k, 4)
        ch = at(b, 128)
        ref[0:576, :] = (keep[0:576, ch] + recv[0:576, ch].astype(F32)).astype(BF)
        rows = pl.ds(pl.multiple_of(576 + 64 * b, 64), 64)
        part = (keep[rows, :] + recv[rows, :].astype(F32)).astype(BF)
        for j in range(4):
            ref[576 + 64 * j : 640 + 64 * j, :] = part[:, 128 * j : 128 * j + 128]


def k4_body(yz, own, r1, r2, r3, nodes_t, all_grad, g0, s1, s2, s3, whole):
    y = yz[0]
    sums = total4(own[...], r1[...], r2[...], r3[...])
    whole[0:1024, :] = dot(nodes_t[...], sums[0:512, :].astype(BF)).astype(BF)
    ot = sums[576:832, :].astype(BF)
    ot = jnp.concatenate([ot[64 * j : 64 * j + 64, :] for j in range(4)], axis=1)
    gen = dot(ot, all_grad[...]).astype(BF)
    for j in range(8):
        whole[1024 + 64 * j : 1088 + 64 * j, :] = gen[:, 128 * j : 128 * j + 128]
    whole[1536:1600, :] = sums[512:576, :].astype(BF)
    for k, ref in enumerate((g0, s1, s2, s3)):
        ref[...] = whole[at(lax.rem(y + k, 4), 400), :]


def sum_body(a, b, c, d, out):
    out[...] = total4(a[...], b[...], c[...], d[...]).astype(BF)


def place_body(i, own, r1, r2, r3, out):
    rows = own.shape[0]
    for k, ref in enumerate((own, r1, r2, r3)):
        out[at(lax.rem(i[0] + 4 - k, 4), rows), :] = ref[...]


def end_body(xc, *refs):
    gne_far, gdt_far, gup_far, gen_far, gne, gdt, gup, gen, sems = refs[8:]
    x, c = xc[0], xc[1]
    copies = []

    def send(near, far):
        copy = pltpu.make_async_copy(near, far, sems.at[len(copies)])
        copy.start()
        copies.append(copy)

    for k in range(4):
        b = lax.rem(x + 4 - k, 4)
        ch = at(b, 128)
        mine, other = refs[k], refs[4 + k]
        for i, (ref, core) in enumerate(((mine, c), (other, 1 - c))):
            slot = 2 * k + i
            gne[slot] = ref[0:1024, :].astype(F32)
            send(gne.at[slot], gne_far.at[at(core, 1024), ch])
            for j in range(8):
                gen[slot, :, 128 * j : 128 * j + 128] = ref[
                    1024 + 64 * j : 1088 + 64 * j, :
                ].astype(F32)
            send(gen.at[slot], gen_far.at[at(2 * b + core, 64), :])
        mine, other = mine[1536:1600, :].astype(F32), other[1536:1600, :].astype(F32)
        gup[:, ch] = jnp.where(c == 0, mine, other)
        gdt[:, ch] = jnp.where(c == 0, other, mine)
    send(gup, gup_far)
    send(gdt, gdt_far)
    for copy in copies:
        copy.wait()


def over_x(value, k):
    perm = [(2 * x + c, 2 * ((x + k) % 4) + c) for x in range(4) for c in range(2)]
    return lax.ppermute(value, "graph", perm)


def over_core(value):
    return lax.ppermute(value, "graph", [(i, i ^ 1) for i in range(8)])


def over_y(value, k):
    perm = [(4 * y + z, 4 * ((y + k) % 4) + z) for y in range(4) for z in range(4)]
    return lax.ppermute(value, "dp", perm)


def over_z(value, k):
    perm = [(4 * y + z, 4 * y + (z + k) % 4) for y in range(4) for z in range(4)]
    return lax.ppermute(value, "dp", perm)


def tie(*values):
    return lax.optimization_barrier(values)


def local(
    nodes, node_grad, edges, source, target, trip_in, trip_out, basis, trip_count,
    w_ne, w_down, w_up, w_en,
):
    g = lax.axis_index("graph")
    d = lax.axis_index("dp")
    xc = jnp.stack([g // 2, g % 2]).astype(jnp.int32)
    yz = jnp.stack([d // 4, d % 4]).astype(jnp.int32)
    near = (1, 2, 3)

    n = [nodes[0]] + [over_x(nodes[0], k) for k in near]
    m = [over_core(n[0])]
    p = [node_grad[0]] + [over_x(node_grad[0], k) for k in near]
    m += [over_core(v) for v in n[1:]]
    down, inner, dsilu = call(
        k1_body,
        [sds((512, 128)), sds((1024, 512)), sds((1024, 512))],
        [xc, source, target, edges[0], w_ne, w_down.T, *n, *m],
        scalars=1,
        scratch=[pltpu.VMEM((512, 1024), BF), pltpu.VMEM((1024, 512), BF),
                 pltpu.VMEM((2048, 512), BF), pltpu.VMEM((1024, 512), BF),
                 pltpu.VMEM((2, 1, 1024), jnp.int32), pltpu.VMEM((64, 512), BF),
                 pltpu.VMEM((1024, 512), BF), pltpu.VMEM((1024, 512), BF),
                 pltpu.SemaphoreType.DMA((24,))],
        vmem=24, far_in=13, far_out=2,
    )

    t = [down] + [over_x(down, k) for k in near]
    u = [over_core(down)]
    _, trip_in, p[1], p[2], p[3] = tie(down, trip_in, *p[1:])
    q = [over_core(v) for v in p]
    st, il, ilt, ol, olt, basis2, in_hi, out_hi = call(
        prep_body,
        [sds((1024, 1024)), sds((2048, 512)), sds((512, 2048)), sds((2048, 512)),
         sds((512, 2048)), sds((2048, 128)), sds((2048, 128), jnp.int32),
         sds((2048, 128), jnp.int32)],
        [trip_count, source, target, trip_in, trip_out, basis[0].T],
        scalars=1, vmem=24,
    )
    (d_outer,) = call(
        kq_body,
        [sds((1024, 512))],
        [xc, target, *p, *q, w_en],
        scalars=1,
        scratch=[pltpu.VMEM((512, 1024), BF), pltpu.VMEM((512, 1024), BF),
                 pltpu.VMEM((512, 512), BF), pltpu.SemaphoreType.DMA((9,))],
        vmem=24, far_in=9,
    )
    *t, il, d_outer = tie(*t, il, d_outer)
    u += [over_core(v) for v in t[1:]]
    keep, send, outer, summed, dzed = call(
        k2_body,
        [sds((512, 512), F32), sds((512, 512)), sds((1024, 512)), sds((512, 128)),
         sds((1024, 512))],
        [xc, *t, *u, il, ilt, ol, olt, in_hi, out_hi, basis2, inner, d_outer, w_up],
        scalars=1,
        scratch=[pltpu.VMEM((512, 1024), BF), pltpu.VMEM((2048, 128), BF),
                 pltpu.VMEM((2048, 1024), BF)], vmem=32,
    )

    recv = over_core(send)
    parts = call(ka_body, [sds((512, 128))] * 4, [xc, keep, recv], scalars=1, vmem=8)
    dd = [parts[0]] + [over_x(parts[k], k) for k in near]
    ot, gup, o_keep, o_send = call(
        ko_body,
        [sds((512, 512)), sds((64, 512), F32), sds((256, 512), F32), sds((256, 512))],
        [xc, outer, st, summed, dzed], scalars=1, vmem=16,
    )
    o_recv = over_core(o_send)
    edge_grad, keep, send = call(
        k3_body,
        [sds((1024, 512)), sds((832, 512), F32), sds((832, 512))],
        [xc, *dd, d_outer, dsilu, inner, st, w_down.T, ot, gup],
        scalars=1, scratch=[pltpu.VMEM((1024, 512), BF)], vmem=24,
    )

    recv = over_core(send)
    parts = call(kb_body, [sds((832, 128))] * 4, [xc, keep, recv], scalars=1, vmem=12)
    recv, o_recv, *held = tie(recv, o_recv, *n, *m, *p, *q)
    o_parts = call(kr_body, [sds((64, 512))] * 4, [xc, o_keep, o_recv], scalars=1, vmem=8)
    nodes_t, all_grad = call(
        kw_body,
        [sds((1024, 512)), sds((512, 1024))],
        [xc, *held],
        scalars=1, scratch=[pltpu.VMEM((512, 1024), BF), pltpu.SemaphoreType.DMA((16,))],
        vmem=16, far_in=16,
    )
    parts = [parts[0]] + [over_x(parts[k], k) for k in near]
    *parts, nodes_t, all_grad = tie(*parts, nodes_t, all_grad)
    parts = call(
        k4_body, [sds((400, 128))] * 4, [yz, *parts, nodes_t, all_grad],
        scalars=1, scratch=[pltpu.VMEM((1600, 128), BF)], vmem=16,
    )
    parts = [parts[0]] + [over_y(parts[k], k) for k in near]
    (part,) = call(sum_body, [sds((400, 128))], parts, vmem=8)
    parts = [part] + [over_z(part, k) for k in near]
    o_parts = [o_parts[0]] + [over_x(o_parts[k], k) for k in near]
    *o_parts, p0, p1, p2, p3 = tie(*o_parts, *parts)
    (part,) = call(sum_body, [sds((400, 128))], [p0, p1, p2, p3], vmem=8)
    (new_nodes,) = call(kn_body, [sds((64, 1024))], [*o_parts, nodes[0], w_en], vmem=16)
    parts = [part] + [over_y(part, k) for k in near]
    new_nodes, *parts = tie(new_nodes, *parts)
    (part,) = call(place_body, [sds((1600, 128))], [yz, *parts], scalars=1, vmem=8)
    parts = [part] + [over_x(part, k) for k in near]
    parts += [over_core(v) for v in parts]
    grad_ne, grad_down_t, grad_up, grad_en = call(
        end_body,
        [sds((2048, 512), F32), sds((64, 512), F32), sds((64, 512), F32), sds((512, 1024), F32)],
        [xc, *parts],
        scalars=1,
        scratch=[pltpu.VMEM((8, 1024, 128), F32), pltpu.VMEM((64, 512), F32),
                 pltpu.VMEM((64, 512), F32), pltpu.VMEM((8, 64, 1024), F32),
                 pltpu.SemaphoreType.DMA((18,))],
        vmem=24, far_out=4,
    )
    return (new_nodes[None], edge_grad[None], grad_ne, grad_down_t.T, grad_up, grad_en)


def solution(mesh):
    split3, split2 = P("dp", "graph", None), P("dp", "graph")
    in_specs = (split3,) * 3 + (split2,) * 4 + (split3, split2) + (P(),) * 4
    out_specs = (split3, split3, P(), P(), P(), P())
    return jax.shard_map(local, mesh=mesh, in_specs=in_specs, out_specs=out_specs, check_vma=False)
```

```python
import jax
import jax.numpy as jnp
from jax import lax
from jax.experimental import pallas as pl
from jax.experimental.pallas import tpu as pltpu
from jax.sharding import PartitionSpec as P

BF = jnp.bfloat16
F32 = jnp.float32
NT = (((1,), (1,)), ((), ()))


def dot(a, b):
    return jnp.dot(a, b, preferred_element_type=F32)


def dot_nt(a, b):
    return lax.dot_general(a, b, NT, preferred_element_type=F32)


def call(
    body, outs, args, scalars=0, scratch=(), vmem=40, any_in=0, far_in=0, far_out=0
):
    n_in, n_out = len(args), len(outs)
    in_specs = [pl.BlockSpec(memory_space=pltpu.SMEM)] * scalars
    in_specs += [pl.BlockSpec(memory_space=pltpu.VMEM)] * (n_in - scalars - any_in - far_in)
    in_specs += [pl.BlockSpec(memory_space=pl.ANY)] * any_in
    in_specs += [pl.BlockSpec(memory_space=pltpu.HBM)] * far_in
    out_specs = [pl.BlockSpec(memory_space=pltpu.VMEM)] * (n_out - far_out)
    out_specs += [pl.BlockSpec(memory_space=pltpu.HBM)] * far_out
    near, far = args[: n_in - far_in], args[n_in - far_in :]
    return pl.pallas_call(
        body,
        out_shape=[
            pltpu.HBM(o.shape, o.dtype) if i >= n_out - far_out else o for i, o in enumerate(outs)
        ],
        in_specs=in_specs,
        out_specs=out_specs,
        scratch_shapes=list(scratch),
        compiler_params=pltpu.CompilerParams(vmem_limit_bytes=vmem << 20),
        cost_estimate=pl.CostEstimate(flops=1, bytes_accessed=1, transcendentals=0),
    )(*near, *(pltpu.with_memory_space_constraint(a, pltpu.HBM) for a in far))


def sds(shape, dtype=BF):
    return jax.ShapeDtypeStruct(shape, dtype)


def at(i, size):
    return pl.ds(pl.multiple_of(i * size, size), size)


def hot(mask):
    return jnp.where(mask, 1.0, 0.0).astype(BF)


def left(w):
    return jnp.concatenate([w, jnp.zeros_like(w)], axis=0)


def right(w):
    return jnp.concatenate([jnp.zeros_like(w), w], axis=0)


def column(row):
    return jnp.broadcast_to(row.astype(F32), (128, row.shape[1])).T.astype(jnp.int32)


def hot_rows(col, width):
    lane = lax.broadcasted_iota(jnp.int32, col.shape, 1)
    return jnp.concatenate([hot(col == lane + j) for j in range(0, width, 128)], axis=1)


def prep_body(
    cnt, src_r, tgt_r, in_r, out_r, basis_t, st, il, ilt, ol, olt, basis, in_hi, out_hi
):
    row = lax.broadcasted_iota(jnp.int32, (128, 1024), 0)
    for i in range(4):
        ch = slice(128 * i, 128 * i + 128)
        st[ch, :] = hot(src_r[...] == row + 128 * i)
        st[512 + 128 * i : 640 + 128 * i, :] = hot(tgt_r[...] == row + 128 * i)
    pos = lax.broadcasted_iota(jnp.int32, (1, 2048), 1)
    live = pos < cnt[0, 0]
    in_lo = jnp.where(live, in_r[...] & 511, -1)
    out_lo = out_r[...] & 511
    for i in range(8):
        ch = slice(256 * i, 256 * i + 256)
        il[ch, :] = hot_rows(column(in_lo[:, ch]), 512)
        ol[ch, :] = hot_rows(column(out_lo[:, ch]), 512)
        in_hi[ch, :] = column(in_r[:, ch] >> 9)
        out_hi[ch, :] = column(out_r[:, ch] >> 9)
    row = lax.broadcasted_iota(jnp.int32, (64, 2048), 0)
    for i in range(8):
        ch = slice(64 * i, 64 * i + 64)
        ilt[ch, :] = hot(in_lo == row + 64 * i)
        olt[ch, :] = hot(out_lo == row + 64 * i)
    basis[...] = jnp.concatenate([basis_t[...], basis_t[...]], axis=0).T


def fetch(far, near, sem):
    copy = pltpu.make_async_copy(far, near, sem)
    copy.start()
    return copy


def gathered(xc, refs, out, sems):
    x, c = xc[0], xc[1]
    copies = []
    for k in range(4):
        g = 2 * lax.rem(x + 4 - k, 4)
        copies.append(fetch(refs[k], out.at[at(g + c, 64), :], sems.at[2 * k]))
        copies.append(fetch(refs[4 + k], out.at[at(g + 1 - c, 64), :], sems.at[2 * k + 1]))
    return copies


def k1_body(xc, *refs):
    ends_far, edges_far, w_far = refs[0:2], refs[2], refs[3]
    down, inner_far, dsilu_far, nodes, ab, w_ne, edges, ends, wd_t, inner, dsilu, s, sems = refs[13:]
    loads = [fetch(ends_far[i], ends.at[i], sems.at[i]) for i in range(2)]
    loads.append(fetch(refs[4], wd_t, sems.at[2]))
    blocks = gathered(xc, refs[5:13], nodes, sems.at[pl.ds(8, 8)])
    halves_of_w = [
        fetch(w_far.at[rows, :], w_ne.at[rows, :], sems.at[3 + h])
        for h, rows in enumerate((slice(0, 1024), slice(1024, 2048)))
    ]
    load_edges = fetch(edges_far, edges, sems.at[5])
    for copy in loads:
        copy.wait()
    wd = (left(wd_t[...]), right(wd_t[...]))
    for i in range(4):
        ch = slice(256 * i, 256 * i + 256)
        for j in range(2):
            s[ch, 512 * j : 512 * j + 512] = hot_rows(column(ends[j, :, ch]), 512)
    for copy in blocks:
        copy.wait()
    for h in range(2):
        halves_of_w[h].wait()
        for i in range(2):
            rows = slice(512 * h + 256 * i, 512 * h + 256 * i + 256)
            ab[rows, :] = dot(
                nodes[256 * i : 256 * i + 256, :], w_ne[1024 * h : 1024 * h + 1024, :]
            ).astype(BF)
    load_edges.wait()
    copies = []
    for i in range(2):
        total = None
        for h in range(2):
            ch = slice(512 * h + 256 * i, 512 * h + 256 * i + 256)
            pre = dot(s[ch, :], ab[...])
            sig = jax.nn.sigmoid(pre)
            held = (edges[ch, :].astype(F32) + pre * sig).astype(BF)
            inner[ch, :] = held
            dsilu[ch, :] = (sig * (1.0 + pre * (1.0 - sig))).astype(BF)
            for near, far in ((inner, inner_far), (dsilu, dsilu_far)):
                copies.append(fetch(near.at[ch, :], far.at[ch, :], sems.at[16 + len(copies)]))
            part = dot_nt(held, wd[h])
            total = part if total is None else total + part
        down[256 * i : 256 * i + 256, :] = total.astype(BF)
    for copy in copies:
        copy.wait()


def kq_body(xc, tgt_r, *refs):
    w_far, d_outer, all_grad, w_en, q, s, sems = refs[8:]
    load = fetch(w_far, w_en, sems.at[8])
    blocks = gathered(xc, refs[:8], all_grad, sems)
    for i in range(4):
        ch = slice(256 * i, 256 * i + 256)
        s[ch, :] = hot_rows(column(tgt_r[:, ch]), 512)
    for copy in blocks:
        copy.wait()
    load.wait()
    for i in range(2):
        ch = slice(256 * i, 256 * i + 256)
        q[ch, :] = dot_nt(all_grad[ch, :], w_en[...]).astype(BF)
    for i in range(4):
        ch = slice(256 * i, 256 * i + 256)
        d_outer[ch, :] = dot(s[ch, :], q[...]).astype(BF)


def kw_body(xc, *refs):
    nodes_t, all_grad, nodes, sems = refs[16:]
    copies = gathered(xc, refs[:8], nodes, sems)
    late = gathered(xc, refs[8:16], all_grad, sems.at[pl.ds(8, 8)])
    for copy in copies:
        copy.wait()
    nodes_t[...] = nodes[...].T
    for copy in late:
        copy.wait()


def halves(value, odd, upper):
    kept = jnp.where(upper == odd, value, 0.0)
    return kept + pltpu.roll(kept, 64, 1)


def k2_body(
    xc, d0, d1, d2, d3, e0, e1, e2, e3, il, ilt, ol, olt, in_hi, out_hi, basis, inner, d_outer, w_up,
    keep, send, outer, summed, dzed, table, gath, spread,
):
    x, c = xc[0], xc[1]
    for k, (mine, other) in enumerate(((d0, e0), (d1, e1), (d2, e2), (d3, e3))):
        g = 2 * lax.rem(x + 4 - k, 4)
        table[:, at(g + c, 128)] = mine[...]
        table[:, at(g + 1 - c, 128)] = other[...]
    upper = lax.broadcasted_iota(jnp.int32, (256, 128), 1) >= 64
    for i in range(8):
        ch = slice(256 * i, 256 * i + 256)
        got = dot(il[ch, :], table[...])
        hi = in_hi[ch, :]
        acc = jnp.zeros((256, 128), F32)
        for g in range(8):
            acc = jnp.where((hi >> 1) == g, got[:, 128 * g : 128 * g + 128], acc)
        term = halves(acc, (hi & 1) == 1, upper) * basis[ch, :].astype(F32)
        gath[ch, :] = jnp.where(upper == (out_hi[ch, :] == 1), term, 0.0).astype(BF)
    held = dot(olt[...], gath[...]).astype(BF)
    summed[...] = held
    d_sum = jnp.zeros((512, 128), F32)
    for h, w in enumerate((left(w_up[...]), right(w_up[...]))):
        ch = slice(512 * h, 512 * h + 512)
        zed = dot(held, w)
        sig = jax.nn.sigmoid(zed)
        outer[ch, :] = (inner[ch, :].astype(F32) + zed * sig).astype(BF)
        dz = (d_outer[ch, :].astype(F32) * (sig * (1.0 + zed * (1.0 - sig)))).astype(BF)
        dzed[ch, :] = dz
        d_sum += dot_nt(dz, w)
    d_sum = d_sum.astype(BF)
    for i in range(8):
        ch = slice(256 * i, 256 * i + 256)
        got = dot(ol[ch, :], d_sum)
        term = halves(got, out_hi[ch, :] == 1, upper) * basis[ch, :].astype(F32)
        hi = in_hi[ch, :]
        term = jnp.where(upper == ((hi & 1) == 1), term, 0.0).astype(BF)
        owner = (hi >> 1).astype(F32).astype(BF)
        for g in range(8):
            spread[ch, 128 * g : 128 * g + 128] = jnp.where(owner == g, term, jnp.zeros_like(term))
    whole = [dot(ilt[...], spread[:, 512 * i : 512 * i + 512]) for i in range(2)]
    for i in range(4):
        ch = slice(128 * i, 128 * i + 128)
        part = whole[i // 2][:, 256 * (i % 2) : 256 * (i % 2) + 256]
        low, high = part[:, 0:128], part[:, 128:256]
        keep[:, ch] = jnp.where(c == 0, low, high)
        send[:, ch] = jnp.where(c == 0, high, low).astype(BF)


def ko_body(xc, outer, st, summed, dzed, ot, gup, keep, send):
    c = xc[1]
    for i in range(2):
        ch = slice(256 * i, 256 * i + 256)
        part = dot(st[512 + 256 * i : 768 + 256 * i, :], outer[...])
        ot[:, ch] = part.T.astype(BF)
        for j in range(2):
            low, high = part[128 * j : 128 * j + 64, :], part[128 * j + 64 : 128 * j + 128, :]
            rows = slice(128 * i + 64 * j, 128 * i + 64 * j + 64)
            keep[rows, :] = jnp.where(c == 0, low, high)
            send[rows, :] = jnp.where(c == 0, high, low).astype(BF)
    summed_t = summed[...].T
    gup[...] = dot(summed_t[0:64, :], dzed[0:512, :]) + dot(summed_t[64:128, :], dzed[512:1024, :])


def kr_body(xc, keep, recv, own, s1, s2, s3):
    x = xc[0]
    for k, ref in enumerate((own, s1, s2, s3)):
        rows = at(lax.rem(x + k, 4), 64)
        ref[...] = (keep[rows, :] + recv[rows, :].astype(F32)).astype(BF)


def kn_body(own, r1, r2, r3, nodes, w_en, out):
    rows = total4(own[...], r1[...], r2[...], r3[...]).astype(BF)
    out[...] = (nodes[...].astype(F32) + dot(rows, w_en[...])).astype(BF)


def ka_body(xc, keep, recv, own, s1, s2, s3):
    x = xc[0]
    for k, ref in enumerate((own, s1, s2, s3)):
        ch = at(lax.rem(x + k, 4), 128)
        ref[...] = (keep[:, ch] + recv[:, ch].astype(F32)).astype(BF)


def total4(a, b, c, d):
    return (a.astype(F32) + c.astype(F32)) + (b.astype(F32) + d.astype(F32))


def k3_body(
    xc, own, r1, r2, r3, d_outer, dsilu, inner, st, w_down_t, ot, gup, edge_grad, keep, send, d_pre
):
    c = xc[1]
    dd = total4(own[...], r1[...], r2[...], r3[...]).astype(BF)
    for h, w in enumerate((left(w_down_t[...]), right(w_down_t[...]))):
        for i in range(2):
            rows = slice(256 * i, 256 * i + 256)
            ch = slice(512 * h + 256 * i, 512 * h + 256 * i + 256)
            d_inner = d_outer[ch, :].astype(F32) + dot(dd[rows, :], w)
            edge_grad[ch, :] = d_inner.astype(BF)
            d_pre[ch, :] = (d_inner * dsilu[ch, :].astype(F32)).astype(BF)
    for i in range(2):
        rows = slice(256 * i, 256 * i + 256)
        send[rows, :] = dot(st[at(2 * (1 - c) + i, 256), :], d_pre[...]).astype(BF)
        keep[rows, :] = dot(st[at(2 * c + i, 256), :], d_pre[...])
    ddt = dd.T
    gdown = dot(ddt[0:64, :], inner[0:512, :]) + dot(ddt[64:128, :], inner[512:1024, :])
    keep[512:576, :] = jnp.where(c == 0, gup[...], gdown)
    send[512:576, :] = jnp.where(c == 0, gdown, gup[...]).astype(BF)
    for i in range(4):
        rows = slice(576 + 64 * i, 640 + 64 * i)
        keep[rows, :] = ot[at(2 * i + c, 64), :].astype(F32)
        send[rows, :] = ot[at(2 * i + 1 - c, 64), :]


def kb_body(xc, keep, recv, own, s1, s2, s3):
    x = xc[0]
    for k, ref in enumerate((own, s1, s2, s3)):
        b = lax.rem(x + k, 4)
        ch = at(b, 128)
        ref[0:576, :] = (keep[0:576, ch] + recv[0:576, ch].astype(F32)).astype(BF)
        rows = pl.ds(pl.multiple_of(576 + 64 * b, 64), 64)
        part = (keep[rows, :] + recv[rows, :].astype(F32)).astype(BF)
        for j in range(4):
            ref[576 + 64 * j : 640 + 64 * j, :] = part[:, 128 * j : 128 * j + 128]


def k4_body(i, own, r1, r2, r3, nodes_t, all_grad, g0, s1, s2, s3, whole):
    sums = total4(own[...], r1[...], r2[...], r3[...])
    gne = dot(nodes_t[...], sums[0:512, :].astype(BF)).astype(BF)
    ot = sums[576:832, :].astype(BF)
    ot = jnp.concatenate([ot[64 * j : 64 * j + 64, :] for j in range(4)], axis=1)
    gen = dot(ot, all_grad[...]).astype(BF)
    for q in range(4):
        at_q = 400 * q
        whole[at_q : at_q + 256, :] = gne[256 * q : 256 * q + 256, :]
        for j in range(2):
            rows = slice(at_q + 256 + 64 * j, at_q + 320 + 64 * j)
            whole[rows, :] = gen[:, 256 * q + 128 * j : 256 * q + 128 * j + 128]
        whole[at_q + 384 : at_q + 400, :] = sums[512 + 16 * q : 528 + 16 * q, :].astype(BF)
    for k, ref in enumerate((g0, s1, s2, s3)):
        ref[...] = whole[at(lax.rem(i[0] + k, 4), 400), :]


def sum_body(a, b, c, d, out):
    out[...] = total4(a[...], b[...], c[...], d[...]).astype(BF)


def place_body(i, own, r1, r2, r3, out):
    rows = own.shape[0]
    for k, ref in enumerate((own, r1, r2, r3)):
        out[at(lax.rem(i[0] + 4 - k, 4), rows), :] = ref[...]


def spread_out(taken, xc, yz, mine, other, gne_far, gen_far, small, rows, cols, gen, sems):
    x, c, z = xc[0], xc[1], yz[1]

    def run(zeros, ones):
        copies = []

        def send(near, far):
            copies.append(fetch(near, far, sems.at[len(copies)]))

        for i, k in enumerate(taken):
            b, q = lax.rem(x + 4 - k, 4), lax.rem(z + 4 - k, 4)
            for j in range(4):
                value = zeros[i][400 * j : 400 * j + 400, :].astype(F32)
                cols[i, 256 * j : 256 * j + 256, :] = value[0:256]
                for h in range(2):
                    gen[0, i, :, 256 * j + 128 * h : 256 * j + 128 * h + 128] = value[
                        256 + 64 * h : 320 + 64 * h
                    ]
                small[0, 16 * j : 16 * j + 16, at(b, 128)] = value[384:400]
            send(cols.at[i], gne_far.at[0:1024, at(b, 128)])
            send(gen.at[0, i], gen_far.at[b, 0])
            for j in range(4):
                value = ones[i][400 * j : 400 * j + 400, :].astype(F32)
                rows[i, :, 128 * j : 128 * j + 128] = value[0:256]
                for h in range(2):
                    gen[1, i, :, 256 * j + 128 * h : 256 * j + 128 * h + 128] = value[
                        256 + 64 * h : 320 + 64 * h
                    ]
                small[1, at(q, 16), 128 * j : 128 * j + 128] = value[384:400]
            send(rows.at[i], gne_far.at[at(4 + q, 256), :])
            for j in range(4):
                send(gen.at[1, i, :, 256 * j : 256 * j + 256], gen_far.at[j, 1, :, at(q, 256)])
        for copy in copies:
            copy.wait()

    @pl.when(c == 0)
    def _():
        run(mine, other)

    @pl.when(c == 1)
    def _():
        run(other, mine)


def end_body(xc, yz, *refs):
    gup, gdt, gne_far, gen_far, small, rows, cols, gen, sems = refs[8:]
    mine, other = refs[0:4], refs[4:8]
    spread_out(range(4), xc, yz, mine, other, gne_far, gen_far, small, rows, cols, gen, sems)
    gup[...] = small[0]
    gdt[...] = small[1]


def over_x(value, k):
    perm = [(2 * x + c, 2 * ((x + k) % 4) + c) for x in range(4) for c in range(2)]
    return lax.ppermute(value, "graph", perm)


def over_core(value):
    return lax.ppermute(value, "graph", [(i, i ^ 1) for i in range(8)])


def over_dp(value, k, axes):
    perm = []
    for y in range(4):
        for z in range(4):
            for x in range(4):
                for c in range(2):
                    at = {"x": x, "y": y, "z": z}
                    at[axes[c]] = (at[axes[c]] + k) % 4
                    to = 8 * (4 * at["y"] + at["z"]) + 2 * at["x"] + c
                    perm.append((8 * (4 * y + z) + 2 * x + c, to))
    return lax.ppermute(value, ("dp", "graph"), perm)


def tie(*values):
    return lax.optimization_barrier(values)


def local(
    nodes, node_grad, edges, source, target, trip_in, trip_out, basis, trip_count,
    w_ne, w_down, w_up, w_en,
):
    g = lax.axis_index("graph")
    d = lax.axis_index("dp")
    xc = jnp.stack([g // 2, g % 2]).astype(jnp.int32)
    yz = jnp.stack([d // 4, d % 4]).astype(jnp.int32)
    of_part = jnp.where(xc[1] == 0, yz[0], yz[1])[None]
    of_place = jnp.where(xc[1] == 0, yz[0], xc[0])[None]
    near = (1, 2, 3)

    n = [nodes[0]] + [over_x(nodes[0], k) for k in near]
    m = [over_core(n[0])]
    p = [node_grad[0]] + [over_x(node_grad[0], k) for k in near]
    m += [over_core(v) for v in n[1:]]
    down, inner, dsilu = call(
        k1_body,
        [sds((512, 128)), sds((1024, 512)), sds((1024, 512))],
        [xc, source, target, edges[0], w_ne, w_down.T, *n, *m],
        scalars=1,
        scratch=[pltpu.VMEM((512, 1024), BF), pltpu.VMEM((1024, 512), BF),
                 pltpu.VMEM((2048, 512), BF), pltpu.VMEM((1024, 512), BF),
                 pltpu.VMEM((2, 1, 1024), jnp.int32), pltpu.VMEM((64, 512), BF),
                 pltpu.VMEM((1024, 512), BF), pltpu.VMEM((1024, 512), BF),
                 pltpu.VMEM((1024, 1024), BF), pltpu.SemaphoreType.DMA((24,))],
        vmem=24, far_in=13, far_out=2,
    )

    t = [down] + [over_x(down, k) for k in near]
    u = [over_core(down)]
    _, trip_in, p[1], p[2], p[3] = tie(down, trip_in, *p[1:])
    q = [over_core(v) for v in p]
    st, il, ilt, ol, olt, basis2, in_hi, out_hi = call(
        prep_body,
        [sds((1024, 1024)), sds((2048, 512)), sds((512, 2048)), sds((2048, 512)),
         sds((512, 2048)), sds((2048, 128)), sds((2048, 128), jnp.int32),
         sds((2048, 128), jnp.int32)],
        [trip_count, source, target, trip_in, trip_out, basis[0].T],
        scalars=1, vmem=24,
    )
    (d_outer,) = call(
        kq_body,
        [sds((1024, 512))],
        [xc, target, *p, *q, w_en],
        scalars=1,
        scratch=[pltpu.VMEM((512, 1024), BF), pltpu.VMEM((512, 1024), BF),
                 pltpu.VMEM((512, 512), BF), pltpu.VMEM((1024, 512), BF),
                 pltpu.SemaphoreType.DMA((9,))],
        vmem=24, far_in=9,
    )
    *t, il, d_outer = tie(*t, il, d_outer)
    u += [over_core(v) for v in t[1:]]
    keep, send, outer, summed, dzed = call(
        k2_body,
        [sds((512, 512), F32), sds((512, 512)), sds((1024, 512)), sds((512, 128)),
         sds((1024, 512))],
        [xc, *t, *u, il, ilt, ol, olt, in_hi, out_hi, basis2, inner, d_outer, w_up],
        scalars=1,
        scratch=[pltpu.VMEM((512, 1024), BF), pltpu.VMEM((2048, 128), BF),
                 pltpu.VMEM((2048, 1024), BF)], vmem=32,
    )

    recv = over_core(send)
    parts = call(ka_body, [sds((512, 128))] * 4, [xc, keep, recv], scalars=1, vmem=8)
    dd = [parts[0]] + [over_x(parts[k], k) for k in near]
    ot, gup, o_keep, o_send = call(
        ko_body,
        [sds((512, 512)), sds((64, 512), F32), sds((256, 512), F32), sds((256, 512))],
        [xc, outer, st, summed, dzed], scalars=1, vmem=16,
    )
    o_recv = over_core(o_send)
    edge_grad, keep, send = call(
        k3_body,
        [sds((1024, 512)), sds((832, 512), F32), sds((832, 512))],
        [xc, *dd, d_outer, dsilu, inner, st, w_down.T, ot, gup],
        scalars=1, scratch=[pltpu.VMEM((1024, 512), BF)], vmem=24,
    )

    recv = over_core(send)
    parts = call(kb_body, [sds((832, 128))] * 4, [xc, keep, recv], scalars=1, vmem=12)
    recv, o_recv, *held = tie(recv, o_recv, *n, *m, *p, *q)
    o_parts = call(kr_body, [sds((64, 512))] * 4, [xc, o_keep, o_recv], scalars=1, vmem=8)
    nodes_t, all_grad = call(
        kw_body,
        [sds((1024, 512)), sds((512, 1024))],
        [xc, *held],
        scalars=1, scratch=[pltpu.VMEM((512, 1024), BF), pltpu.SemaphoreType.DMA((16,))],
        vmem=16, far_in=16,
    )
    parts = [parts[0]] + [over_x(parts[k], k) for k in near]
    *parts, nodes_t, all_grad = tie(*parts, nodes_t, all_grad)
    parts = call(
        k4_body, [sds((400, 128))] * 4, [of_part, *parts, nodes_t, all_grad],
        scalars=1, scratch=[pltpu.VMEM((1600, 128), BF)], vmem=16,
    )
    parts = [parts[0]] + [over_dp(parts[k], k, "yz") for k in near]
    (part,) = call(sum_body, [sds((400, 128))], parts, vmem=8)
    parts = [part] + [over_dp(part, k, "zy") for k in near]
    o_parts = [o_parts[0]] + [over_x(o_parts[k], k) for k in near]
    *o_parts, p0, p1, p2, p3 = tie(*o_parts, *parts)
    (part,) = call(sum_body, [sds((400, 128))], [p0, p1, p2, p3], vmem=8)
    (new_nodes,) = call(kn_body, [sds((64, 1024))], [*o_parts, nodes[0], w_en], vmem=16)
    parts = [part] + [over_dp(part, k, "yx") for k in near]
    new_nodes, *parts = tie(new_nodes, *parts)
    (part,) = call(place_body, [sds((1600, 128))], [of_place, *parts], scalars=1, vmem=8)
    parts = [part] + [over_dp(part, k, "xz") for k in near]
    grad_up, grad_down_t, grad_ne, grad_en = call(
        end_body,
        [sds((64, 512), F32), sds((64, 512), F32), sds((2048, 512), F32),
         sds((4, 2, 64, 1024), F32)],
        [xc, yz, *parts, *[over_core(v) for v in parts]],
        scalars=2,
        scratch=[pltpu.VMEM((2, 64, 512), F32), pltpu.VMEM((4, 256, 512), F32),
                 pltpu.VMEM((4, 1024, 128), F32), pltpu.VMEM((2, 4, 64, 1024), F32),
                 pltpu.SemaphoreType.DMA((28,))],
        vmem=24, far_out=2,
    )
    grad_en = grad_en.reshape(512, 1024)
    return (new_nodes[None], edge_grad[None], grad_ne, grad_down_t.T, grad_up, grad_en)


def solution(mesh):
    split3, split2 = P("dp", "graph", None), P("dp", "graph")
    in_specs = (split3,) * 3 + (split2,) * 4 + (split3, split2) + (P(),) * 4
    out_specs = (split3, split3, P(), P(), P(), P())
    return jax.shard_map(local, mesh=mesh, in_specs=in_specs, out_specs=out_specs, check_vma=False)
```

```python
import jax
import jax.numpy as jnp
from jax import lax
from jax.experimental import pallas as pl
from jax.experimental.pallas import tpu as pltpu
from jax.sharding import PartitionSpec as P

BF = jnp.bfloat16
F32 = jnp.float32
NT = (((1,), (1,)), ((), ()))


def dot(a, b):
    return jnp.dot(a, b, preferred_element_type=F32)


def dot_nt(a, b):
    return lax.dot_general(a, b, NT, preferred_element_type=F32)


def call(
    body, outs, args, here="", scalars=0, scratch=(), vmem=40, any_in=0, far_in=0, far_out=0
):
    n_in, n_out = len(args), len(outs)

    def placed(*refs):
        g, d = lax.axis_index("graph"), lax.axis_index("dp")
        x, c, y, z = g >> 1, g & 1, d >> 2, d & 3
        names = {
            "": (), "x": ((x, c),), "xy": ((x, c), (y, z)),
            "part": ((jnp.where(c == 0, y, z),),), "place": ((jnp.where(c == 0, y, x),),),
        }
        body(*names[here], *refs)

    in_specs = [pl.BlockSpec(memory_space=pltpu.SMEM)] * scalars
    in_specs += [pl.BlockSpec(memory_space=pltpu.VMEM)] * (n_in - scalars - any_in - far_in)
    in_specs += [pl.BlockSpec(memory_space=pl.ANY)] * any_in
    in_specs += [pl.BlockSpec(memory_space=pltpu.HBM)] * far_in
    out_specs = [pl.BlockSpec(memory_space=pltpu.VMEM)] * (n_out - far_out)
    out_specs += [pl.BlockSpec(memory_space=pltpu.HBM)] * far_out
    near, far = args[: n_in - far_in], args[n_in - far_in :]
    return pl.pallas_call(
        placed if here else body,
        out_shape=[
            pltpu.HBM(o.shape, o.dtype) if i >= n_out - far_out else o for i, o in enumerate(outs)
        ],
        in_specs=in_specs,
        out_specs=out_specs,
        scratch_shapes=list(scratch),
        compiler_params=pltpu.CompilerParams(vmem_limit_bytes=vmem << 20),
        cost_estimate=pl.CostEstimate(flops=1, bytes_accessed=1, transcendentals=0),
    )(*near, *(pltpu.with_memory_space_constraint(a, pltpu.HBM) for a in far))


def sds(shape, dtype=BF):
    return jax.ShapeDtypeStruct(shape, dtype)


def at(i, size):
    return pl.ds(pl.multiple_of(i * size, size), size)


def hot(mask):
    return jnp.where(mask, 1.0, 0.0).astype(BF)


def left(w):
    return jnp.concatenate([w, jnp.zeros_like(w)], axis=0)


def right(w):
    return jnp.concatenate([jnp.zeros_like(w), w], axis=0)


def column(row):
    return jnp.broadcast_to(row.astype(F32), (128, row.shape[1])).T.astype(jnp.int32)


def hot_rows(col, width):
    lane = lax.broadcasted_iota(jnp.int32, col.shape, 1)
    return jnp.concatenate([hot(col == lane + j) for j in range(0, width, 128)], axis=1)


def prep_body(cnt, *refs):
    s, st, il, ilt, ol, olt, basis, in_hi, out_hi, w_ne, edges = refs[7:18]
    src_r, tgt_r, in_r, out_r, basis_t, sems = refs[18:]
    nears = (src_r, tgt_r, in_r, out_r, basis_t, w_ne, edges)
    loads = [fetch(refs[i], near, sems.at[i]) for i, near in enumerate(nears)]
    for copy in loads[:4]:
        copy.wait()
    for i in range(4):
        ch = slice(256 * i, 256 * i + 256)
        s[ch, 0:512] = hot_rows(column(src_r[:, ch]), 512)
        s[ch, 512:1024] = hot_rows(column(tgt_r[:, ch]), 512)
    row = lax.broadcasted_iota(jnp.int32, (128, 1024), 0)
    for i in range(4):
        ch = slice(128 * i, 128 * i + 128)
        st[ch, :] = hot(src_r[...] == row + 128 * i)
        st[512 + 128 * i : 640 + 128 * i, :] = hot(tgt_r[...] == row + 128 * i)
    pos = lax.broadcasted_iota(jnp.int32, (1, 2048), 1)
    live = pos < cnt[0, 0]
    in_lo = jnp.where(live, in_r[...] & 511, -1)
    out_lo = out_r[...] & 511
    for i in range(8):
        ch = slice(256 * i, 256 * i + 256)
        il[ch, :] = hot_rows(column(in_lo[:, ch]), 512)
        ol[ch, :] = hot_rows(column(out_lo[:, ch]), 512)
        in_hi[ch, :] = column(in_r[:, ch] >> 9)
        out_hi[ch, :] = column(out_r[:, ch] >> 9)
    row = lax.broadcasted_iota(jnp.int32, (64, 2048), 0)
    for i in range(8):
        ch = slice(64 * i, 64 * i + 64)
        ilt[ch, :] = hot(in_lo == row + 64 * i)
        olt[ch, :] = hot(out_lo == row + 64 * i)
    for copy in loads[4:]:
        copy.wait()
    basis[...] = jnp.concatenate([basis_t[...], basis_t[...]], axis=0).T


def fetch(far, near, sem):
    copy = pltpu.make_async_copy(far, near, sem)
    copy.start()
    return copy


def gathered(xc, refs, out):
    x, c = xc
    for k in range(4):
        g = 2 * lax.rem(x + 4 - k, 4)
        out[at(g + c, 64), :] = refs[k][...]
        out[at(g + 1 - c, 64), :] = refs[4 + k][...]


def k1_body(xc, *refs):
    s, edges, w_ne, w_down_t, down, inner, dsilu, nodes, ab = refs[8:]
    gathered(xc, refs[:8], nodes)
    for h in range(2):
        for i in range(2):
            rows = slice(512 * h + 256 * i, 512 * h + 256 * i + 256)
            ab[rows, :] = dot(
                nodes[256 * i : 256 * i + 256, :], w_ne[1024 * h : 1024 * h + 1024, :]
            ).astype(BF)
    wd = (left(w_down_t[...]), right(w_down_t[...]))
    for i in range(2):
        total = None
        for h in range(2):
            ch = slice(512 * h + 256 * i, 512 * h + 256 * i + 256)
            pre = dot(s[ch, :], ab[...])
            sig = jax.nn.sigmoid(pre)
            held = (edges[ch, :].astype(F32) + pre * sig).astype(BF)
            inner[ch, :] = held
            dsilu[ch, :] = (sig * (1.0 + pre * (1.0 - sig))).astype(BF)
            part = dot_nt(held, wd[h])
            total = part if total is None else total + part
        down[256 * i : 256 * i + 256, :] = total.astype(BF)


def kq_body(xc, *refs):
    w_en, s, d_outer, all_grad, q = refs[8:]
    gathered(xc, refs[:8], all_grad)
    for i in range(2):
        ch = slice(256 * i, 256 * i + 256)
        q[ch, :] = dot_nt(all_grad[ch, :], w_en[...]).astype(BF)
    for i in range(4):
        ch = slice(256 * i, 256 * i + 256)
        d_outer[ch, :] = dot(s[ch, 512:1024], q[...]).astype(BF)


def kw_body(nodes, nodes_t):
    nodes_t[...] = nodes[...].T


def halves(value, odd, upper):
    kept = jnp.where(upper == odd, value, 0.0)
    return kept + pltpu.roll(kept, 64, 1)


def k2_body(
    xc, d0, d1, d2, d3, e0, e1, e2, e3, il, ilt, ol, olt, in_hi, out_hi, basis, inner, d_outer, w_up,
    keep, send, outer, summed, dzed, table, gath, spread,
):
    x, c = xc[0], xc[1]
    for k, (mine, other) in enumerate(((d0, e0), (d1, e1), (d2, e2), (d3, e3))):
        g = 2 * lax.rem(x + 4 - k, 4)
        table[:, at(g + c, 128)] = mine[...]
        table[:, at(g + 1 - c, 128)] = other[...]
    upper = lax.broadcasted_iota(jnp.int32, (256, 128), 1) >= 64
    for i in range(8):
        ch = slice(256 * i, 256 * i + 256)
        got = dot(il[ch, :], table[...])
        hi = in_hi[ch, :]
        acc = jnp.zeros((256, 128), F32)
        for g in range(8):
            acc = jnp.where((hi >> 1) == g, got[:, 128 * g : 128 * g + 128], acc)
        term = halves(acc, (hi & 1) == 1, upper) * basis[ch, :].astype(F32)
        gath[ch, :] = jnp.where(upper == (out_hi[ch, :] == 1), term, 0.0).astype(BF)
    held = dot(olt[...], gath[...]).astype(BF)
    summed[...] = held
    d_sum = jnp.zeros((512, 128), F32)
    for h, w in enumerate((left(w_up[...]), right(w_up[...]))):
        ch = slice(512 * h, 512 * h + 512)
        zed = dot(held, w)
        sig = jax.nn.sigmoid(zed)
        outer[ch, :] = (inner[ch, :].astype(F32) + zed * sig).astype(BF)
        dz = (d_outer[ch, :].astype(F32) * (sig * (1.0 + zed * (1.0 - sig)))).astype(BF)
        dzed[ch, :] = dz
        d_sum += dot_nt(dz, w)
    d_sum = d_sum.astype(BF)
    for i in range(8):
        ch = slice(256 * i, 256 * i + 256)
        got = dot(ol[ch, :], d_sum)
        term = halves(got, out_hi[ch, :] == 1, upper) * basis[ch, :].astype(F32)
        hi = in_hi[ch, :]
        term = jnp.where(upper == ((hi & 1) == 1), term, 0.0).astype(BF)
        owner = (hi >> 1).astype(F32).astype(BF)
        for g in range(8):
            spread[ch, 128 * g : 128 * g + 128] = jnp.where(owner == g, term, jnp.zeros_like(term))
    whole = [dot(ilt[...], spread[:, 512 * i : 512 * i + 512]) for i in range(2)]
    for i in range(4):
        ch = slice(128 * i, 128 * i + 128)
        part = whole[i // 2][:, 256 * (i % 2) : 256 * (i % 2) + 256]
        low, high = part[:, 0:128], part[:, 128:256]
        keep[:, ch] = jnp.where(c == 0, low, high)
        send[:, ch] = jnp.where(c == 0, high, low).astype(BF)


def ko_body(xc, outer, st, summed, dzed, ot, gup, keep, send):
    c = xc[1]
    for i in range(2):
        ch = slice(256 * i, 256 * i + 256)
        part = dot(st[512 + 256 * i : 768 + 256 * i, :], outer[...])
        ot[:, ch] = part.T.astype(BF)
        for j in range(2):
            low, high = part[128 * j : 128 * j + 64, :], part[128 * j + 64 : 128 * j + 128, :]
            rows = slice(128 * i + 64 * j, 128 * i + 64 * j + 64)
            keep[rows, :] = jnp.where(c == 0, low, high)
            send[rows, :] = jnp.where(c == 0, high, low).astype(BF)
    summed_t = summed[...].T
    gup[...] = dot(summed_t[0:64, :], dzed[0:512, :]) + dot(summed_t[64:128, :], dzed[512:1024, :])


def kr_body(xc, keep, recv, own, s1, s2, s3):
    x = xc[0]
    for k, ref in enumerate((own, s1, s2, s3)):
        rows = at(lax.rem(x + k, 4), 64)
        ref[...] = (keep[rows, :] + recv[rows, :].astype(F32)).astype(BF)


def kn_body(own, r1, r2, r3, nodes, w_en, out):
    rows = total4(own[...], r1[...], r2[...], r3[...]).astype(BF)
    out[...] = (nodes[...].astype(F32) + dot(rows, w_en[...])).astype(BF)


def ka_body(xc, keep, recv, own, s1, s2, s3):
    x = xc[0]
    for k, ref in enumerate((own, s1, s2, s3)):
        ch = at(lax.rem(x + k, 4), 128)
        ref[...] = (keep[:, ch] + recv[:, ch].astype(F32)).astype(BF)


def total4(a, b, c, d):
    return (a.astype(F32) + c.astype(F32)) + (b.astype(F32) + d.astype(F32))


def k3_body(
    xc, own, r1, r2, r3, d_outer, dsilu, inner, st, w_down_t, ot, gup, edge_grad, keep, send, d_pre
):
    c = xc[1]
    dd = total4(own[...], r1[...], r2[...], r3[...]).astype(BF)
    for h, w in enumerate((left(w_down_t[...]), right(w_down_t[...]))):
        for i in range(2):
            rows = slice(256 * i, 256 * i + 256)
            ch = slice(512 * h + 256 * i, 512 * h + 256 * i + 256)
            d_inner = d_outer[ch, :].astype(F32) + dot(dd[rows, :], w)
            edge_grad[ch, :] = d_inner.astype(BF)
            d_pre[ch, :] = (d_inner * dsilu[ch, :].astype(F32)).astype(BF)
    for i in range(2):
        rows = slice(256 * i, 256 * i + 256)
        send[rows, :] = dot(st[at(2 * (1 - c) + i, 256), :], d_pre[...]).astype(BF)
        keep[rows, :] = dot(st[at(2 * c + i, 256), :], d_pre[...])
    ddt = dd.T
    gdown = dot(ddt[0:64, :], inner[0:512, :]) + dot(ddt[64:128, :], inner[512:1024, :])
    keep[512:576, :] = jnp.where(c == 0, gup[...], gdown)
    send[512:576, :] = jnp.where(c == 0, gdown, gup[...]).astype(BF)
    for i in range(4):
        rows = slice(576 + 64 * i, 640 + 64 * i)
        keep[rows, :] = ot[at(2 * i + c, 64), :].astype(F32)
        send[rows, :] = ot[at(2 * i + 1 - c, 64), :]


def kb_body(xc, keep, recv, own, s1, s2, s3):
    x = xc[0]
    for k, ref in enumerate((own, s1, s2, s3)):
        b = lax.rem(x + k, 4)
        ch = at(b, 128)
        ref[0:576, :] = (keep[0:576, ch] + recv[0:576, ch].astype(F32)).astype(BF)
        rows = pl.ds(pl.multiple_of(576 + 64 * b, 64), 64)
        part = (keep[rows, :] + recv[rows, :].astype(F32)).astype(BF)
        for j in range(4):
            ref[576 + 64 * j : 640 + 64 * j, :] = part[:, 128 * j : 128 * j + 128]


def k4_body(i, own, r1, r2, r3, nodes_t, all_grad, g0, s1, s2, s3, whole):
    sums = total4(own[...], r1[...], r2[...], r3[...])
    gne = dot(nodes_t[...], sums[0:512, :].astype(BF)).astype(BF)
    ot = sums[576:832, :].astype(BF)
    ot = jnp.concatenate([ot[64 * j : 64 * j + 64, :] for j in range(4)], axis=1)
    gen = dot(ot, all_grad[...]).astype(BF)
    for q in range(4):
        at_q = 400 * q
        whole[at_q : at_q + 256, :] = gne[256 * q : 256 * q + 256, :]
        for j in range(2):
            rows = slice(at_q + 256 + 64 * j, at_q + 320 + 64 * j)
            whole[rows, :] = gen[:, 256 * q + 128 * j : 256 * q + 128 * j + 128]
        whole[at_q + 384 : at_q + 400, :] = sums[512 + 16 * q : 528 + 16 * q, :].astype(BF)
    for k, ref in enumerate((g0, s1, s2, s3)):
        ref[...] = whole[at(lax.rem(i[0] + k, 4), 400), :]


def sum_body(a, b, c, d, out):
    out[...] = total4(a[...], b[...], c[...], d[...]).astype(BF)


def place_body(i, own, r1, r2, r3, out):
    rows = own.shape[0]
    for k, ref in enumerate((own, r1, r2, r3)):
        out[at(lax.rem(i[0] + 4 - k, 4), rows), :] = ref[...]


def end_body(xc, yz, *refs):
    gup, gdt, gne_far, gen_far, gne, gen, sems = refs[8:]
    x, c, z = xc[0], xc[1], yz[1]

    def run(zeros, ones):
        copies = []

        def send(near, far):
            copies.append(fetch(near, far, sems.at[len(copies)]))

        def take(ref, j, rows, lanes, far_row, far_lane, small, small_row):
            value = ref[400 * j : 400 * j + 400, :].astype(F32)
            gne[rows, lanes] = value[0:256]
            for h in range(2):
                gen[far_row, :, far_lane(h)] = value[256 + 64 * h : 320 + 64 * h]
            small[small_row, lanes] = value[384:400]

        for k in range(4):
            q = lax.rem(z + 4 - k, 4)
            for j in range(4):
                take(
                    ones[k], j, at(4 + q, 256), slice(128 * j, 128 * j + 128),
                    2 * j + 1, lambda h: at(2 * q + h, 128), gdt, at(q, 16),
                )
            send(gne.at[at(4 + q, 256), :], gne_far.at[at(4 + q, 256), :])
        for j in range(4):
            send(gen.at[2 * j + 1], gen_far.at[2 * j + 1])
        for j in range(4):
            for k in range(4):
                b = lax.rem(x + 4 - k, 4)
                take(
                    zeros[k], j, slice(256 * j, 256 * j + 256), at(b, 128),
                    2 * b, lambda h: slice(256 * j + 128 * h, 256 * j + 128 * h + 128),
                    gup, slice(16 * j, 16 * j + 16),
                )
            rows = slice(256 * j, 256 * j + 256)
            send(gne.at[rows, :], gne_far.at[rows, :])
        for j in range(4):
            send(gen.at[2 * j], gen_far.at[2 * j])
        for copy in copies:
            copy.wait()

    @pl.when(c == 0)
    def _():
        run(refs[0:4], refs[4:8])

    @pl.when(c == 1)
    def _():
        run(refs[4:8], refs[0:4])


def over_x(value, k):
    perm = [(2 * x + c, 2 * ((x + k) % 4) + c) for x in range(4) for c in range(2)]
    return lax.ppermute(value, "graph", perm)


def over_core(value):
    return lax.ppermute(value, "graph", [(i, i ^ 1) for i in range(8)])


def over_dp(value, k, axes):
    perm = []
    for y in range(4):
        for z in range(4):
            for x in range(4):
                for c in range(2):
                    at = {"x": x, "y": y, "z": z}
                    at[axes[c]] = (at[axes[c]] + k) % 4
                    to = 8 * (4 * at["y"] + at["z"]) + 2 * at["x"] + c
                    perm.append((8 * (4 * y + z) + 2 * x + c, to))
    return lax.ppermute(value, ("dp", "graph"), perm)


def tie(*values):
    return lax.optimization_barrier(values)


def local(
    nodes, node_grad, edges, source, target, trip_in, trip_out, basis, trip_count,
    w_ne, w_down, w_up, w_en,
):
    near = (1, 2, 3)

    n = [nodes[0]] + [over_x(nodes[0], k) for k in near]
    m = [over_core(n[0])]
    p = [node_grad[0]] + [over_x(node_grad[0], k) for k in near]
    s, st, il, ilt, ol, olt, basis2, in_hi, out_hi, w_near, edges_near = call(
        prep_body,
        [sds((1024, 1024)), sds((1024, 1024)), sds((2048, 512)), sds((512, 2048)),
         sds((2048, 512)), sds((512, 2048)), sds((2048, 128)), sds((2048, 128), jnp.int32),
         sds((2048, 128), jnp.int32), sds((2048, 512)), sds((1024, 512))],
        [trip_count, source, target, trip_in, trip_out, basis[0].T, w_ne, edges[0]],
        scalars=1,
        scratch=[pltpu.VMEM((1, 1024), jnp.int32), pltpu.VMEM((1, 1024), jnp.int32),
                 pltpu.VMEM((1, 2048), jnp.int32), pltpu.VMEM((1, 2048), jnp.int32),
                 pltpu.VMEM((64, 2048), BF), pltpu.SemaphoreType.DMA((7,))],
        vmem=12, far_in=7,
    )
    *n, s = tie(*n, s)
    m += [over_core(v) for v in n[1:]]
    down, inner, dsilu, all_nodes = call(
        k1_body,
        [sds((512, 128)), sds((1024, 512)), sds((1024, 512)), sds((512, 1024))],
        [*n, *m, s, edges_near, w_near, w_down.T],
        here="x", scratch=[pltpu.VMEM((1024, 512), BF)], vmem=12,
    )

    t = [down] + [over_x(down, k) for k in near]
    u = [over_core(down)]
    t[1], t[2], t[3], p[1], p[2], p[3] = tie(*t[1:], *p[1:])
    q = [over_core(v) for v in p]
    d_outer, all_grad = call(
        kq_body,
        [sds((1024, 512)), sds((512, 1024))],
        [*p, *q, w_en, s],
        here="x", scratch=[pltpu.VMEM((512, 512), BF)], vmem=12,
    )
    *t, il, d_outer = tie(*t, il, d_outer)
    u += [over_core(v) for v in t[1:]]
    keep, send, outer, summed, dzed = call(
        k2_body,
        [sds((512, 512), F32), sds((512, 512)), sds((1024, 512)), sds((512, 128)),
         sds((1024, 512))],
        [*t, *u, il, ilt, ol, olt, in_hi, out_hi, basis2, inner, d_outer, w_up],
        here="x",
        scratch=[pltpu.VMEM((512, 1024), BF), pltpu.VMEM((2048, 128), BF),
                 pltpu.VMEM((2048, 1024), BF)], vmem=20,
    )

    recv = over_core(send)
    parts = call(ka_body, [sds((512, 128))] * 4, [keep, recv], here="x", vmem=8)
    dd = [parts[0]] + [over_x(parts[k], k) for k in near]
    ot, gup, o_keep, o_send = call(
        ko_body,
        [sds((512, 512)), sds((64, 512), F32), sds((256, 512), F32), sds((256, 512))],
        [outer, st, summed, dzed], here="x", vmem=16,
    )
    o_recv = over_core(o_send)
    edge_grad, keep, send = call(
        k3_body,
        [sds((1024, 512)), sds((832, 512), F32), sds((832, 512))],
        [*dd, d_outer, dsilu, inner, st, w_down.T, ot, gup],
        here="x", scratch=[pltpu.VMEM((1024, 512), BF)], vmem=16,
    )

    recv = over_core(send)
    parts = call(kb_body, [sds((832, 128))] * 4, [keep, recv], here="x", vmem=12)
    recv, o_recv, all_nodes = tie(recv, o_recv, all_nodes)
    o_parts = call(kr_body, [sds((64, 512))] * 4, [o_keep, o_recv], here="x", vmem=8)
    (nodes_t,) = call(kw_body, [sds((1024, 512))], [all_nodes], vmem=8)
    parts = [parts[0]] + [over_x(parts[k], k) for k in near]
    *parts, nodes_t = tie(*parts, nodes_t)
    parts = call(
        k4_body, [sds((400, 128))] * 4, [*parts, nodes_t, all_grad],
        here="part", scratch=[pltpu.VMEM((1600, 128), BF)], vmem=16,
    )
    parts = [parts[0]] + [over_dp(parts[k], k, "yz") for k in near]
    (part,) = call(sum_body, [sds((400, 128))], parts, vmem=8)
    parts = [part] + [over_dp(part, k, "zy") for k in near]
    o_parts = [o_parts[0]] + [over_x(o_parts[k], k) for k in near]
    *o_parts, p0, p1, p2, p3 = tie(*o_parts, *parts)
    (part,) = call(sum_body, [sds((400, 128))], [p0, p1, p2, p3], vmem=8)
    (new_nodes,) = call(kn_body, [sds((64, 1024))], [*o_parts, nodes[0], w_en], vmem=16)
    parts = [part] + [over_dp(part, k, "yx") for k in near]
    new_nodes, *parts = tie(new_nodes, *parts)
    (part,) = call(place_body, [sds((1600, 128))], [*parts], here="place", vmem=8)
    parts = [part] + [over_dp(part, k, "xz") for k in near]
    grad_up, grad_down_t, grad_ne, grad_en = call(
        end_body,
        [sds((64, 512), F32), sds((64, 512), F32), sds((2048, 512), F32), sds((8, 64, 1024), F32)],
        [*parts, *[over_core(v) for v in parts]],
        here="xy",
        scratch=[pltpu.VMEM((2048, 512), F32), pltpu.VMEM((8, 64, 1024), F32),
                 pltpu.SemaphoreType.DMA((16,))],
        vmem=16, far_out=2,
    )
    grad_en = grad_en.reshape(512, 1024)
    return (new_nodes[None], edge_grad[None], grad_ne, grad_down_t.T, grad_up, grad_en)


def solution(mesh):
    split3, split2 = P("dp", "graph", None), P("dp", "graph")
    in_specs = (split3,) * 3 + (split2,) * 4 + (split3, split2) + (P(),) * 4
    out_specs = (split3, split3, P(), P(), P(), P())
    return jax.shard_map(local, mesh=mesh, in_specs=in_specs, out_specs=out_specs, check_vma=False)
```

```python
import jax
import jax.numpy as jnp
from jax import lax
from jax.experimental import pallas as pl
from jax.experimental.pallas import tpu as pltpu
from jax.sharding import PartitionSpec as P

BF = jnp.bfloat16
F32 = jnp.float32
NT = (((1,), (1,)), ((), ()))


def dot(a, b):
    return jnp.dot(a, b, preferred_element_type=F32)


def dot_nt(a, b):
    return lax.dot_general(a, b, NT, preferred_element_type=F32)


def call(
    body, outs, args, here="", scalars=0, scratch=(), vmem=40, any_in=0, far_in=0, far_out=0
):
    n_in, n_out = len(args), len(outs)

    def placed(*refs):
        g, d = lax.axis_index("graph"), lax.axis_index("dp")
        x, c, y, z = g >> 1, g & 1, d >> 2, d & 3
        names = {
            "": (), "x": ((x, c),), "xy": ((x, c), (y, z)),
            "part": ((jnp.where(c == 0, y, z),),), "place": ((jnp.where(c == 0, y, x),),),
        }
        body(*names[here], *refs)

    in_specs = [pl.BlockSpec(memory_space=pltpu.SMEM)] * scalars
    in_specs += [pl.BlockSpec(memory_space=pltpu.VMEM)] * (n_in - scalars - any_in - far_in)
    in_specs += [pl.BlockSpec(memory_space=pl.ANY)] * any_in
    in_specs += [pl.BlockSpec(memory_space=pltpu.HBM)] * far_in
    out_specs = [pl.BlockSpec(memory_space=pltpu.VMEM)] * (n_out - far_out)
    out_specs += [pl.BlockSpec(memory_space=pltpu.HBM)] * far_out
    near, far = args[: n_in - far_in], args[n_in - far_in :]
    return pl.pallas_call(
        placed if here else body,
        out_shape=[
            pltpu.HBM(o.shape, o.dtype) if i >= n_out - far_out else o for i, o in enumerate(outs)
        ],
        in_specs=in_specs,
        out_specs=out_specs,
        scratch_shapes=list(scratch),
        compiler_params=pltpu.CompilerParams(vmem_limit_bytes=vmem << 20),
        cost_estimate=pl.CostEstimate(flops=1, bytes_accessed=1, transcendentals=0),
    )(*near, *(pltpu.with_memory_space_constraint(a, pltpu.HBM) for a in far))


def sds(shape, dtype=BF):
    return jax.ShapeDtypeStruct(shape, dtype)


def at(i, size):
    return pl.ds(pl.multiple_of(i * size, size), size)


def hot(mask):
    return jnp.where(mask, 1.0, 0.0).astype(BF)


def left(w):
    return jnp.concatenate([w, jnp.zeros_like(w)], axis=0)


def right(w):
    return jnp.concatenate([jnp.zeros_like(w), w], axis=0)


def column(row):
    return jnp.broadcast_to(row.astype(F32), (128, row.shape[1])).T.astype(jnp.int32)


def hot_rows(col, width):
    lane = lax.broadcasted_iota(jnp.int32, col.shape, 1)
    return jnp.concatenate([hot(col == lane + j) for j in range(0, width, 128)], axis=1)


def prep_body(cnt, *refs):
    s, st, il, ilt, ol, olt, basis, in_hi, out_hi, w_ne, edges = refs[7:18]
    src_r, tgt_r, in_r, out_r, basis_t, sems = refs[18:]
    nears = (src_r, tgt_r, in_r, out_r, basis_t, w_ne, edges)
    loads = [fetch(refs[i], near, sems.at[i]) for i, near in enumerate(nears)]
    for copy in loads[:4]:
        copy.wait()
    for i in range(4):
        ch = slice(256 * i, 256 * i + 256)
        s[ch, 0:512] = hot_rows(column(src_r[:, ch]), 512)
        s[ch, 512:1024] = hot_rows(column(tgt_r[:, ch]), 512)
    row = lax.broadcasted_iota(jnp.int32, (128, 1024), 0)
    for i in range(4):
        ch = slice(128 * i, 128 * i + 128)
        st[ch, :] = hot(src_r[...] == row + 128 * i)
        st[512 + 128 * i : 640 + 128 * i, :] = hot(tgt_r[...] == row + 128 * i)
    pos = lax.broadcasted_iota(jnp.int32, (1, 2048), 1)
    live = pos < cnt[0, 0]
    in_lo = jnp.where(live, in_r[...] & 1023, -1)
    out_lo = out_r[...] & 511
    for i in range(8):
        ch = slice(256 * i, 256 * i + 256)
        il[ch, :] = hot_rows(column(in_lo[:, ch]), 1024)
        ol[ch, :] = hot_rows(column(out_lo[:, ch]), 512)
        in_hi[ch, :] = column(in_r[:, ch] >> 9)
        out_hi[ch, :] = column(out_r[:, ch] >> 9)
    row = lax.broadcasted_iota(jnp.int32, (64, 2048), 0)
    for i in range(8):
        ch = slice(64 * i, 64 * i + 64)
        ilt[ch, :] = hot(in_lo == row + 64 * i)
        ilt[512 + 64 * i : 576 + 64 * i, :] = hot(in_lo == row + 512 + 64 * i)
        olt[ch, :] = hot(out_lo == row + 64 * i)
    for copy in loads[4:]:
        copy.wait()
    basis[...] = jnp.concatenate([basis_t[...], basis_t[...]], axis=0).T


def fetch(far, near, sem):
    copy = pltpu.make_async_copy(far, near, sem)
    copy.start()
    return copy


def gathered(xc, refs, out):
    x, c = xc
    for k in range(4):
        g = 2 * lax.rem(x + 4 - k, 4)
        out[at(g + c, 64), :] = refs[k][...]
        out[at(g + 1 - c, 64), :] = refs[4 + k][...]


def k1_body(xc, *refs):
    s, edges, w_ne, w_down_t, down, inner, dsilu, nodes, ab = refs[8:]
    gathered(xc, refs[:8], nodes)
    for h in range(2):
        for i in range(2):
            rows = slice(512 * h + 256 * i, 512 * h + 256 * i + 256)
            ab[rows, :] = dot(
                nodes[256 * i : 256 * i + 256, :], w_ne[1024 * h : 1024 * h + 1024, :]
            ).astype(BF)
    wd = swapped(xc[1], left(w_down_t[...]), right(w_down_t[...]))
    for i in range(2):
        total = None
        for h in range(2):
            ch = slice(512 * h + 256 * i, 512 * h + 256 * i + 256)
            pre = dot(s[ch, :], ab[...])
            sig = jax.nn.sigmoid(pre)
            held = (edges[ch, :].astype(F32) + pre * sig).astype(BF)
            inner[ch, :] = held
            dsilu[ch, :] = (sig * (1.0 + pre * (1.0 - sig))).astype(BF)
            part = dot_nt(held, wd[h])
            total = part if total is None else total + part
        down[256 * i : 256 * i + 256, :] = total.astype(BF)


def kw_body(nodes, nodes_t):
    nodes_t[...] = nodes[...].T


def swapped(c, first, second):
    a, b = first.astype(F32), second.astype(F32)
    return jnp.where(c == 0, a, b).astype(BF), jnp.where(c == 0, b, a).astype(BF)


def lane_key(c):
    lane = lax.broadcasted_iota(jnp.int32, (512, 128), 1)
    return jnp.where(c == 0, lane, 127 - lane)


def halves(value, odd, upper):
    kept = jnp.where(upper == odd, value, 0.0)
    return kept + pltpu.roll(kept, 64, 1)


def k2_body(xc, *refs):
    pieces, grads = refs[0:8], refs[8:16]
    il, ilt, ol, olt, in_hi, out_hi, basis, inner, w_up, w_en, s = refs[16:27]
    keep, send, outer, summed, dzed, d_outer, all_grad, table, gath, spread, q = refs[27:]
    x, c = xc
    gathered(xc, grads, all_grad)
    for i in range(2):
        ch = slice(256 * i, 256 * i + 256)
        q[ch, :] = dot_nt(all_grad[ch, :], w_en[...]).astype(BF)
    key = lane_key(c)
    is_mine = key.astype(F32).astype(BF) < 64
    for k in range(4):
        cols = at(lax.rem(x + 4 - k, 4), 128)
        mine, other = pieces[k][...], pieces[4 + k][...]
        table[0:512, cols] = jnp.where(is_mine, mine, other)
        table[512:1024, cols] = jnp.where(is_mine, other, mine)
    upper = lax.broadcasted_iota(jnp.int32, (256, 128), 1) >= 64
    for i in range(8):
        ch = slice(256 * i, 256 * i + 256)
        got = dot(il[ch, :], table[...])
        hi = in_hi[ch, :]
        acc = jnp.zeros((256, 128), F32)
        for b in range(4):
            acc = jnp.where((hi >> 2) == b, got[:, 128 * b : 128 * b + 128], acc)
        term = halves(acc, ((hi ^ (hi >> 1)) & 1) == 1, upper) * basis[ch, :].astype(F32)
        gath[ch, :] = jnp.where(upper == (out_hi[ch, :] == 1), term, 0.0).astype(BF)
    held = dot(olt[...], gath[...]).astype(BF)
    summed[...] = held
    d_sum = jnp.zeros((512, 128), F32)
    for h, w in enumerate((left(w_up[...]), right(w_up[...]))):
        ch = slice(512 * h, 512 * h + 512)
        zed = dot(held, w)
        sig = jax.nn.sigmoid(zed)
        outer[ch, :] = (inner[ch, :].astype(F32) + zed * sig).astype(BF)
        back = dot(s[ch, 512:1024], q[...])
        d_outer[ch, :] = back.astype(BF)
        dz = (back * (sig * (1.0 + zed * (1.0 - sig)))).astype(BF)
        dzed[ch, :] = dz
        d_sum += dot_nt(dz, w)
    d_sum = d_sum.astype(BF)
    for i in range(8):
        ch = slice(256 * i, 256 * i + 256)
        got = dot(ol[ch, :], d_sum)
        term = halves(got, out_hi[ch, :] == 1, upper) * basis[ch, :].astype(F32)
        hi = in_hi[ch, :]
        term = jnp.where(upper == (((hi ^ (hi >> 1)) & 1) == 1), term, 0.0).astype(BF)
        owner = (hi >> 2).astype(F32).astype(BF)
        for b in range(4):
            spread[ch, 128 * b : 128 * b + 128] = jnp.where(owner == b, term, jnp.zeros_like(term))
    part = dot(ilt[...], spread[...])
    for b in range(4):
        ch = slice(128 * b, 128 * b + 128)
        low, high = part[0:512, ch], part[512:1024, ch]
        keep[:, ch] = jnp.where(key < 64, low, high)
        send[:, ch] = jnp.where(key < 64, high, low).astype(BF)


def ko_body(xc, outer, st, summed, dzed, ot, gup, keep, send):
    c = xc[1]
    for i in range(2):
        ch = slice(256 * i, 256 * i + 256)
        part = dot(st[512 + 256 * i : 768 + 256 * i, :], outer[...])
        ot[:, ch] = part.T.astype(BF)
        for j in range(2):
            low, high = part[128 * j : 128 * j + 64, :], part[128 * j + 64 : 128 * j + 128, :]
            rows = slice(128 * i + 64 * j, 128 * i + 64 * j + 64)
            keep[rows, :] = jnp.where(c == 0, low, high)
            send[rows, :] = jnp.where(c == 0, high, low).astype(BF)
    summed_t = summed[...].T
    gup[...] = dot(summed_t[0:64, :], dzed[0:512, :]) + dot(summed_t[64:128, :], dzed[512:1024, :])


def kr_body(xc, keep, recv, own, s1, s2, s3):
    x = xc[0]
    for k, ref in enumerate((own, s1, s2, s3)):
        rows = at(lax.rem(x + k, 4), 64)
        ref[...] = (keep[rows, :] + recv[rows, :].astype(F32)).astype(BF)


def kn_body(own, r1, r2, r3, nodes, w_en, out):
    rows = total4(own[...], r1[...], r2[...], r3[...]).astype(BF)
    out[...] = (nodes[...].astype(F32) + dot(rows, w_en[...])).astype(BF)


def ka_body(xc, keep, recv, own, s1, s2, s3):
    x = xc[0]
    for k, ref in enumerate((own, s1, s2, s3)):
        ch = at(lax.rem(x + k, 4), 128)
        ref[...] = (keep[:, ch] + recv[:, ch].astype(F32)).astype(BF)


def total4(a, b, c, d):
    return (a.astype(F32) + c.astype(F32)) + (b.astype(F32) + d.astype(F32))


def k3_body(
    xc, own, r1, r2, r3, d_outer, dsilu, inner, st, w_down_t, ot, gup, edge_grad, keep, send, d_pre
):
    c = xc[1]
    dd = total4(own[...], r1[...], r2[...], r3[...]).astype(BF)
    for h, w in enumerate(swapped(c, left(w_down_t[...]), right(w_down_t[...]))):
        for i in range(2):
            rows = slice(256 * i, 256 * i + 256)
            ch = slice(512 * h + 256 * i, 512 * h + 256 * i + 256)
            d_inner = d_outer[ch, :].astype(F32) + dot(dd[rows, :], w)
            edge_grad[ch, :] = d_inner.astype(BF)
            d_pre[ch, :] = (d_inner * dsilu[ch, :].astype(F32)).astype(BF)
    for i in range(2):
        rows = slice(256 * i, 256 * i + 256)
        send[rows, :] = dot(st[at(2 * (1 - c) + i, 256), :], d_pre[...]).astype(BF)
        keep[rows, :] = dot(st[at(2 * c + i, 256), :], d_pre[...])
    ddt = dd.T
    first, second = swapped(c, ddt[0:64, :], ddt[64:128, :])
    gdown = dot(first, inner[0:512, :]) + dot(second, inner[512:1024, :])
    keep[512:576, :] = jnp.where(c == 0, gup[...], gdown)
    send[512:576, :] = jnp.where(c == 0, gdown, gup[...]).astype(BF)
    for i in range(4):
        rows = slice(576 + 64 * i, 640 + 64 * i)
        keep[rows, :] = ot[at(2 * i + c, 64), :].astype(F32)
        send[rows, :] = ot[at(2 * i + 1 - c, 64), :]


def kb_body(xc, keep, recv, own, s1, s2, s3):
    x = xc[0]
    for k, ref in enumerate((own, s1, s2, s3)):
        b = lax.rem(x + k, 4)
        ch = at(b, 128)
        ref[0:576, :] = (keep[0:576, ch] + recv[0:576, ch].astype(F32)).astype(BF)
        rows = pl.ds(pl.multiple_of(576 + 64 * b, 64), 64)
        part = (keep[rows, :] + recv[rows, :].astype(F32)).astype(BF)
        for j in range(4):
            ref[576 + 64 * j : 640 + 64 * j, :] = part[:, 128 * j : 128 * j + 128]


def k4_body(i, own, r1, r2, r3, nodes_t, all_grad, g0, s1, s2, s3, whole):
    sums = total4(own[...], r1[...], r2[...], r3[...])
    gne = dot(nodes_t[...], sums[0:512, :].astype(BF)).astype(BF)
    ot = sums[576:832, :].astype(BF)
    ot = jnp.concatenate([ot[64 * j : 64 * j + 64, :] for j in range(4)], axis=1)
    gen = dot(ot, all_grad[...]).astype(BF)
    for q in range(4):
        at_q = 400 * q
        whole[at_q : at_q + 256, :] = gne[256 * q : 256 * q + 256, :]
        for j in range(2):
            rows = slice(at_q + 256 + 64 * j, at_q + 320 + 64 * j)
            whole[rows, :] = gen[:, 256 * q + 128 * j : 256 * q + 128 * j + 128]
        whole[at_q + 384 : at_q + 400, :] = sums[512 + 16 * q : 528 + 16 * q, :].astype(BF)
    for k, ref in enumerate((g0, s1, s2, s3)):
        ref[...] = whole[at(lax.rem(i[0] + k, 4), 400), :]


def sum_body(a, b, c, d, out):
    out[...] = total4(a[...], b[...], c[...], d[...]).astype(BF)


def place_body(i, own, r1, r2, r3, out):
    rows = own.shape[0]
    for k, ref in enumerate((own, r1, r2, r3)):
        out[at(lax.rem(i[0] + 4 - k, 4), rows), :] = ref[...]


def end_body(xc, yz, *refs):
    gup, gdt, gne_far, gen_far, gne, gen, sems = refs[8:]
    x, c, z = xc[0], xc[1], yz[1]

    def run(zeros, ones):
        copies = []

        def send(near, far):
            copies.append(fetch(near, far, sems.at[len(copies)]))

        def take(ref, j, rows, lanes, far_row, far_lane, small, small_row):
            value = ref[400 * j : 400 * j + 400, :].astype(F32)
            gne[rows, lanes] = value[0:256]
            for h in range(2):
                gen[far_row, :, far_lane(h)] = value[256 + 64 * h : 320 + 64 * h]
            small[small_row, lanes] = value[384:400]

        for k in range(4):
            q = lax.rem(z + 4 - k, 4)
            for j in range(4):
                take(
                    ones[k], j, at(4 + q, 256), slice(128 * j, 128 * j + 128),
                    2 * j + 1, lambda h: at(2 * q + h, 128), gdt, at(q, 16),
                )
            send(gne.at[at(4 + q, 256), :], gne_far.at[at(4 + q, 256), :])
        for j in range(4):
            send(gen.at[2 * j + 1], gen_far.at[2 * j + 1])
        for j in range(4):
            for k in range(4):
                b = lax.rem(x + 4 - k, 4)
                take(
                    zeros[k], j, slice(256 * j, 256 * j + 256), at(b, 128),
                    2 * b, lambda h: slice(256 * j + 128 * h, 256 * j + 128 * h + 128),
                    gup, slice(16 * j, 16 * j + 16),
                )
            rows = slice(256 * j, 256 * j + 256)
            send(gne.at[rows, :], gne_far.at[rows, :])
        for j in range(4):
            send(gen.at[2 * j], gen_far.at[2 * j])
        for copy in copies:
            copy.wait()

    @pl.when(c == 0)
    def _():
        run(refs[0:4], refs[4:8])

    @pl.when(c == 1)
    def _():
        run(refs[4:8], refs[0:4])


def over_x(value, k):
    perm = [(2 * x + c, 2 * ((x + k) % 4) + c) for x in range(4) for c in range(2)]
    return lax.ppermute(value, "graph", perm)


def over_core(value):
    return lax.ppermute(value, "graph", [(i, i ^ 1) for i in range(8)])


def over_dp(value, k, axes):
    perm = []
    for y in range(4):
        for z in range(4):
            for x in range(4):
                for c in range(2):
                    at = {"x": x, "y": y, "z": z}
                    at[axes[c]] = (at[axes[c]] + k) % 4
                    to = 8 * (4 * at["y"] + at["z"]) + 2 * at["x"] + c
                    perm.append((8 * (4 * y + z) + 2 * x + c, to))
    return lax.ppermute(value, ("dp", "graph"), perm)


def tie(*values):
    return lax.optimization_barrier(values)


def local(
    nodes, node_grad, edges, source, target, trip_in, trip_out, basis, trip_count,
    w_ne, w_down, w_up, w_en,
):
    near = (1, 2, 3)

    n = [nodes[0]] + [over_x(nodes[0], k) for k in near]
    m = [over_core(n[0])]
    p = [node_grad[0]] + [over_x(node_grad[0], k) for k in near]
    s, st, il, ilt, ol, olt, basis2, in_hi, out_hi, w_near, edges_near = call(
        prep_body,
        [sds((1024, 1024)), sds((1024, 1024)), sds((2048, 1024)), sds((1024, 2048)),
         sds((2048, 512)), sds((512, 2048)), sds((2048, 128)), sds((2048, 128), jnp.int32),
         sds((2048, 128), jnp.int32), sds((2048, 512)), sds((1024, 512))],
        [trip_count, source, target, trip_in, trip_out, basis[0].T, w_ne, edges[0]],
        scalars=1,
        scratch=[pltpu.VMEM((1, 1024), jnp.int32), pltpu.VMEM((1, 1024), jnp.int32),
                 pltpu.VMEM((1, 2048), jnp.int32), pltpu.VMEM((1, 2048), jnp.int32),
                 pltpu.VMEM((64, 2048), BF), pltpu.SemaphoreType.DMA((7,))],
        vmem=12, far_in=7,
    )
    *n, s = tie(*n, s)
    m += [over_core(v) for v in n[1:]]
    down, inner, dsilu, all_nodes = call(
        k1_body,
        [sds((512, 128)), sds((1024, 512)), sds((1024, 512)), sds((512, 1024))],
        [*n, *m, s, edges_near, w_near, w_down.T],
        here="x", scratch=[pltpu.VMEM((1024, 512), BF)], vmem=12,
    )

    t = [down] + [over_x(down, k) for k in near]
    u = [over_core(down)]
    t[1], t[2], t[3], p[1], p[2], p[3] = tie(*t[1:], *p[1:])
    q = [over_core(v) for v in p]
    u += [over_core(v) for v in t[1:]]
    keep, send, outer, summed, dzed, d_outer, all_grad = call(
        k2_body,
        [sds((512, 512), F32), sds((512, 512)), sds((1024, 512)), sds((512, 128)),
         sds((1024, 512)), sds((1024, 512)), sds((512, 1024))],
        [*t, *u, *p, *q, il, ilt, ol, olt, in_hi, out_hi, basis2, inner, w_up, w_en, s],
        here="x",
        scratch=[pltpu.VMEM((1024, 512), BF), pltpu.VMEM((2048, 128), BF),
                 pltpu.VMEM((2048, 512), BF), pltpu.VMEM((512, 512), BF)],
        vmem=20,
    )

    recv = over_core(send)
    parts = call(ka_body, [sds((512, 128))] * 4, [keep, recv], here="x", vmem=8)
    dd = [parts[0]] + [over_x(parts[k], k) for k in near]
    ot, gup, o_keep, o_send = call(
        ko_body,
        [sds((512, 512)), sds((64, 512), F32), sds((256, 512), F32), sds((256, 512))],
        [outer, st, summed, dzed], here="x", vmem=16,
    )
    o_recv = over_core(o_send)
    edge_grad, keep, send = call(
        k3_body,
        [sds((1024, 512)), sds((832, 512), F32), sds((832, 512))],
        [*dd, d_outer, dsilu, inner, st, w_down.T, ot, gup],
        here="x", scratch=[pltpu.VMEM((1024, 512), BF)], vmem=16,
    )

    recv = over_core(send)
    parts = call(kb_body, [sds((832, 128))] * 4, [keep, recv], here="x", vmem=12)
    recv, o_recv, all_nodes = tie(recv, o_recv, all_nodes)
    o_parts = call(kr_body, [sds((64, 512))] * 4, [o_keep, o_recv], here="x", vmem=8)
    (nodes_t,) = call(kw_body, [sds((1024, 512))], [all_nodes], vmem=8)
    parts = [parts[0]] + [over_x(parts[k], k) for k in near]
    *parts, nodes_t = tie(*parts, nodes_t)
    parts = call(
        k4_body, [sds((400, 128))] * 4, [*parts, nodes_t, all_grad],
        here="part", scratch=[pltpu.VMEM((1600, 128), BF)], vmem=16,
    )
    parts = [parts[0]] + [over_dp(parts[k], k, "yz") for k in near]
    (part,) = call(sum_body, [sds((400, 128))], parts, vmem=8)
    parts = [part] + [over_dp(part, k, "zy") for k in near]
    o_parts = [o_parts[0]] + [over_x(o_parts[k], k) for k in near]
    *o_parts, p0, p1, p2, p3 = tie(*o_parts, *parts)
    (part,) = call(sum_body, [sds((400, 128))], [p0, p1, p2, p3], vmem=8)
    (new_nodes,) = call(kn_body, [sds((64, 1024))], [*o_parts, nodes[0], w_en], vmem=16)
    parts = [part] + [over_dp(part, k, "yx") for k in near]
    new_nodes, *parts = tie(new_nodes, *parts)
    (part,) = call(place_body, [sds((1600, 128))], [*parts], here="place", vmem=8)
    parts = [part] + [over_dp(part, k, "xz") for k in near]
    grad_up, grad_down_t, grad_ne, grad_en = call(
        end_body,
        [sds((64, 512), F32), sds((64, 512), F32), sds((2048, 512), F32), sds((8, 64, 1024), F32)],
        [*parts, *[over_core(v) for v in parts]],
        here="xy",
        scratch=[pltpu.VMEM((2048, 512), F32), pltpu.VMEM((8, 64, 1024), F32),
                 pltpu.SemaphoreType.DMA((16,))],
        vmem=16, far_out=2,
    )
    grad_en = grad_en.reshape(512, 1024)
    return (new_nodes[None], edge_grad[None], grad_ne, grad_down_t.T, grad_up, grad_en)


def solution(mesh):
    split3, split2 = P("dp", "graph", None), P("dp", "graph")
    in_specs = (split3,) * 3 + (split2,) * 4 + (split3, split2) + (P(),) * 4
    out_specs = (split3, split3, P(), P(), P(), P())
    return jax.shard_map(local, mesh=mesh, in_specs=in_specs, out_specs=out_specs, check_vma=False)
```

```python
import jax
import jax.numpy as jnp
from jax import lax
from jax.experimental import pallas as pl
from jax.experimental.pallas import tpu as pltpu
from jax.sharding import PartitionSpec as P

BF = jnp.bfloat16
F32 = jnp.float32
NT = (((1,), (1,)), ((), ()))


def dot(a, b):
    return jnp.dot(a, b, preferred_element_type=F32)


def dot_nt(a, b):
    return lax.dot_general(a, b, NT, preferred_element_type=F32)


def call(
    body, outs, args, here="", scalars=0, scratch=(), vmem=40, any_in=0, far_in=0, far_out=0
):
    n_in, n_out = len(args), len(outs)

    def placed(*refs):
        g, d = lax.axis_index("graph"), lax.axis_index("dp")
        x, c, y, z = g >> 1, g & 1, d >> 2, d & 3
        names = {
            "": (), "x": ((x, c),), "xy": ((x, c), (y, z)),
            "part": ((jnp.where(c == 0, y, z),),), "place": ((jnp.where(c == 0, y, x),),),
        }
        body(*names[here], *refs)

    in_specs = [pl.BlockSpec(memory_space=pltpu.SMEM)] * scalars
    in_specs += [pl.BlockSpec(memory_space=pltpu.VMEM)] * (n_in - scalars - any_in - far_in)
    in_specs += [pl.BlockSpec(memory_space=pl.ANY)] * any_in
    in_specs += [pl.BlockSpec(memory_space=pltpu.HBM)] * far_in
    out_specs = [pl.BlockSpec(memory_space=pltpu.VMEM)] * (n_out - far_out)
    out_specs += [pl.BlockSpec(memory_space=pltpu.HBM)] * far_out
    near, far = args[: n_in - far_in], args[n_in - far_in :]
    return pl.pallas_call(
        placed if here else body,
        out_shape=[
            pltpu.HBM(o.shape, o.dtype) if i >= n_out - far_out else o for i, o in enumerate(outs)
        ],
        in_specs=in_specs,
        out_specs=out_specs,
        scratch_shapes=list(scratch),
        compiler_params=pltpu.CompilerParams(vmem_limit_bytes=vmem << 20),
        cost_estimate=pl.CostEstimate(flops=1, bytes_accessed=1, transcendentals=0),
    )(*near, *(pltpu.with_memory_space_constraint(a, pltpu.HBM) for a in far))


def sds(shape, dtype=BF):
    return jax.ShapeDtypeStruct(shape, dtype)


def at(i, size):
    return pl.ds(pl.multiple_of(i * size, size), size)


def hot(mask):
    return jnp.where(mask, 1.0, 0.0).astype(BF)


def left(w):
    return jnp.concatenate([w, jnp.zeros_like(w)], axis=0)


def right(w):
    return jnp.concatenate([jnp.zeros_like(w), w], axis=0)


def column(row):
    return jnp.broadcast_to(row.astype(F32), (128, row.shape[1])).T.astype(jnp.int32)


def hot_rows(col, width):
    lane = lax.broadcasted_iota(jnp.int32, col.shape, 1)
    return jnp.concatenate([hot(col == lane + j) for j in range(0, width, 128)], axis=1)


def prep_body(cnt, *refs):
    s, st, il, ilt, ol, olt, basis, in_hi, out_hi, w_ne, edges = refs[7:18]
    src_r, tgt_r, in_r, out_r, basis_t, sems = refs[18:]
    nears = (src_r, tgt_r, in_r, out_r, basis_t, w_ne, edges)
    loads = [fetch(refs[i], near, sems.at[i]) for i, near in enumerate(nears)]
    for copy in loads[:4]:
        copy.wait()
    for i in range(4):
        ch = slice(256 * i, 256 * i + 256)
        s[ch, 0:512] = hot_rows(column(src_r[:, ch]), 512)
        s[ch, 512:1024] = hot_rows(column(tgt_r[:, ch]), 512)
    row = lax.broadcasted_iota(jnp.int32, (128, 1024), 0)
    for i in range(4):
        ch = slice(128 * i, 128 * i + 128)
        st[ch, :] = hot(src_r[...] == row + 128 * i)
        st[512 + 128 * i : 640 + 128 * i, :] = hot(tgt_r[...] == row + 128 * i)
    pos = lax.broadcasted_iota(jnp.int32, (1, 2048), 1)
    live = pos < cnt[0, 0]
    in_lo = jnp.where(live, in_r[...] & 1023, -1)
    out_lo = out_r[...] & 511
    for i in range(8):
        ch = slice(256 * i, 256 * i + 256)
        il[ch, :] = hot_rows(column(in_lo[:, ch]), 1024)
        ol[ch, :] = hot_rows(column(out_lo[:, ch]), 512)
        in_hi[ch, :] = column(in_r[:, ch] >> 9)
        out_hi[ch, :] = column(out_r[:, ch] >> 9)
    row = lax.broadcasted_iota(jnp.int32, (64, 2048), 0)
    for i in range(8):
        ch = slice(64 * i, 64 * i + 64)
        ilt[ch, :] = hot(in_lo == row + 64 * i)
        ilt[512 + 64 * i : 576 + 64 * i, :] = hot(in_lo == row + 512 + 64 * i)
        olt[ch, :] = hot(out_lo == row + 64 * i)
    for copy in loads[4:]:
        copy.wait()
    basis[...] = jnp.concatenate([basis_t[...], basis_t[...]], axis=0).T


def fetch(far, near, sem):
    copy = pltpu.make_async_copy(far, near, sem)
    copy.start()
    return copy


def gathered(xc, refs, out):
    x, c = xc
    for k in range(4):
        g = 2 * lax.rem(x + 4 - k, 4)
        out[at(g + c, 64), :] = refs[k][...]
        out[at(g + 1 - c, 64), :] = refs[4 + k][...]


def k1_body(xc, *refs):
    s, edges, w_ne, w_down_t, down, inner, dsilu, nodes, ab = refs[8:]
    gathered(xc, refs[:8], nodes)
    for h in range(2):
        for i in range(2):
            rows = slice(512 * h + 256 * i, 512 * h + 256 * i + 256)
            ab[rows, :] = dot(
                nodes[256 * i : 256 * i + 256, :], w_ne[1024 * h : 1024 * h + 1024, :]
            ).astype(BF)
    wd = swapped(xc[1], left(w_down_t[...]), right(w_down_t[...]))
    for i in range(2):
        total = None
        for h in range(2):
            ch = slice(512 * h + 256 * i, 512 * h + 256 * i + 256)
            pre = dot(s[ch, :], ab[...])
            sig = jax.nn.sigmoid(pre)
            held = (edges[ch, :].astype(F32) + pre * sig).astype(BF)
            inner[ch, :] = held
            dsilu[ch, :] = (sig * (1.0 + pre * (1.0 - sig))).astype(BF)
            part = dot_nt(held, wd[h])
            total = part if total is None else total + part
        down[256 * i : 256 * i + 256, :] = total.astype(BF)


def kw_body(nodes, nodes_t):
    nodes_t[...] = nodes[...].T


def swapped(c, first, second):
    a, b = first.astype(F32), second.astype(F32)
    return jnp.where(c == 0, a, b).astype(BF), jnp.where(c == 0, b, a).astype(BF)


def lane_key(c):
    lane = lax.broadcasted_iota(jnp.int32, (512, 128), 1)
    return jnp.where(c == 0, lane, 127 - lane)


def halves(value, odd, upper):
    kept = jnp.where(upper == odd, value, 0.0)
    return kept + pltpu.roll(kept, 64, 1)


def k2_body(xc, *refs):
    pieces, grads = refs[0:8], refs[8:16]
    il, ilt, ol, olt, in_hi, out_hi, basis, inner, w_up, w_en, s = refs[16:27]
    keep, send, outer, summed, dzed, d_outer, all_grad, table, gath, spread, q = refs[27:]
    x, c = xc
    gathered(xc, grads, all_grad)
    for i in range(2):
        ch = slice(256 * i, 256 * i + 256)
        q[ch, :] = dot_nt(all_grad[ch, :], w_en[...]).astype(BF)
    key = lane_key(c)
    is_mine = key.astype(F32).astype(BF) < 64
    for k in range(4):
        cols = at(lax.rem(x + 4 - k, 4), 128)
        mine, other = pieces[k][...], pieces[4 + k][...]
        table[0:512, cols] = jnp.where(is_mine, mine, other)
        table[512:1024, cols] = jnp.where(is_mine, other, mine)
    upper = lax.broadcasted_iota(jnp.int32, (256, 128), 1) >= 64
    for i in range(8):
        ch = slice(256 * i, 256 * i + 256)
        got = dot(il[ch, :], table[...])
        hi = in_hi[ch, :]
        acc = jnp.zeros((256, 128), F32)
        for b in range(4):
            acc = jnp.where((hi >> 2) == b, got[:, 128 * b : 128 * b + 128], acc)
        term = halves(acc, ((hi ^ (hi >> 1)) & 1) == 1, upper) * basis[ch, :].astype(F32)
        gath[ch, :] = jnp.where(upper == (out_hi[ch, :] == 1), term, 0.0).astype(BF)
    held = dot(olt[...], gath[...]).astype(BF)
    summed[...] = held
    d_sum = jnp.zeros((512, 128), F32)
    for h, w in enumerate((left(w_up[...]), right(w_up[...]))):
        ch = slice(512 * h, 512 * h + 512)
        zed = dot(held, w)
        sig = jax.nn.sigmoid(zed)
        outer[ch, :] = (inner[ch, :].astype(F32) + zed * sig).astype(BF)
        back = dot(s[ch, 512:1024], q[...])
        d_outer[ch, :] = back.astype(BF)
        dz = (back * (sig * (1.0 + zed * (1.0 - sig)))).astype(BF)
        dzed[ch, :] = dz
        d_sum += dot_nt(dz, w)
    d_sum = d_sum.astype(BF)
    for i in range(8):
        ch = slice(256 * i, 256 * i + 256)
        got = dot(ol[ch, :], d_sum)
        term = halves(got, out_hi[ch, :] == 1, upper) * basis[ch, :].astype(F32)
        hi = in_hi[ch, :]
        term = jnp.where(upper == (((hi ^ (hi >> 1)) & 1) == 1), term, 0.0).astype(BF)
        owner = (hi >> 2).astype(F32).astype(BF)
        for b in range(4):
            spread[ch, 128 * b : 128 * b + 128] = jnp.where(owner == b, term, jnp.zeros_like(term))
    part = dot(ilt[...], spread[...])
    for b in range(4):
        ch = slice(128 * b, 128 * b + 128)
        low, high = part[0:512, ch], part[512:1024, ch]
        keep[:, ch] = jnp.where(key < 64, low, high)
        send[:, ch] = jnp.where(key < 64, high, low).astype(BF)


def ko_body(xc, outer, st, summed, dzed, ot, gup, keep, send):
    c = xc[1]
    for i in range(2):
        ch = slice(256 * i, 256 * i + 256)
        part = dot(st[512 + 256 * i : 768 + 256 * i, :], outer[...])
        ot[:, ch] = part.T.astype(BF)
        for j in range(2):
            low, high = part[128 * j : 128 * j + 64, :], part[128 * j + 64 : 128 * j + 128, :]
            rows = slice(128 * i + 64 * j, 128 * i + 64 * j + 64)
            keep[rows, :] = jnp.where(c == 0, low, high)
            send[rows, :] = jnp.where(c == 0, high, low).astype(BF)
    summed_t = summed[...].T
    gup[...] = dot(summed_t[0:64, :], dzed[0:512, :]) + dot(summed_t[64:128, :], dzed[512:1024, :])


def kr_body(xc, keep, recv, own, s1, s2, s3):
    x = xc[0]
    for k, ref in enumerate((own, s1, s2, s3)):
        rows = at(lax.rem(x + k, 4), 64)
        ref[...] = (keep[rows, :] + recv[rows, :].astype(F32)).astype(BF)


def kn_body(own, r1, r2, r3, nodes, w_en, out):
    rows = total4(own[...], r1[...], r2[...], r3[...]).astype(BF)
    out[...] = (nodes[...].astype(F32) + dot(rows, w_en[...])).astype(BF)


def ka_body(xc, keep, recv, own, s1, s2, s3):
    x = xc[0]
    for k, ref in enumerate((own, s1, s2, s3)):
        ch = at(lax.rem(x + k, 4), 128)
        ref[...] = (keep[:, ch] + recv[:, ch].astype(F32)).astype(BF)


def total4(a, b, c, d):
    return (a.astype(F32) + c.astype(F32)) + (b.astype(F32) + d.astype(F32))


def k3_body(
    xc, own, r1, r2, r3, d_outer, dsilu, inner, st, w_down_t, ot, gup, edge_grad, keep, send, d_pre
):
    c = xc[1]
    dd = total4(own[...], r1[...], r2[...], r3[...]).astype(BF)
    for h, w in enumerate(swapped(c, left(w_down_t[...]), right(w_down_t[...]))):
        for i in range(2):
            rows = slice(256 * i, 256 * i + 256)
            ch = slice(512 * h + 256 * i, 512 * h + 256 * i + 256)
            d_inner = d_outer[ch, :].astype(F32) + dot(dd[rows, :], w)
            edge_grad[ch, :] = d_inner.astype(BF)
            d_pre[ch, :] = (d_inner * dsilu[ch, :].astype(F32)).astype(BF)
    for i in range(2):
        rows = slice(256 * i, 256 * i + 256)
        send[rows, :] = dot(st[at(2 * (1 - c) + i, 256), :], d_pre[...]).astype(BF)
        keep[rows, :] = dot(st[at(2 * c + i, 256), :], d_pre[...])
    ddt = dd.T
    first, second = swapped(c, ddt[0:64, :], ddt[64:128, :])
    gdown = dot(first, inner[0:512, :]) + dot(second, inner[512:1024, :])
    keep[512:576, :] = jnp.where(c == 0, gup[...], gdown)
    send[512:576, :] = jnp.where(c == 0, gdown, gup[...]).astype(BF)
    for i in range(4):
        rows = slice(576 + 64 * i, 640 + 64 * i)
        keep[rows, :] = ot[at(2 * i + c, 64), :].astype(F32)
        send[rows, :] = ot[at(2 * i + 1 - c, 64), :]


def kb_body(xc, keep, recv, own, s1, s2, s3):
    x = xc[0]
    for k, ref in enumerate((own, s1, s2, s3)):
        b = lax.rem(x + k, 4)
        ch = at(b, 128)
        ref[0:576, :] = (keep[0:576, ch] + recv[0:576, ch].astype(F32)).astype(BF)
        rows = pl.ds(pl.multiple_of(576 + 64 * b, 64), 64)
        part = (keep[rows, :] + recv[rows, :].astype(F32)).astype(BF)
        for j in range(4):
            ref[576 + 64 * j : 640 + 64 * j, :] = part[:, 128 * j : 128 * j + 128]


def k4_body(i, own, r1, r2, r3, nodes_t, all_grad, g0, s1, s2, s3, whole):
    sums = total4(own[...], r1[...], r2[...], r3[...])
    gne = dot(nodes_t[...], sums[0:512, :].astype(BF)).astype(BF)
    ot = sums[576:832, :].astype(BF)
    ot = jnp.concatenate([ot[64 * j : 64 * j + 64, :] for j in range(4)], axis=1)
    gen = dot(ot, all_grad[...]).astype(BF)
    for q in range(4):
        at_q = 400 * q
        whole[at_q : at_q + 256, :] = gne[256 * q : 256 * q + 256, :]
        for j in range(2):
            rows = slice(at_q + 256 + 64 * j, at_q + 320 + 64 * j)
            whole[rows, :] = gen[:, 256 * q + 128 * j : 256 * q + 128 * j + 128]
        whole[at_q + 384 : at_q + 400, :] = sums[512 + 16 * q : 528 + 16 * q, :].astype(BF)
    for k, ref in enumerate((g0, s1, s2, s3)):
        ref[...] = whole[at(lax.rem(i[0] + k, 4), 400), :]


def sum_body(a, b, c, d, out):
    out[...] = total4(a[...], b[...], c[...], d[...]).astype(BF)


def place_body(i, own, r1, r2, r3, out):
    rows = own.shape[0]
    for k, ref in enumerate((own, r1, r2, r3)):
        out[at(lax.rem(i[0] + 4 - k, 4), rows), :] = ref[...]


def end_body(xc, yz, *refs):
    gup, gdt, gne_far, gen_far, gne, gen, sems = refs[8:]
    x, c, z = xc[0], xc[1], yz[1]

    def run(zeros, ones):
        copies = []

        def send(near, far):
            copies.append(fetch(near, far, sems.at[len(copies)]))

        def take(ref, j, rows, lanes, far_row, far_lane, small, small_row):
            value = ref[400 * j : 400 * j + 400, :].astype(F32)
            gne[rows, lanes] = value[0:256]
            for h in range(2):
                gen[far_row, :, far_lane(h)] = value[256 + 64 * h : 320 + 64 * h]
            small[small_row, lanes] = value[384:400]

        for k in range(4):
            q = lax.rem(z + 4 - k, 4)
            for j in range(4):
                take(
                    ones[k], j, at(4 + q, 256), slice(128 * j, 128 * j + 128),
                    2 * j + 1, lambda h: at(2 * q + h, 128), gdt, at(q, 16),
                )
            send(gne.at[at(4 + q, 256), :], gne_far.at[at(4 + q, 256), :])
        for j in range(4):
            send(gen.at[2 * j + 1], gen_far.at[2 * j + 1])
        for j in range(4):
            for k in range(4):
                b = lax.rem(x + 4 - k, 4)
                take(
                    zeros[k], j, slice(256 * j, 256 * j + 256), at(b, 128),
                    2 * b, lambda h: slice(256 * j + 128 * h, 256 * j + 128 * h + 128),
                    gup, slice(16 * j, 16 * j + 16),
                )
            rows = slice(256 * j, 256 * j + 256)
            send(gne.at[rows, :], gne_far.at[rows, :])
        for j in range(4):
            send(gen.at[2 * j], gen_far.at[2 * j])
        for copy in copies:
            copy.wait()

    @pl.when(c == 0)
    def _():
        run(refs[0:4], refs[4:8])

    @pl.when(c == 1)
    def _():
        run(refs[4:8], refs[0:4])


def over_x(value, k):
    perm = [(2 * x + c, 2 * ((x + k) % 4) + c) for x in range(4) for c in range(2)]
    return lax.ppermute(value, "graph", perm)


def over_core(value):
    return lax.ppermute(value, "graph", [(i, i ^ 1) for i in range(8)])


def over_dp(value, k, axes):
    perm = []
    for y in range(4):
        for z in range(4):
            for x in range(4):
                for c in range(2):
                    at = {"x": x, "y": y, "z": z}
                    at[axes[c]] = (at[axes[c]] + k) % 4
                    to = 8 * (4 * at["y"] + at["z"]) + 2 * at["x"] + c
                    perm.append((8 * (4 * y + z) + 2 * x + c, to))
    return lax.ppermute(value, ("dp", "graph"), perm)


def tie(*values):
    return lax.optimization_barrier(values)


def local(
    nodes, node_grad, edges, source, target, trip_in, trip_out, basis, trip_count,
    w_ne, w_down, w_up, w_en,
):
    near = (1, 2, 3)

    n = [nodes[0]] + [over_x(nodes[0], k) for k in near]
    m = [over_core(n[0])]
    p = [node_grad[0]] + [over_x(node_grad[0], k) for k in near]
    s, st, il, ilt, ol, olt, basis2, in_hi, out_hi, w_near, edges_near = call(
        prep_body,
        [sds((1024, 1024)), sds((1024, 1024)), sds((2048, 1024)), sds((1024, 2048)),
         sds((2048, 512)), sds((512, 2048)), sds((2048, 128)), sds((2048, 128), jnp.int32),
         sds((2048, 128), jnp.int32), sds((2048, 512)), sds((1024, 512))],
        [trip_count, source, target, trip_in, trip_out, basis[0].T, w_ne, edges[0]],
        scalars=1,
        scratch=[pltpu.VMEM((1, 1024), jnp.int32), pltpu.VMEM((1, 1024), jnp.int32),
                 pltpu.VMEM((1, 2048), jnp.int32), pltpu.VMEM((1, 2048), jnp.int32),
                 pltpu.VMEM((64, 2048), BF), pltpu.SemaphoreType.DMA((7,))],
        vmem=12, far_in=7,
    )
    *n, s = tie(*n, s)
    m += [over_core(v) for v in n[1:]]
    down, inner, dsilu, all_nodes = call(
        k1_body,
        [sds((512, 128)), sds((1024, 512)), sds((1024, 512)), sds((512, 1024))],
        [*n, *m, s, edges_near, w_near, w_down.T],
        here="x", scratch=[pltpu.VMEM((1024, 512), BF)], vmem=12,
    )

    t = [down] + [over_x(down, k) for k in near]
    u = [over_core(down)]
    t[2], t[3], p[1], p[2], p[3] = tie(*t[2:], *p[1:])
    q = [over_core(v) for v in p]
    u += [over_core(v) for v in t[1:]]
    keep, send, outer, summed, dzed, d_outer, all_grad = call(
        k2_body,
        [sds((512, 512), F32), sds((512, 512)), sds((1024, 512)), sds((512, 128)),
         sds((1024, 512)), sds((1024, 512)), sds((512, 1024))],
        [*t, *u, *p, *q, il, ilt, ol, olt, in_hi, out_hi, basis2, inner, w_up, w_en, s],
        here="x",
        scratch=[pltpu.VMEM((1024, 512), BF), pltpu.VMEM((2048, 128), BF),
                 pltpu.VMEM((2048, 512), BF), pltpu.VMEM((512, 512), BF)],
        vmem=20,
    )

    recv = over_core(send)
    parts = call(ka_body, [sds((512, 128))] * 4, [keep, recv], here="x", vmem=8)
    dd = [parts[0]] + [over_x(parts[k], k) for k in near]
    ot, gup, o_keep, o_send = call(
        ko_body,
        [sds((512, 512)), sds((64, 512), F32), sds((256, 512), F32), sds((256, 512))],
        [outer, st, summed, dzed], here="x", vmem=16,
    )
    o_recv = over_core(o_send)
    edge_grad, keep, send = call(
        k3_body,
        [sds((1024, 512)), sds((832, 512), F32), sds((832, 512))],
        [*dd, d_outer, dsilu, inner, st, w_down.T, ot, gup],
        here="x", scratch=[pltpu.VMEM((1024, 512), BF)], vmem=16,
    )

    recv = over_core(send)
    parts = call(kb_body, [sds((832, 128))] * 4, [keep, recv], here="x", vmem=12)
    recv, o_recv, all_nodes = tie(recv, o_recv, all_nodes)
    o_parts = call(kr_body, [sds((64, 512))] * 4, [o_keep, o_recv], here="x", vmem=8)
    (nodes_t,) = call(kw_body, [sds((1024, 512))], [all_nodes], vmem=8)
    parts = [parts[0]] + [over_x(parts[k], k) for k in near]
    *parts, nodes_t = tie(*parts, nodes_t)
    parts = call(
        k4_body, [sds((400, 128))] * 4, [*parts, nodes_t, all_grad],
        here="part", scratch=[pltpu.VMEM((1600, 128), BF)], vmem=16,
    )
    parts = [parts[0]] + [over_dp(parts[k], k, "yz") for k in near]
    (part,) = call(sum_body, [sds((400, 128))], parts, vmem=8)
    parts = [part] + [over_dp(part, k, "zy") for k in near]
    o_parts = [o_parts[0]] + [over_x(o_parts[k], k) for k in near]
    *o_parts, p0, p1, p2, p3 = tie(*o_parts, *parts)
    (part,) = call(sum_body, [sds((400, 128))], [p0, p1, p2, p3], vmem=8)
    (new_nodes,) = call(kn_body, [sds((64, 1024))], [*o_parts, nodes[0], w_en], vmem=16)
    parts = [part] + [over_dp(part, k, "yx") for k in near]
    new_nodes, *parts = tie(new_nodes, *parts)
    (part,) = call(place_body, [sds((1600, 128))], [*parts], here="place", vmem=8)
    parts = [part] + [over_dp(part, k, "xz") for k in near]
    grad_up, grad_down_t, grad_ne, grad_en = call(
        end_body,
        [sds((64, 512), F32), sds((64, 512), F32), sds((2048, 512), F32), sds((8, 64, 1024), F32)],
        [*parts, *[over_core(v) for v in parts]],
        here="xy",
        scratch=[pltpu.VMEM((2048, 512), F32), pltpu.VMEM((8, 64, 1024), F32),
                 pltpu.SemaphoreType.DMA((16,))],
        vmem=16, far_out=2,
    )
    grad_en = grad_en.reshape(512, 1024)
    return (new_nodes[None], edge_grad[None], grad_ne, grad_down_t.T, grad_up, grad_en)


def solution(mesh):
    split3, split2 = P("dp", "graph", None), P("dp", "graph")
    in_specs = (split3,) * 3 + (split2,) * 4 + (split3, split2) + (P(),) * 4
    out_specs = (split3, split3, P(), P(), P(), P())
    return jax.shard_map(local, mesh=mesh, in_specs=in_specs, out_specs=out_specs, check_vma=False)
```

```python
import jax
import jax.numpy as jnp
from jax import lax
from jax.experimental import pallas as pl
from jax.experimental.pallas import tpu as pltpu
from jax.sharding import PartitionSpec as P

BF = jnp.bfloat16
F32 = jnp.float32
NT = (((1,), (1,)), ((), ()))


def dot(a, b):
    return jnp.dot(a, b, preferred_element_type=F32)


def dot_nt(a, b):
    return lax.dot_general(a, b, NT, preferred_element_type=F32)


def call(
    body, outs, args, here="", scalars=0, scratch=(), vmem=40, any_in=0, far_in=0, far_out=0
):
    n_in, n_out = len(args), len(outs)

    def placed(*refs):
        g, d = lax.axis_index("graph"), lax.axis_index("dp")
        x, c, y, z = g >> 1, g & 1, d >> 2, d & 3
        names = {
            "": (), "x": ((x, c),), "xy": ((x, c), (y, z)),
            "part": ((jnp.where(c == 0, y, z),),), "place": ((jnp.where(c == 0, y, x),),),
        }
        body(*names[here], *refs)

    in_specs = [pl.BlockSpec(memory_space=pltpu.SMEM)] * scalars
    in_specs += [pl.BlockSpec(memory_space=pltpu.VMEM)] * (n_in - scalars - any_in - far_in)
    in_specs += [pl.BlockSpec(memory_space=pl.ANY)] * any_in
    in_specs += [pl.BlockSpec(memory_space=pltpu.HBM)] * far_in
    out_specs = [pl.BlockSpec(memory_space=pltpu.VMEM)] * (n_out - far_out)
    out_specs += [pl.BlockSpec(memory_space=pltpu.HBM)] * far_out
    near, far = args[: n_in - far_in], args[n_in - far_in :]
    return pl.pallas_call(
        placed if here else body,
        out_shape=[
            pltpu.HBM(o.shape, o.dtype) if i >= n_out - far_out else o for i, o in enumerate(outs)
        ],
        in_specs=in_specs,
        out_specs=out_specs,
        scratch_shapes=list(scratch),
        compiler_params=pltpu.CompilerParams(vmem_limit_bytes=vmem << 20),
        cost_estimate=pl.CostEstimate(flops=1, bytes_accessed=1, transcendentals=0),
    )(*near, *(pltpu.with_memory_space_constraint(a, pltpu.HBM) for a in far))


def sds(shape, dtype=BF):
    return jax.ShapeDtypeStruct(shape, dtype)


def at(i, size):
    return pl.ds(pl.multiple_of(i * size, size), size)


def hot(mask):
    return jnp.where(mask, 1.0, 0.0).astype(BF)


def left(w):
    return jnp.concatenate([w, jnp.zeros_like(w)], axis=0)


def right(w):
    return jnp.concatenate([jnp.zeros_like(w), w], axis=0)


def column(row):
    return jnp.broadcast_to(row.astype(F32), (128, row.shape[1])).T.astype(jnp.int32)


def hot_rows(col, width):
    lane = lax.broadcasted_iota(jnp.int32, col.shape, 1)
    return jnp.concatenate([hot(col == lane + j) for j in range(0, width, 128)], axis=1)


def prep_body(cnt, *refs):
    s, st, il, ilt, ol, olt, basis, in_hi, out_hi, w_ne, edges = refs[7:18]
    src_r, tgt_r, in_r, out_r, basis_t, sems = refs[18:]
    nears = (src_r, tgt_r, in_r, out_r, basis_t, w_ne, edges)
    loads = [fetch(refs[i], near, sems.at[i]) for i, near in enumerate(nears)]
    for copy in loads[:4]:
        copy.wait()
    for i in range(4):
        ch = slice(256 * i, 256 * i + 256)
        s[ch, 0:512] = hot_rows(column(src_r[:, ch]), 512)
        s[ch, 512:1024] = hot_rows(column(tgt_r[:, ch]), 512)
    row = lax.broadcasted_iota(jnp.int32, (128, 1024), 0)
    for i in range(4):
        ch = slice(128 * i, 128 * i + 128)
        st[ch, :] = hot(src_r[...] == row + 128 * i)
        st[512 + 128 * i : 640 + 128 * i, :] = hot(tgt_r[...] == row + 128 * i)
    pos = lax.broadcasted_iota(jnp.int32, (1, 2048), 1)
    live = pos < cnt[0, 0]
    in_lo = jnp.where(live, in_r[...] & 1023, -1)
    out_lo = out_r[...] & 511
    for i in range(8):
        ch = slice(256 * i, 256 * i + 256)
        il[ch, :] = hot_rows(column(in_lo[:, ch]), 1024)
        ol[ch, :] = hot_rows(column(out_lo[:, ch]), 512)
        in_hi[ch, :] = column(in_r[:, ch] >> 9)
        out_hi[ch, :] = column(out_r[:, ch] >> 9)
    row = lax.broadcasted_iota(jnp.int32, (64, 2048), 0)
    for i in range(8):
        ch = slice(64 * i, 64 * i + 64)
        ilt[ch, :] = hot(in_lo == row + 64 * i)
        ilt[512 + 64 * i : 576 + 64 * i, :] = hot(in_lo == row + 512 + 64 * i)
        olt[ch, :] = hot(out_lo == row + 64 * i)
    for copy in loads[4:]:
        copy.wait()
    basis[...] = jnp.concatenate([basis_t[...], basis_t[...]], axis=0).T


def fetch(far, near, sem):
    copy = pltpu.make_async_copy(far, near, sem)
    copy.start()
    return copy


def gathered(xc, refs, out):
    x, c = xc
    for k in range(4):
        g = 2 * lax.rem(x + 4 - k, 4)
        out[at(g + c, 64), :] = refs[k][...]
        out[at(g + 1 - c, 64), :] = refs[4 + k][...]


def k1_body(xc, *refs):
    s, edges, w_ne, w_down_t, down, inner, dsilu, nodes, ab = refs[8:]
    gathered(xc, refs[:8], nodes)
    for h in range(2):
        for i in range(2):
            rows = slice(512 * h + 256 * i, 512 * h + 256 * i + 256)
            ab[rows, :] = dot(
                nodes[256 * i : 256 * i + 256, :], w_ne[1024 * h : 1024 * h + 1024, :]
            ).astype(BF)
    wd = swapped(xc[1], left(w_down_t[...]), right(w_down_t[...]))
    for i in range(2):
        total = None
        for h in range(2):
            ch = slice(512 * h + 256 * i, 512 * h + 256 * i + 256)
            pre = dot(s[ch, :], ab[...])
            sig = jax.nn.sigmoid(pre)
            held = (edges[ch, :].astype(F32) + pre * sig).astype(BF)
            inner[ch, :] = held
            dsilu[ch, :] = (sig * (1.0 + pre * (1.0 - sig))).astype(BF)
            part = dot_nt(held, wd[h])
            total = part if total is None else total + part
        down[256 * i : 256 * i + 256, :] = total.astype(BF)


def kw_body(nodes, nodes_t):
    nodes_t[...] = nodes[...].T


def swapped(c, first, second):
    a, b = first.astype(F32), second.astype(F32)
    return jnp.where(c == 0, a, b).astype(BF), jnp.where(c == 0, b, a).astype(BF)


def lane_key(c):
    lane = lax.broadcasted_iota(jnp.int32, (512, 128), 1)
    return jnp.where(c == 0, lane, 127 - lane)


def halves(value, odd, upper):
    kept = jnp.where(upper == odd, value, 0.0)
    return kept + pltpu.roll(kept, 64, 1)


def k2_body(xc, *refs):
    pieces, grads = refs[0:8], refs[8:16]
    il, ilt, ol, olt, in_hi, out_hi, basis, inner, w_up, w_en, s = refs[16:27]
    keep, send, outer, summed, dzed, d_outer, all_grad, table, gath, spread, q = refs[27:]
    x, c = xc
    gathered(xc, grads, all_grad)
    for i in range(2):
        ch = slice(256 * i, 256 * i + 256)
        q[ch, :] = dot_nt(all_grad[ch, :], w_en[...]).astype(BF)
    key = lane_key(c)
    is_mine = key.astype(F32).astype(BF) < 64
    for k in range(4):
        cols = at(lax.rem(x + 4 - k, 4), 128)
        mine, other = pieces[k][...], pieces[4 + k][...]
        table[0:512, cols] = jnp.where(is_mine, mine, other)
        table[512:1024, cols] = jnp.where(is_mine, other, mine)
    upper = lax.broadcasted_iota(jnp.int32, (256, 128), 1) >= 64
    for i in range(8):
        ch = slice(256 * i, 256 * i + 256)
        got = dot(il[ch, :], table[...])
        hi = in_hi[ch, :]
        acc = jnp.zeros((256, 128), F32)
        for b in range(4):
            acc = jnp.where((hi >> 2) == b, got[:, 128 * b : 128 * b + 128], acc)
        term = halves(acc, ((hi ^ (hi >> 1)) & 1) == 1, upper) * basis[ch, :].astype(F32)
        gath[ch, :] = jnp.where(upper == (out_hi[ch, :] == 1), term, 0.0).astype(BF)
    held = dot(olt[...], gath[...]).astype(BF)
    summed[...] = held
    d_sum = jnp.zeros((512, 128), F32)
    for h, w in enumerate((left(w_up[...]), right(w_up[...]))):
        ch = slice(512 * h, 512 * h + 512)
        zed = dot(held, w)
        sig = jax.nn.sigmoid(zed)
        outer[ch, :] = (inner[ch, :].astype(F32) + zed * sig).astype(BF)
        back = dot(s[ch, 512:1024], q[...])
        d_outer[ch, :] = back.astype(BF)
        dz = (back * (sig * (1.0 + zed * (1.0 - sig)))).astype(BF)
        dzed[ch, :] = dz
        d_sum += dot_nt(dz, w)
    d_sum = d_sum.astype(BF)
    for i in range(8):
        ch = slice(256 * i, 256 * i + 256)
        got = dot(ol[ch, :], d_sum)
        term = halves(got, out_hi[ch, :] == 1, upper) * basis[ch, :].astype(F32)
        hi = in_hi[ch, :]
        term = jnp.where(upper == (((hi ^ (hi >> 1)) & 1) == 1), term, 0.0).astype(BF)
        owner = (hi >> 2).astype(F32).astype(BF)
        for b in range(4):
            spread[ch, 128 * b : 128 * b + 128] = jnp.where(owner == b, term, jnp.zeros_like(term))
    part = dot(ilt[...], spread[...])
    for b in range(4):
        ch = slice(128 * b, 128 * b + 128)
        low, high = part[0:512, ch], part[512:1024, ch]
        keep[:, ch] = jnp.where(key < 64, low, high)
        send[:, ch] = jnp.where(key < 64, high, low).astype(BF)


def ko_body(xc, outer, st, summed, dzed, ot, gup, keep, send):
    c = xc[1]
    for i in range(2):
        ch = slice(256 * i, 256 * i + 256)
        part = dot(st[512 + 256 * i : 768 + 256 * i, :], outer[...])
        ot[:, ch] = part.T.astype(BF)
        for j in range(2):
            low, high = part[128 * j : 128 * j + 64, :], part[128 * j + 64 : 128 * j + 128, :]
            rows = slice(128 * i + 64 * j, 128 * i + 64 * j + 64)
            keep[rows, :] = jnp.where(c == 0, low, high)
            send[rows, :] = jnp.where(c == 0, high, low).astype(BF)
    summed_t = summed[...].T
    gup[...] = dot(summed_t[0:64, :], dzed[0:512, :]) + dot(summed_t[64:128, :], dzed[512:1024, :])


def kr_body(xc, keep, recv, own, s1, s2, s3):
    x = xc[0]
    for k, ref in enumerate((own, s1, s2, s3)):
        rows = at(lax.rem(x + k, 4), 64)
        ref[...] = (keep[rows, :] + recv[rows, :].astype(F32)).astype(BF)


def kn_body(own, r1, r2, r3, nodes, w_en, out):
    rows = total4(own[...], r1[...], r2[...], r3[...]).astype(BF)
    out[...] = (nodes[...].astype(F32) + dot(rows, w_en[...])).astype(BF)


def ka_body(xc, keep, recv, own, s1, s2, s3):
    x = xc[0]
    for k, ref in enumerate((own, s1, s2, s3)):
        ch = at(lax.rem(x + k, 4), 128)
        ref[...] = (keep[:, ch] + recv[:, ch].astype(F32)).astype(BF)


def total4(a, b, c, d):
    return (a.astype(F32) + c.astype(F32)) + (b.astype(F32) + d.astype(F32))


def k3_body(
    xc, own, r1, r2, r3, d_outer, dsilu, inner, st, w_down_t, ot, gup, send, d_pre, grads, gdown
):
    c = xc[1]
    dd = total4(own[...], r1[...], r2[...], r3[...]).astype(BF)
    for h, w in enumerate(swapped(c, left(w_down_t[...]), right(w_down_t[...]))):
        for i in range(2):
            rows = slice(256 * i, 256 * i + 256)
            ch = slice(512 * h + 256 * i, 512 * h + 256 * i + 256)
            d_inner = d_outer[ch, :].astype(F32) + dot(dd[rows, :], w)
            grads[ch, :] = d_inner.astype(BF)
            d_pre[ch, :] = (d_inner * dsilu[ch, :].astype(F32)).astype(BF)
    for i in range(2):
        rows = slice(256 * i, 256 * i + 256)
        send[rows, :] = dot(st[at(2 * (1 - c) + i, 256), :], d_pre[...]).astype(BF)
    ddt = dd.T
    first, second = swapped(c, ddt[0:64, :], ddt[64:128, :])
    gdown[...] = dot(first, inner[0:512, :]) + dot(second, inner[512:1024, :])
    send[512:576, :] = jnp.where(c == 0, gdown[...], gup[...]).astype(BF)
    for i in range(4):
        rows = slice(576 + 64 * i, 640 + 64 * i)
        send[rows, :] = ot[at(2 * i + 1 - c, 64), :]


def k3_own_body(xc, st, d_pre, grads, gdown, ot, gup, edge_grad, keep):
    c = xc[1]
    edge_grad[...] = grads[...]
    for i in range(2):
        rows = slice(256 * i, 256 * i + 256)
        keep[rows, :] = dot(st[at(2 * c + i, 256), :], d_pre[...])
    keep[512:576, :] = jnp.where(c == 0, gup[...], gdown[...])
    for i in range(4):
        rows = slice(576 + 64 * i, 640 + 64 * i)
        keep[rows, :] = ot[at(2 * i + c, 64), :].astype(F32)


def kb_body(xc, keep, recv, own, s1, s2, s3):
    x = xc[0]
    for k, ref in enumerate((own, s1, s2, s3)):
        b = lax.rem(x + k, 4)
        ch = at(b, 128)
        ref[0:576, :] = (keep[0:576, ch] + recv[0:576, ch].astype(F32)).astype(BF)
        rows = pl.ds(pl.multiple_of(576 + 64 * b, 64), 64)
        part = (keep[rows, :] + recv[rows, :].astype(F32)).astype(BF)
        for j in range(4):
            ref[576 + 64 * j : 640 + 64 * j, :] = part[:, 128 * j : 128 * j + 128]


def k4_body(i, own, r1, r2, r3, nodes_t, all_grad, g0, s1, s2, s3, whole):
    sums = total4(own[...], r1[...], r2[...], r3[...])
    gne = dot(nodes_t[...], sums[0:512, :].astype(BF)).astype(BF)
    ot = sums[576:832, :].astype(BF)
    ot = jnp.concatenate([ot[64 * j : 64 * j + 64, :] for j in range(4)], axis=1)
    gen = dot(ot, all_grad[...]).astype(BF)
    for q in range(4):
        at_q = 400 * q
        whole[at_q : at_q + 256, :] = gne[256 * q : 256 * q + 256, :]
        for j in range(2):
            rows = slice(at_q + 256 + 64 * j, at_q + 320 + 64 * j)
            whole[rows, :] = gen[:, 256 * q + 128 * j : 256 * q + 128 * j + 128]
        whole[at_q + 384 : at_q + 400, :] = sums[512 + 16 * q : 528 + 16 * q, :].astype(BF)
    for k, ref in enumerate((g0, s1, s2, s3)):
        ref[...] = whole[at(lax.rem(i[0] + k, 4), 400), :]


def sum_body(a, b, c, d, out):
    out[...] = total4(a[...], b[...], c[...], d[...]).astype(BF)


def place_body(i, own, r1, r2, r3, out):
    rows = own.shape[0]
    for k, ref in enumerate((own, r1, r2, r3)):
        out[at(lax.rem(i[0] + 4 - k, 4), rows), :] = ref[...]


def end_body(xc, yz, *refs):
    gup, gdt, gne_far, gen_far, gne, gen, sems = refs[8:]
    x, c, z = xc[0], xc[1], yz[1]

    def run(zeros, ones):
        copies = []

        def send(near, far):
            copies.append(fetch(near, far, sems.at[len(copies)]))

        def take(ref, j, rows, lanes, far_row, far_lane, small, small_row):
            value = ref[400 * j : 400 * j + 400, :].astype(F32)
            gne[rows, lanes] = value[0:256]
            for h in range(2):
                gen[far_row, :, far_lane(h)] = value[256 + 64 * h : 320 + 64 * h]
            small[small_row, lanes] = value[384:400]

        for k in range(4):
            q = lax.rem(z + 4 - k, 4)
            for j in range(4):
                take(
                    ones[k], j, at(4 + q, 256), slice(128 * j, 128 * j + 128),
                    2 * j + 1, lambda h: at(2 * q + h, 128), gdt, at(q, 16),
                )
            send(gne.at[at(4 + q, 256), :], gne_far.at[at(4 + q, 256), :])
        for j in range(4):
            send(gen.at[2 * j + 1], gen_far.at[2 * j + 1])
        for j in range(4):
            for k in range(4):
                b = lax.rem(x + 4 - k, 4)
                take(
                    zeros[k], j, slice(256 * j, 256 * j + 256), at(b, 128),
                    2 * b, lambda h: slice(256 * j + 128 * h, 256 * j + 128 * h + 128),
                    gup, slice(16 * j, 16 * j + 16),
                )
            rows = slice(256 * j, 256 * j + 256)
            send(gne.at[rows, :], gne_far.at[rows, :])
        for j in range(4):
            send(gen.at[2 * j], gen_far.at[2 * j])
        for copy in copies:
            copy.wait()

    @pl.when(c == 0)
    def _():
        run(refs[0:4], refs[4:8])

    @pl.when(c == 1)
    def _():
        run(refs[4:8], refs[0:4])


def over_x(value, k):
    perm = [(2 * x + c, 2 * ((x + k) % 4) + c) for x in range(4) for c in range(2)]
    return lax.ppermute(value, "graph", perm)


def over_core(value):
    return lax.ppermute(value, "graph", [(i, i ^ 1) for i in range(8)])


def over_dp(value, k, axes):
    perm = []
    for y in range(4):
        for z in range(4):
            for x in range(4):
                for c in range(2):
                    at = {"x": x, "y": y, "z": z}
                    at[axes[c]] = (at[axes[c]] + k) % 4
                    to = 8 * (4 * at["y"] + at["z"]) + 2 * at["x"] + c
                    perm.append((8 * (4 * y + z) + 2 * x + c, to))
    return lax.ppermute(value, ("dp", "graph"), perm)


def tie(*values):
    return lax.optimization_barrier(values)


def local(
    nodes, node_grad, edges, source, target, trip_in, trip_out, basis, trip_count,
    w_ne, w_down, w_up, w_en,
):
    near = (1, 2, 3)

    n = [nodes[0]] + [over_x(nodes[0], k) for k in near]
    m = [over_core(n[0])]
    p = [node_grad[0]] + [over_x(node_grad[0], k) for k in near]
    s, st, il, ilt, ol, olt, basis2, in_hi, out_hi, w_near, edges_near = call(
        prep_body,
        [sds((1024, 1024)), sds((1024, 1024)), sds((2048, 1024)), sds((1024, 2048)),
         sds((2048, 512)), sds((512, 2048)), sds((2048, 128)), sds((2048, 128), jnp.int32),
         sds((2048, 128), jnp.int32), sds((2048, 512)), sds((1024, 512))],
        [trip_count, source, target, trip_in, trip_out, basis[0].T, w_ne, edges[0]],
        scalars=1,
        scratch=[pltpu.VMEM((1, 1024), jnp.int32), pltpu.VMEM((1, 1024), jnp.int32),
                 pltpu.VMEM((1, 2048), jnp.int32), pltpu.VMEM((1, 2048), jnp.int32),
                 pltpu.VMEM((64, 2048), BF), pltpu.SemaphoreType.DMA((7,))],
        vmem=12, far_in=7,
    )
    *n, s = tie(*n, s)
    m += [over_core(v) for v in n[1:]]
    down, inner, dsilu, all_nodes = call(
        k1_body,
        [sds((512, 128)), sds((1024, 512)), sds((1024, 512)), sds((512, 1024))],
        [*n, *m, s, edges_near, w_near, w_down.T],
        here="x", scratch=[pltpu.VMEM((1024, 512), BF)], vmem=12,
    )

    t = [down] + [over_x(down, k) for k in near]
    u = [over_core(down)]
    t[2], t[3], p[1], p[2], p[3] = tie(*t[2:], *p[1:])
    q = [over_core(v) for v in p]
    u += [over_core(v) for v in t[1:]]
    keep, send, outer, summed, dzed, d_outer, all_grad = call(
        k2_body,
        [sds((512, 512), F32), sds((512, 512)), sds((1024, 512)), sds((512, 128)),
         sds((1024, 512)), sds((1024, 512)), sds((512, 1024))],
        [*t, *u, *p, *q, il, ilt, ol, olt, in_hi, out_hi, basis2, inner, w_up, w_en, s],
        here="x",
        scratch=[pltpu.VMEM((1024, 512), BF), pltpu.VMEM((2048, 128), BF),
                 pltpu.VMEM((2048, 512), BF), pltpu.VMEM((512, 512), BF)],
        vmem=20,
    )

    recv = over_core(send)
    parts = call(ka_body, [sds((512, 128))] * 4, [keep, recv], here="x", vmem=8)
    dd = [parts[0]] + [over_x(parts[k], k) for k in near]
    ot, gup, o_keep, o_send = call(
        ko_body,
        [sds((512, 512)), sds((64, 512), F32), sds((256, 512), F32), sds((256, 512))],
        [outer, st, summed, dzed], here="x", vmem=16,
    )
    o_recv = over_core(o_send)
    send, d_pre, grads, gdown = call(
        k3_body,
        [sds((832, 512)), sds((1024, 512)), sds((1024, 512)), sds((64, 512), F32)],
        [*dd, d_outer, dsilu, inner, st, w_down.T, ot, gup], here="x", vmem=16,
    )
    recv = over_core(send)
    edge_grad, keep = call(
        k3_own_body,
        [sds((1024, 512)), sds((832, 512), F32)],
        [st, d_pre, grads, gdown, ot, gup], here="x", vmem=16,
    )
    parts = call(kb_body, [sds((832, 128))] * 4, [keep, recv], here="x", vmem=12)
    recv, o_recv, all_nodes = tie(recv, o_recv, all_nodes)
    o_parts = call(kr_body, [sds((64, 512))] * 4, [o_keep, o_recv], here="x", vmem=8)
    (nodes_t,) = call(kw_body, [sds((1024, 512))], [all_nodes], vmem=8)
    parts = [parts[0]] + [over_x(parts[k], k) for k in near]
    *parts, nodes_t = tie(*parts, nodes_t)
    parts = call(
        k4_body, [sds((400, 128))] * 4, [*parts, nodes_t, all_grad],
        here="part", scratch=[pltpu.VMEM((1600, 128), BF)], vmem=16,
    )
    parts = [parts[0]] + [over_dp(parts[k], k, "yz") for k in near]
    (part,) = call(sum_body, [sds((400, 128))], parts, vmem=8)
    parts = [part] + [over_dp(part, k, "zy") for k in near]
    o_parts = [o_parts[0]] + [over_x(o_parts[k], k) for k in near]
    *o_parts, p0, p1, p2, p3 = tie(*o_parts, *parts)
    (part,) = call(sum_body, [sds((400, 128))], [p0, p1, p2, p3], vmem=8)
    (new_nodes,) = call(kn_body, [sds((64, 1024))], [*o_parts, nodes[0], w_en], vmem=16)
    parts = [part] + [over_dp(part, k, "yx") for k in near]
    new_nodes, *parts = tie(new_nodes, *parts)
    (part,) = call(place_body, [sds((1600, 128))], [*parts], here="place", vmem=8)
    parts = [part] + [over_dp(part, k, "xz") for k in near]
    grad_up, grad_down_t, grad_ne, grad_en = call(
        end_body,
        [sds((64, 512), F32), sds((64, 512), F32), sds((2048, 512), F32), sds((8, 64, 1024), F32)],
        [*parts, *[over_core(v) for v in parts]],
        here="xy",
        scratch=[pltpu.VMEM((2048, 512), F32), pltpu.VMEM((8, 64, 1024), F32),
                 pltpu.SemaphoreType.DMA((16,))],
        vmem=16, far_out=2,
    )
    grad_en = grad_en.reshape(512, 1024)
    return (new_nodes[None], edge_grad[None], grad_ne, grad_down_t.T, grad_up, grad_en)


def solution(mesh):
    split3, split2 = P("dp", "graph", None), P("dp", "graph")
    in_specs = (split3,) * 3 + (split2,) * 4 + (split3, split2) + (P(),) * 4
    out_specs = (split3, split3, P(), P(), P(), P())
    return jax.shard_map(local, mesh=mesh, in_specs=in_specs, out_specs=out_specs, check_vma=False)
```
